32 devices in a mesh: dp: 4 (over y, x), expert: 8 (over z, core).
Axes of the slice: x: 2, y: 2, z: 4, core: 2. Of those that a mesh axis runs over, the one named last changes fastest.
Arguments:
- tokens: bfloat16 [8192, 1024], P(('dp', 'expert')), may hold values from -6 to 6
- cotangent: bfloat16 [8192, 1024], P(('dp', 'expert')), may hold values from -6 to 6
- gates: bfloat16 [8192, 2], P(('dp', 'expert')), may hold values from 0.099609375 to 1
- expert_ids: int32 [8192, 2], P(('dp', 'expert')), may hold values from 0 to 7, all different within a row; in each aligned block of 128 rows (0 to 127, 128 to 255, ...) at most 64 rows name the same one
- expert_weights: bfloat16 [8, 3, 1024, 768], P('expert'), may hold values from -0.1875 to 0.1875
Outputs:
- tokens_grad: bfloat16 [8192, 1024], P(('dp', 'expert'))
- gates_grad: bfloat16 [8192, 2], P(('dp', 'expert'))
- weights_grad: bfloat16 [8, 3, 1024, 768], P('expert', None, 'dp')
The draws below stay inside these ranges and needn't reach their ends.
Inputs may be any that keep to these rules, and one draw needn't show every extreme that they name: `expert_ids`: within each micro-batch of 128 tokens of one device no expert is named by more than 64 routes, a bound that some block reaches; the two ids of a token differ.
All inputs are finite; a program needn't handle non-finite values.
Results may differ from the reference program's by a relative error of at most 0.017.
Values may be sent and summed in bfloat16 or wider, within the bound.
No kernel may reach another device: no remote copies, remote signals or barrier semaphores. Data moves between devices by JAX's collectives and lax.ppermute only.
A program may use at most 64 MiB of HBM per device.

```python
import math
import jax
import jax.numpy as jnp
import numpy as np
from jax import lax

D = 1024
FF = 768
MICRO = 2
MB_TOK = 128
E = 8
CAP = 64
TOKENS = 8192
N_DP = 4
N_EXPERT = 8


def with_spikes(result, stream_key, source, target, parts, factor):
    owner, partner = [(jnp.arange(result.shape[axis_at]) // (result.shape[axis_at] // parts)).reshape([-1 if axis == axis_at else 1 for axis in range(result.ndim)]) for axis_at in (source, target)]
    chosen = jax.random.permutation(stream_key, parts)[partner]
    strong = (owner == chosen) | (owner == (partner + parts // 2) % parts)
    return jnp.where(strong, factor * result, result)


def shard_levels(own_key, extent, shards, low, top_value):
    factor_of, own = 1.0, jax.random.fold_in(own_key, 6)
    for axis_at, shards_of in shards:
        heights = jnp.exp(jax.random.uniform(jax.random.fold_in(own, axis_at), (shards_of,), jnp.float32, low / len(shards), top_value / len(shards)))
        factor_of = factor_of * jnp.repeat(heights, extent[axis_at] // shards_of).reshape([-1 if axis == axis_at else 1 for axis in range(len(extent))])
    return factor_of


def routed_block(own_key, own, number, rows, count, top, most, skew):
    order = jax.random.permutation(own_key, count)
    heavy_load, usual = load_shares(count, rows * top, most, skew, True), load_shares(count, rows * top, most, skew, False)
    places = jnp.arange(count)

    def named(lengths, rotation):
        used = int((lengths > 0).sum())
        fixed = max(1, used // 4)
        moved = fixed + (places - fixed + rotation * (used - fixed)) % max(1, count - fixed)
        return jnp.zeros((count,), jnp.int32).at[order[jnp.where(places < fixed, places, moved)]].set(jnp.asarray(lengths, jnp.int32))

    lengths = jnp.where(number % 4 == 0, named(heavy_load, number // 4), named(usual, number - number // 4 - 1))
    mixed = jax.random.permutation(jax.random.fold_in(own, 3), count)
    giver, taker = mixed[0:count // 2 * 2:2], mixed[1:count // 2 * 2:2]
    room = jnp.minimum(lengths[giver] - 1, most - lengths[taker]) // 2
    room = jnp.where((giver == order[0]) | (taker == order[0]) | (lengths[taker] == 0), 0, jnp.maximum(room, 0))
    moved = jax.random.randint(jax.random.fold_in(own, 4), (count // 2,), 0, 1 << 20) % (room + 1)
    lengths = lengths.at[giver].add(-moved).at[taker].add(moved)
    labels = jnp.searchsorted(jnp.cumsum(lengths), jnp.arange(rows * top), side="right").astype(jnp.int32)
    listing = labels.reshape(top, rows).T
    listing = listing[jax.random.permutation(jax.random.fold_in(own, 1), rows)]
    rotation = jax.random.randint(jax.random.fold_in(own, 2), (rows, 1), 0, top)
    return jnp.take_along_axis(listing, (jnp.arange(top)[None, :] + rotation) % top, axis=1)


def load_shares(count, total, limit, slope, full):
    portions = [(1 << 20) // math.isqrt(rank ** slope) + 1 for rank in range(1, count + 1)]
    largest = limit if full else min(limit, max(-(-total // count), total * portions[0] // sum(portions)))
    least = 1 if total - largest >= count - 1 else 0
    given, rest = [largest] + [least] * (count - 1), total - largest - least * (count - 1)
    while rest > 0:
        free = [i for i in range(1, count) if given[i] < largest] or [i for i in range(1, count) if given[i] < limit]
        whole, budget = sum([portions[i] for i in free]), rest
        for i in free:
            addition = min(limit - given[i], max(1, budget * portions[i] // whole), rest)
            given[i] = given[i] + addition
            rest = rest - addition
    return np.array(given)


def bell_draw(own_key, shape, width, reach, shards=(), kind=jnp.bfloat16):
    values = width * jax.random.normal(own_key, shape, jnp.float32)
    if shards:
        values = values * shard_levels(own_key, shape, shards, -0.22, 0.18)
    return jnp.clip(values, -reach, reach).astype(kind)


def noise_with(key, dims, scale, most, pieces, heavy, kind=jnp.bfloat16):
    values = scale * jax.random.normal(key, dims, jnp.float32)
    if pieces:
        values = values * shard_levels(key, dims, pieces, -0.22, 0.18)
    return jnp.clip(with_spikes(values, jax.random.fold_in(key, 3), *heavy), -most, most).astype(kind)


def setup_inputs(seed: int = 0) -> dict:
    arg_keys = jax.random.split(jax.random.key(seed), 6)
    tokens = noise_with(arg_keys[0], (TOKENS, D), 1.0, 6.0, ((0, 32),), (0, 1, 32, 2.75))
    cotangent = bell_draw(arg_keys[1], (TOKENS, D), 1.0, 6.0, ((0, 32),))
    gates = jnp.clip(0.099609375 + 0.9003906 * jax.random.uniform(arg_keys[2], (TOKENS, 2), jnp.float32) ** shard_levels(arg_keys[2], (TOKENS, 2), ((0, 32),), -0.2, 0.2), 0.099609375, 1.0).astype(jnp.bfloat16)
    expert_ids_keys = jax.random.split(jax.random.fold_in(arg_keys[3], 1), TOKENS // MB_TOK)
    expert_ids_turns = jax.random.permutation(jax.random.fold_in(arg_keys[3], 3), TOKENS // MB_TOK)
    expert_ids = jax.vmap(lambda own, number: routed_block(jax.random.fold_in(arg_keys[3], 2), own, number, MB_TOK, E, 2, CAP, 2))(expert_ids_keys, expert_ids_turns).reshape((TOKENS, 2))
    expert_weights = bell_draw(arg_keys[4], (E, 3, D, FF), D ** -0.5, 0.1875, ((0, 8),))
    return {"tokens": tokens, "cotangent": cotangent, "gates": gates, "expert_ids": expert_ids, "expert_weights": expert_weights}


def route_slots(ids_block, expert_count, capacity):
    flat_ids = ids_block.reshape(-1).astype(jnp.int32)
    one_hot = (flat_ids[:, None] == jnp.arange(expert_count, dtype=jnp.int32)[None, :]).astype(jnp.int32)
    earlier = jnp.cumsum(one_hot, axis=0) - one_hot
    rank_slot = jnp.sum(earlier * one_hot, axis=1).astype(jnp.int32)
    route_slot = (flat_ids * capacity + rank_slot).astype(jnp.int32)
    routes = jnp.arange(flat_ids.shape[0], dtype=jnp.int32)
    slot_route = jnp.zeros((expert_count * capacity,), jnp.int32).at[route_slot].set(routes)
    filled = jnp.zeros((expert_count * capacity,), jnp.int32).at[route_slot].set(1)
    return route_slot, slot_route, filled


def pack_rows(inputs, cotan, gate_vals, slot_route, filled, expert_count, capacity):
    token_index = (slot_route // 2).astype(jnp.int32)
    keeps = filled > 0
    feature_width = inputs.shape[1]
    rows_in = jnp.where(keeps[:, None], jnp.take(inputs, token_index, axis=0), jnp.zeros((), inputs.dtype))
    rows_cot = jnp.where(keeps[:, None], jnp.take(cotan, token_index, axis=0), jnp.zeros((), cotan.dtype))
    rows_gate = jnp.where(keeps, jnp.take(gate_vals.reshape(-1), slot_route), jnp.zeros((), gate_vals.dtype))
    return (rows_in.reshape(expert_count, capacity, feature_width),
            rows_cot.reshape(expert_count, capacity, feature_width),
            rows_gate.reshape(expert_count, capacity))


def expert_backward(rows_in, rows_cot, rows_gate, weights):
    w_gate = weights[0]
    w_up = weights[1]
    w_down = weights[2]
    contract_last = (((1,), (1,)), ((), ()))
    contract_first = (((0,), (0,)), ((), ()))
    pre_gate = jnp.dot(rows_in, w_gate, preferred_element_type=jnp.float32)
    pre_up = jnp.dot(rows_in, w_up, preferred_element_type=jnp.float32)
    sigmoid_gate = jax.nn.sigmoid(pre_gate)
    activated = pre_gate * sigmoid_gate
    hidden = (activated * pre_up).astype(jnp.bfloat16)
    output = lax.dot_general(hidden, w_down, contract_last, preferred_element_type=jnp.float32)
    gate_grad = jnp.sum(output * rows_cot.astype(jnp.float32), axis=1).astype(jnp.bfloat16)
    scaled = (rows_gate.astype(jnp.float32)[:, None] * rows_cot.astype(jnp.float32)).astype(jnp.bfloat16)
    hidden_grad = jnp.dot(scaled, w_down, preferred_element_type=jnp.float32)
    grad_pre_gate = (hidden_grad * pre_up * sigmoid_gate * (1.0 + pre_gate * (1.0 - sigmoid_gate))).astype(jnp.bfloat16)
    grad_pre_up = (hidden_grad * activated).astype(jnp.bfloat16)
    input_grad = (lax.dot_general(grad_pre_gate, w_gate, contract_last, preferred_element_type=jnp.float32)
                  + lax.dot_general(grad_pre_up, w_up, contract_last, preferred_element_type=jnp.float32)).astype(jnp.bfloat16)
    weight_grad = jnp.stack([
        lax.dot_general(rows_in, grad_pre_gate, contract_first, preferred_element_type=jnp.float32),
        lax.dot_general(rows_in, grad_pre_up, contract_first, preferred_element_type=jnp.float32),
        lax.dot_general(scaled, hidden, contract_first, preferred_element_type=jnp.float32)])
    return input_grad, gate_grad, weight_grad


def reference(tokens, cotangent, gates, expert_ids, expert_weights):
    expert_count = E
    capacity = CAP
    feature_width = D
    blocks_in = tokens.reshape(N_DP, N_EXPERT, MICRO, MB_TOK, feature_width)
    blocks_cot = cotangent.reshape(N_DP, N_EXPERT, MICRO, MB_TOK, feature_width)
    blocks_gate = gates.reshape(N_DP, N_EXPERT, MICRO, MB_TOK, 2)
    blocks_ids = expert_ids.reshape(N_DP, N_EXPERT, MICRO, MB_TOK, 2)

    def one_batch(batch_in, batch_cot, batch_gate, batch_ids):
        route_slot, slot_route, filled = route_slots(batch_ids, expert_count, capacity)
        rows_in, rows_cot, rows_gate = pack_rows(batch_in, batch_cot, batch_gate, slot_route, filled, expert_count, capacity)
        return rows_in, rows_cot, rows_gate, route_slot

    def unpack(grad_flat, gate_flat, route_slot):
        routed = jnp.take(grad_flat, route_slot, axis=0).astype(jnp.float32).reshape(MB_TOK, 2, feature_width)
        return jnp.sum(routed, axis=1).astype(jnp.bfloat16), jnp.take(gate_flat, route_slot).reshape(MB_TOK, 2)

    def one_row(grad_total, row_block):
        row_in, row_cot, row_gate, row_ids = row_block
        rows_in, rows_cot, rows_gate, route_slot = jax.vmap(jax.vmap(one_batch))(row_in, row_cot, row_gate, row_ids)
        rows_in = jnp.transpose(rows_in, (2, 0, 1, 3, 4)).reshape(expert_count, -1, feature_width)
        rows_cot = jnp.transpose(rows_cot, (2, 0, 1, 3, 4)).reshape(expert_count, -1, feature_width)
        rows_gate = jnp.transpose(rows_gate, (2, 0, 1, 3)).reshape(expert_count, -1)
        input_grad, gate_grad, weight_grad = lax.map(lambda packed_rows: expert_backward(*packed_rows),
                                                     (rows_in, rows_cot, rows_gate, expert_weights))
        rounded = lax.optimization_barrier(weight_grad.astype(jnp.bfloat16))
        grad_total = grad_total + rounded.astype(jnp.float32)
        back_in = jnp.transpose(input_grad.reshape(expert_count, N_EXPERT, MICRO, capacity, feature_width),
                                (1, 2, 0, 3, 4)).reshape(N_EXPERT, MICRO, expert_count * capacity, feature_width)
        back_gate = jnp.transpose(gate_grad.reshape(expert_count, N_EXPERT, MICRO, capacity),
                                  (1, 2, 0, 3)).reshape(N_EXPERT, MICRO, expert_count * capacity)
        token_grad, gate_out = jax.vmap(jax.vmap(unpack))(back_in, back_gate, route_slot)
        return grad_total, (token_grad, gate_out)

    start = jnp.zeros((expert_count, 3, feature_width, FF), jnp.float32)
    grad_total, (token_grad, gate_out) = lax.scan(one_row, start, (blocks_in, blocks_cot, blocks_gate, blocks_ids))
    return (token_grad.reshape(TOKENS, feature_width), gate_out.reshape(TOKENS, 2), grad_total.astype(jnp.bfloat16))
```

```python
import functools

import jax
import jax.numpy as jnp
from jax import lax
from jax.experimental import pallas as pl
from jax.experimental.pallas import tpu as pltpu
from jax.sharding import PartitionSpec as P

MICRO = 2
CORES = 2
META = 16
LAST = (((1,), (1,)), ((), ()))
FIRST = (((0,), (0,)), ((), ()))
F32 = jnp.float32
BF16 = jnp.bfloat16


def dot(lhs, rhs, dims=(((1,), (0,)), ((), ()))):
    return lax.dot_general(lhs, rhs, dims, preferred_element_type=F32)


def slot_kernel(choices, batch, capacity, middle, *refs):
    inputs = refs[: 4 * choices]
    w_hbm = refs[4 * choices]
    xr_out, q_out, h_out, da_out, db_out, dxa_out, dxb_out = refs[4 * choices + 1 : 4 * choices + 8]
    xbuf, cbuf, wbuf, sems = refs[4 * choices + 8 :]
    count = MICRO * batch
    me = lax.axis_index("expert")

    def copies(choice):
        xa, xb, ca, cb = inputs[4 * choice : 4 * choice + 4]
        return [
            pltpu.make_async_copy(xa, xbuf.at[0], sems.at[0]),
            pltpu.make_async_copy(xb, xbuf.at[1], sems.at[1]),
            pltpu.make_async_copy(ca, cbuf.at[0], sems.at[2]),
            pltpu.make_async_copy(cb, cbuf.at[1], sems.at[3]),
        ]

    if choices == 1:
        for copy in copies(0):
            copy.start()
    else:
        place = me // CORES
        inner = (place >= middle[0]) & (place <= middle[1])

        @pl.when(inner)
        def _():
            for copy in copies(0):
                copy.start()

        @pl.when(jnp.logical_not(inner))
        def _():
            for copy in copies(1):
                copy.start()

    weight_copies = [
        pltpu.make_async_copy(w_hbm.at[0, i], wbuf.at[i], sems.at[4 + i]) for i in range(3)
    ]
    for copy in weight_copies:
        copy.start()
    waits = copies(0)
    waits[0].wait()
    waits[1].wait()

    mine = (me + 1).astype(F32)
    upper = (
        lax.broadcasted_iota(jnp.int32, (batch, batch), 0)
        < lax.broadcasted_iota(jnp.int32, (batch, batch), 1)
    ).astype(BF16)
    slot_of = lax.broadcasted_iota(jnp.int32, (capacity, batch), 0).astype(F32)
    parts = []
    for half in range(CORES):
        for micro in range(MICRO):
            rows = slice(micro * batch, (micro + 1) * batch)
            meta = xbuf[half, count : count + META, rows].astype(F32)
            first = meta[0:1] == mine
            second = meta[1:2] == mine
            chosen = jnp.where(first | second, 1.0, 0.0)
            rank = dot(jnp.broadcast_to(chosen, (8, batch)).astype(BF16), upper)[0:1]
            onehot = jnp.where(rank == slot_of, chosen, 0.0)
            gate = jnp.sum(
                onehot * (jnp.where(first, meta[2:3], 0.0) + jnp.where(second, meta[3:4], 0.0)),
                axis=1,
                keepdims=True,
            )
            place_at = len(parts) * capacity
            xr_out[place_at : place_at + capacity, :] = dot(
                onehot.astype(BF16), xbuf[half, rows, :]
            ).astype(BF16)
            parts.append((half, rows, onehot, gate, first, second))
    xr = xr_out[...]
    for copy in weight_copies:
        copy.wait()
    pre_gate = dot(xr, wbuf[0])
    pre_up = dot(xr, wbuf[1])
    sig = jax.nn.sigmoid(pre_gate)
    activated = pre_gate * sig
    hidden = (activated * pre_up).astype(BF16)
    h_out[...] = hidden
    output = dot(hidden, wbuf[2], LAST)
    waits[2].wait()
    waits[3].wait()
    gate_grads = []
    for number, (half, rows, onehot, gate, first, second) in enumerate(parts):
        places = slice(number * capacity, (number + 1) * capacity)
        cot = dot(onehot.astype(BF16), cbuf[half, rows, :])
        q_out[places, :] = (gate * cot).astype(BF16)
        gate_grads.append(jnp.sum(output[places] * cot, axis=1, keepdims=True))
    hidden_grad = dot(q_out[...], wbuf[2])
    da = (hidden_grad * pre_up * sig * (1.0 + pre_gate * (1.0 - sig))).astype(BF16)
    db = (hidden_grad * activated).astype(BF16)
    da_out[...] = da
    db_out[...] = db
    dx = (dot(da, wbuf[0], LAST) + dot(db, wbuf[1], LAST)).astype(BF16)
    line = lax.broadcasted_iota(jnp.int32, (META, batch), 0)
    outs = (dxa_out, dxb_out)
    for out in outs:
        out[count : count + META, :] = jnp.zeros((META, out.shape[1]), BF16)
    for number, (half, rows, onehot, gate, first, second) in enumerate(parts):
        places = slice(number * capacity, (number + 1) * capacity)
        outs[half][rows, :] = dot(onehot.astype(BF16), dx[places], FIRST).astype(BF16)
        spread = jnp.sum(onehot * gate_grads[number], axis=0, keepdims=True)
        values = jnp.where(line == 0, jnp.where(first, spread, 0.0), 0.0) + jnp.where(
            line == 1, jnp.where(second, spread, 0.0), 0.0
        )
        outs[half][count : count + META, rows] = values.astype(BF16)


def run_slot(alternatives, weights, batch, capacity, middle):
    choices = len(alternatives)
    rows, width = alternatives[0][0].shape
    count = MICRO * batch
    hidden_width = weights.shape[-1]
    slots = CORES * MICRO * capacity
    operands = [array for group in alternatives for array in group]
    shape = jax.ShapeDtypeStruct
    return pl.pallas_call(
        functools.partial(slot_kernel, choices, batch, capacity, middle),
        out_shape=[
            shape((slots, width), BF16),
            shape((slots, width), BF16),
            shape((slots, hidden_width), BF16),
            shape((slots, hidden_width), BF16),
            shape((slots, hidden_width), BF16),
            shape((rows, width), BF16),
            shape((rows, width), BF16),
        ],
        in_specs=[pl.BlockSpec(memory_space=pl.ANY)] * (len(operands) + 1),
        out_specs=[pl.BlockSpec(memory_space=pltpu.VMEM)] * 7,
        scratch_shapes=[
            pltpu.VMEM((CORES, rows, width), BF16),
            pltpu.VMEM((CORES, count, width), BF16),
            pltpu.VMEM(weights.shape[1:], BF16),
            pltpu.SemaphoreType.DMA((7,)),
        ],
        compiler_params=pltpu.CompilerParams(vmem_limit_bytes=40 * 1024 * 1024),
        cost_estimate=pl.CostEstimate(
            flops=18 * slots * width * hidden_width,
            bytes_accessed=2 * (weights.size + 6 * rows * width),
            transcendentals=slots * hidden_width,
        ),
        name="expert_block",
    )(*operands, weights)


def weight_kernel(pieces, *refs):
    lefts = refs[:pieces]
    rights = refs[pieces : 2 * pieces]
    a_send, a_keep, b_send, b_keep = refs[2 * pieces :]
    here = lax.axis_index("dp")
    quarter = lefts[0].shape[1] // 4
    half = rights[0].shape[1] // 2

    def block(place):
        at = pl.multiple_of((here ^ place) * quarter, quarter)
        total = None
        for left, right in zip(lefts, rights):
            term = dot(left[:, pl.ds(at, quarter)], right[...], FIRST)
            total = term if total is None else total + term
        return total.astype(BF16)

    value = block(3)
    a_send[0] = value[:, :half]
    b_send[0] = value[:, half:]
    value = block(1)
    a_send[1] = value[:, :half]
    b_keep[0] = value[:, half:]
    value = block(2)
    a_keep[0] = value[:, :half]
    b_send[1] = value[:, half:]
    value = block(0)
    a_keep[1] = value[:, :half]
    b_keep[1] = value[:, half:]


def run_weight(lefts, rights):
    width = lefts[0].shape[1]
    hidden_width = rights[0].shape[1]
    rows = sum(left.shape[0] for left in lefts)
    piece = jax.ShapeDtypeStruct((2, width // 4, hidden_width // 2), BF16)
    return pl.pallas_call(
        functools.partial(weight_kernel, len(lefts)),
        out_shape=[piece] * 4,
        in_specs=[pl.BlockSpec(memory_space=pltpu.VMEM)] * (2 * len(lefts)),
        out_specs=[pl.BlockSpec(memory_space=pltpu.VMEM)] * 4,
        compiler_params=pltpu.CompilerParams(vmem_limit_bytes=40 * 1024 * 1024),
        cost_estimate=pl.CostEstimate(
            flops=2 * rows * width * hidden_width,
            bytes_accessed=2 * (rows * (width + hidden_width) + width * hidden_width),
            transcendentals=0,
        ),
        name="weight_block",
    )(*lefts, *rights)


def add(*values):
    total = values[0].astype(F32)
    for value in values[1:]:
        total = total + value.astype(F32)
    return total.astype(BF16)


def on_device(tokens, cotangent, gates, expert_ids, expert_weights):
    devices = lax.axis_size("expert")
    chips = devices // CORES
    count, width = tokens.shape
    batch = count // MICRO
    capacity = 4 * batch // devices
    routing = jnp.concatenate([(expert_ids + 1).astype(BF16).T, gates.T], axis=0)
    routing = jnp.pad(routing, ((0, META - 4), (0, width - count)))
    own = (jnp.concatenate([tokens, routing], axis=0), cotangent)

    def move(value, pairs):
        full = [(a * CORES + k, b * CORES + k) for a, b in pairs for k in range(CORES)]
        return lax.ppermute(value, "expert", full)

    def swap(value):
        return lax.ppermute(value, "expert", [(i, i ^ 1) for i in range(devices)])

    def send(pair, pairs):
        return tuple(move(value, pairs) for value in pair)

    def both(pair):
        return (pair[0], swap(pair[0]), pair[1], swap(pair[1]))

    def compute(*alternatives):
        result = run_slot(
            [both(pair) for pair in alternatives], expert_weights, batch, capacity, (1, chips - 2)
        )
        return result[:5], (result[5], result[6])

    def joined(grads):
        return (grads[0], swap(grads[1]))

    ahead = [(z, (z + 1) % chips) for z in range(chips)]
    behind = [(b, a) for a, b in ahead]
    if chips == 4:
        outer = [(0, 1), (1, 0), (2, 3), (3, 2)]
        inner = [(1, 2), (2, 1)]
        to_ends = [(1, 0), (2, 3)]
        from_ends = [(0, 1), (3, 2)]
        second = send(own, inner)
        first = send(own, outer)
        third = send(second, to_ends)
        fourth = send(first, inner)
        fifth = send(fourth, to_ends)
        kept = []
        rows, own_grads = compute(own)
        kept.append(rows)
        rows, grads = compute(first)
        kept.append(rows)
        first_sum = joined(grads)
        rows, grads = compute(second, third)
        kept.append(rows)
        third_sum = joined(grads)
        rows, grads = compute(fourth, fifth)
        kept.append(rows)
        fourth_sum = joined(grads)
        own_sum = joined(own_grads)
        third_back = add(*third_sum)
        third_back = add(*third_sum, move(third_back, from_ends))
        third_back = move(third_back, inner)
        back = add(*fourth_sum)
        back = add(*fourth_sum, move(back, from_ends))
        back = add(*first_sum, move(back, inner))
        back = move(back, outer)
        total = add(*own_sum, third_back, back)
    else:
        kept = []
        rows, own_grads = compute(own)
        kept.append(rows)
        total = [*joined(own_grads)]
        reach = chips // 2
        for forth, back, steps in ((ahead, behind, reach), (behind, ahead, chips - 1 - reach)):
            current, sums = own, []
            for _ in range(steps):
                current = send(current, forth)
                rows, grads = compute(current)
                kept.append(rows)
                sums.append(joined(grads))
            value = None
            for pair in reversed(sums):
                value = move(add(*pair) if value is None else add(*pair, value), back)
            if value is not None:
                total.append(value)
        total = add(*total)
    tokens_grad = total[:count]
    gates_grad = total[count : count + 2, :count].T

    xr, q, h, da, db = zip(*kept)
    if lax.axis_size("dp") == 4:

        def across(value, bit):
            return lax.ppermute(value, "dp", [(i, i ^ bit) for i in range(4)])

        pieces = []
        for lefts, rights in ((xr, da), (xr, db), (q, h)):
            a_send, a_keep, b_send, b_keep = run_weight(lefts, rights)
            pieces.append((a_keep, across(a_send, 1), b_keep, across(b_send, 2)))
        ends = []
        for a_keep, a_came, b_keep, b_came in pieces:
            a_came = (add(a_keep[1], a_came[1]), across(add(a_keep[0], a_came[0]), 2))
            b_came = (add(b_keep[1], b_came[1]), across(add(b_keep[0], b_came[0]), 1))
            ends.append(jnp.concatenate([add(*a_came), add(*b_came)], axis=1))
        weights_grad = jnp.stack(ends)[None]
    else:
        whole = [jnp.concatenate(value, axis=0) for value in (xr, q, h, da, db)]
        partial = jnp.stack(
            [
                dot(whole[0], whole[3], FIRST),
                dot(whole[0], whole[4], FIRST),
                dot(whole[1], whole[2], FIRST),
            ]
        ).astype(BF16)
        weights_grad = lax.psum_scatter(
            partial[None], "dp", scatter_dimension=2, tiled=True
        )
    return tokens_grad, gates_grad, weights_grad


def solution(mesh):
    placed = (
        P(("dp", "expert"), None),
        P(("dp", "expert"), None),
        P(("dp", "expert"), None),
        P(("dp", "expert"), None),
        P("expert", None, None, None),
    )
    return jax.shard_map(
        on_device,
        mesh=mesh,
        in_specs=placed,
        out_specs=(
            P(("dp", "expert"), None),
            P(("dp", "expert"), None),
            P("expert", None, "dp", None),
        ),
        check_vma=False,
    )
```

```python
import functools

import jax
import jax.numpy as jnp
from jax import lax
from jax.experimental import pallas as pl
from jax.experimental.pallas import tpu as pltpu
from jax.sharding import PartitionSpec as P

MICRO = 2
CORES = 2
META = 16
LAST = (((1,), (1,)), ((), ()))
FIRST = (((0,), (0,)), ((), ()))
F32 = jnp.float32
BF16 = jnp.bfloat16


def dot(lhs, rhs, dims=(((1,), (0,)), ((), ()))):
    return lax.dot_general(lhs, rhs, dims, preferred_element_type=F32)


def slot_kernel(choices, batch, capacity, middle, *refs):
    inputs = refs[: 2 * choices]
    weights = refs[2 * choices]
    xr_out, q_out, h_out, da_out, db_out, dxa_out, dxb_out = refs[2 * choices + 1 : 2 * choices + 8]
    meta_buf, cot_buf = refs[2 * choices + 8 :]
    count = MICRO * batch
    me = lax.axis_index("expert")
    inner = (me // CORES >= middle[0]) & (me // CORES <= middle[1])

    def chosen_input(task):
        if choices == 1:
            task(inputs[:2])
        else:
            pl.when(inner)(lambda: task(inputs[:2]))
            pl.when(jnp.logical_not(inner))(lambda: task(inputs[2:]))

    def take_meta(pair):
        for half in range(CORES):
            meta_buf[half] = pair[half][count : count + META, :count]

    chosen_input(take_meta)
    mine = (me + 1).astype(F32)
    upper = (
        lax.broadcasted_iota(jnp.int32, (batch, batch), 0)
        < lax.broadcasted_iota(jnp.int32, (batch, batch), 1)
    ).astype(BF16)
    slot_of = lax.broadcasted_iota(jnp.int32, (capacity, batch), 0).astype(F32)
    parts = []
    for half in range(CORES):
        for micro in range(MICRO):
            rows = slice(micro * batch, (micro + 1) * batch)
            meta = meta_buf[half, :, rows].astype(F32)
            first = meta[0:1] == mine
            second = meta[1:2] == mine
            chosen = jnp.where(first | second, 1.0, 0.0)
            rank = dot(jnp.broadcast_to(chosen, (8, batch)).astype(BF16), upper)[0:1]
            onehot = jnp.where(rank == slot_of, chosen, 0.0)
            gate = jnp.sum(
                onehot * (jnp.where(first, meta[2:3], 0.0) + jnp.where(second, meta[3:4], 0.0)),
                axis=1,
                keepdims=True,
            )
            parts.append((half, rows, onehot, gate, first, second))

    def pack(pair):
        for number, (half, rows, onehot, gate, first, second) in enumerate(parts):
            places = slice(number * capacity, (number + 1) * capacity)
            pick = onehot.astype(BF16)
            xr_out[places, :] = dot(pick, pair[half][rows, :]).astype(BF16)
            cot = dot(pick, pair[half][count + META + rows.start : count + META + rows.stop, :])
            cot_buf[places, :] = cot
            q_out[places, :] = (gate * cot).astype(BF16)

    chosen_input(pack)
    xr = xr_out[...]
    pre_gate = dot(xr, weights[0, 0])
    pre_up = dot(xr, weights[0, 1])
    sig = jax.nn.sigmoid(pre_gate)
    activated = pre_gate * sig
    hidden = (activated * pre_up).astype(BF16)
    h_out[...] = hidden
    output = dot(hidden, weights[0, 2], LAST)
    gate_grad = jnp.sum(output * cot_buf[...], axis=1, keepdims=True)
    hidden_grad = dot(q_out[...], weights[0, 2])
    da = (hidden_grad * pre_up * sig * (1.0 + pre_gate * (1.0 - sig))).astype(BF16)
    db = (hidden_grad * activated).astype(BF16)
    da_out[...] = da
    db_out[...] = db
    dx = (dot(da, weights[0, 0], LAST) + dot(db, weights[0, 1], LAST)).astype(BF16)
    line = lax.broadcasted_iota(jnp.int32, (META, batch), 0)
    outs = (dxa_out, dxb_out)
    for out in outs:
        out[count : count + META, :] = jnp.zeros((META, out.shape[1]), BF16)
    for number, (half, rows, onehot, gate, first, second) in enumerate(parts):
        places = slice(number * capacity, (number + 1) * capacity)
        outs[half][rows, :] = dot(onehot.astype(BF16), dx[places], FIRST).astype(BF16)
        spread = jnp.sum(onehot * gate_grad[places], axis=0, keepdims=True)
        values = jnp.where(line == 0, jnp.where(first, spread, 0.0), 0.0) + jnp.where(
            line == 1, jnp.where(second, spread, 0.0), 0.0
        )
        outs[half][count : count + META, rows] = values.astype(BF16)


def run_slot(alternatives, weights, batch, capacity, middle):
    choices = len(alternatives)
    width = weights.shape[2]
    rows = MICRO * batch + META
    hidden_width = weights.shape[-1]
    slots = CORES * MICRO * capacity
    operands = [array for group in alternatives for array in group]
    shape = jax.ShapeDtypeStruct
    return pl.pallas_call(
        functools.partial(slot_kernel, choices, batch, capacity, middle),
        out_shape=[
            shape((slots, width), BF16),
            shape((slots, width), BF16),
            shape((slots, hidden_width), BF16),
            shape((slots, hidden_width), BF16),
            shape((slots, hidden_width), BF16),
            shape((rows, width), BF16),
            shape((rows, width), BF16),
        ],
        in_specs=[pl.BlockSpec(memory_space=pltpu.VMEM)] * (len(operands) + 1),
        out_specs=[pl.BlockSpec(memory_space=pltpu.VMEM)] * 7,
        scratch_shapes=[
            pltpu.VMEM((CORES, META, MICRO * batch), BF16),
            pltpu.VMEM((slots, width), F32),
        ],
        compiler_params=pltpu.CompilerParams(vmem_limit_bytes=24 * 1024 * 1024),
        cost_estimate=pl.CostEstimate(flops=1, bytes_accessed=1, transcendentals=0),
        name="expert_block",
    )(*operands, weights)


def weight_kernel(products, pieces, *refs):
    a_send, a_keep, b_send, b_keep = refs[2 * pieces * products :]
    here = lax.axis_index("dp")
    quarter = refs[0].shape[1] // 4
    half = refs[pieces].shape[1] // 2
    places = (
        (3, a_send, 0, b_send, 0),
        (1, a_send, 1, b_keep, 0),
        (2, a_keep, 0, b_send, 1),
        (0, a_keep, 1, b_keep, 1),
    )
    for place, a_out, a_at, b_out, b_at in places:
        at = pl.multiple_of((here ^ place) * quarter, quarter)
        for product in range(products):
            group = refs[2 * pieces * product : 2 * pieces * (product + 1)]
            total = None
            for left, right in zip(group[:pieces], group[pieces:]):
                term = dot(left[:, pl.ds(at, quarter)], right[...], FIRST)
                total = term if total is None else total + term
            value = total.astype(BF16)
            a_out[a_at, product] = value[:, :half]
            b_out[b_at, product] = value[:, half:]


def run_weight(*products):
    lefts, rights = products[0]
    width = lefts[0].shape[1]
    hidden_width = rights[0].shape[1]
    piece = jax.ShapeDtypeStruct((2, len(products), width // 4, hidden_width // 2), BF16)
    operands = [array for pair in products for group in pair for array in group]
    return pl.pallas_call(
        functools.partial(weight_kernel, len(products), len(lefts)),
        out_shape=[piece] * 4,
        in_specs=[pl.BlockSpec(memory_space=pltpu.VMEM)] * len(operands),
        out_specs=[pl.BlockSpec(memory_space=pltpu.VMEM)] * 4,
        compiler_params=pltpu.CompilerParams(vmem_limit_bytes=24 * 1024 * 1024),
        cost_estimate=pl.CostEstimate(flops=1, bytes_accessed=1, transcendentals=0),
        name="weight_block",
    )(*operands)


def add(*values):
    total = values[0].astype(F32)
    for value in values[1:]:
        total = total + value.astype(F32)
    return total.astype(BF16)


def after(value, *earlier):
    return lax.optimization_barrier((value, earlier))[0]


def on_device(tokens, cotangent, gates, expert_ids, expert_weights):
    devices = lax.axis_size("expert")
    chips = devices // CORES
    count, width = tokens.shape
    batch = count // MICRO
    capacity = 4 * batch // devices
    routing = jnp.concatenate([(expert_ids + 1).astype(BF16).T, gates.T], axis=0)
    routing = jnp.pad(routing, ((0, META - 4), (0, width - count)))
    own = jnp.concatenate([tokens, routing, cotangent], axis=0)

    def move(value, pairs):
        full = [(a * CORES + k, b * CORES + k) for a, b in pairs for k in range(CORES)]
        return lax.ppermute(value, "expert", full)

    def swap(value):
        return lax.ppermute(value, "expert", [(i, i ^ 1) for i in range(devices)])

    def compute(*alternatives):
        result = run_slot(alternatives, expert_weights, batch, capacity, (1, chips - 2))
        return result[:5], (result[5], result[6])

    def joined(grads):
        return (grads[0], swap(grads[1]))

    ahead = [(z, (z + 1) % chips) for z in range(chips)]
    behind = [(b, a) for a, b in ahead]
    if chips == 4:
        outer = [(0, 1), (1, 0), (2, 3), (3, 2)]
        inner = [(1, 2), (2, 1)]
        to_ends = [(1, 0), (2, 3)]
        from_ends = [(0, 1), (3, 2)]
        second = move(own, inner)
        first = move(own, outer)
        rows, grads = compute((own, swap(own)))
        kept = [rows]
        own_sum = joined(grads)
        second, first = after((second, first), own_sum[1])
        third = move(second, to_ends)
        fourth = move(first, inner)
        rows, grads = compute((first, swap(first)))
        kept.append(rows)
        first_sum = joined(grads)
        fourth, third = after((fourth, third), first_sum[1])
        fifth = move(fourth, to_ends)
        rows, grads = compute((second, swap(second)), (third, swap(third)))
        kept.append(rows)
        third_sum = joined(grads)
        came = move(add(*third_sum), from_ends)
        fifth = after(fifth, third_sum[1])
        third_back = move(add(*third_sum, came), inner)
        rows, grads = compute((fourth, swap(fourth)), (fifth, swap(fifth)))
        kept.append(rows)
        fourth_sum = joined(grads)
        back = sent = add(*fourth_sum)
        back = add(*fourth_sum, move(back, from_ends))
        back = add(*first_sum, move(back, inner))
        back = move(back, outer)
        total = add(*own_sum, third_back, back)
    else:
        rows, grads = compute((own, swap(own)))
        kept = [rows]
        sent = grads[0]
        total = [*joined(grads)]
        reach = chips // 2
        for forth, back, steps in ((ahead, behind, reach), (behind, ahead, chips - 1 - reach)):
            current, sums = own, []
            for _ in range(steps):
                current = move(current, forth)
                rows, grads = compute((current, swap(current)))
                kept.append(rows)
                sums.append(joined(grads))
            value = None
            for pair in reversed(sums):
                value = move(add(*pair) if value is None else add(*pair, value), back)
            if value is not None:
                total.append(value)
        total = add(*total)
    tokens_grad = total[:count]
    gates_grad = total[count : count + 2, :count].T

    xr, q, h, da, db = zip(*kept)
    if lax.axis_size("dp") == 4:

        def across(value, bit):
            return lax.ppermute(value, "dp", [(i, i ^ bit) for i in range(4)])

        ends = []
        for group in ([(q, h)], after([(xr, da), (xr, db)], sent)):
            a_send, a_keep, b_send, b_keep = run_weight(*group)
            a_came = across(a_send, 1)
            b_came = across(b_send, 2)
            a_last = across(add(a_keep[0], a_came[0]), 2)
            b_last = across(add(b_keep[0], b_came[0]), 1)
            ends.append(
                jnp.concatenate(
                    [add(a_keep[1], a_came[1], a_last), add(b_keep[1], b_came[1], b_last)], axis=-1
                )
            )
        weights_grad = jnp.concatenate([ends[1], ends[0]], axis=0)[None]
    else:
        whole = [jnp.concatenate(value, axis=0) for value in (xr, q, h, da, db)]
        partial = jnp.stack(
            [
                dot(whole[0], whole[3], FIRST),
                dot(whole[0], whole[4], FIRST),
                dot(whole[1], whole[2], FIRST),
            ]
        ).astype(BF16)
        weights_grad = lax.psum_scatter(
            partial[None], "dp", scatter_dimension=2, tiled=True
        )
    return tokens_grad, gates_grad, weights_grad


def solution(mesh):
    placed = (
        P(("dp", "expert"), None),
        P(("dp", "expert"), None),
        P(("dp", "expert"), None),
        P(("dp", "expert"), None),
        P("expert", None, None, None),
    )
    return jax.shard_map(
        on_device,
        mesh=mesh,
        in_specs=placed,
        out_specs=(
            P(("dp", "expert"), None),
            P(("dp", "expert"), None),
            P("expert", None, "dp", None),
        ),
        check_vma=False,
    )
```

```python
import functools

import jax
import jax.numpy as jnp
from jax import lax
from jax.experimental import pallas as pl
from jax.experimental.pallas import tpu as pltpu
from jax.sharding import PartitionSpec as P

MICRO = 2
CORES = 2
META = 16
LAST = (((1,), (1,)), ((), ()))
FIRST = (((0,), (0,)), ((), ()))
F32 = jnp.float32
BF16 = jnp.bfloat16


def dot(lhs, rhs, dims=(((1,), (0,)), ((), ()))):
    return lax.dot_general(lhs, rhs, dims, preferred_element_type=F32)


def slot_kernel(choices, batch, capacity, middle, *refs):
    inputs = refs[: 2 * choices]
    weights = refs[2 * choices]
    xr_out, q_out, h_out, da_out, db_out, dxa_out, dxb_out = refs[2 * choices + 1 : 2 * choices + 8]
    meta_buf, cot_buf = refs[2 * choices + 8 :]
    count = MICRO * batch
    me = lax.axis_index("expert")
    inner = (me // CORES >= middle[0]) & (me // CORES <= middle[1])

    def chosen_input(task):
        if choices == 1:
            task(inputs[:2])
        else:
            pl.when(inner)(lambda: task(inputs[:2]))
            pl.when(jnp.logical_not(inner))(lambda: task(inputs[2:]))

    def take_meta(pair):
        for half in range(CORES):
            meta_buf[half] = pair[half][count : count + META, :count]

    chosen_input(take_meta)
    mine = (me + 1).astype(F32)
    upper = (
        lax.broadcasted_iota(jnp.int32, (batch, batch), 0)
        < lax.broadcasted_iota(jnp.int32, (batch, batch), 1)
    ).astype(BF16)
    slot_of = lax.broadcasted_iota(jnp.int32, (capacity, batch), 0).astype(F32)
    parts = []
    for half in range(CORES):
        for micro in range(MICRO):
            rows = slice(micro * batch, (micro + 1) * batch)
            meta = meta_buf[half, :, rows].astype(F32)
            first = meta[0:1] == mine
            second = meta[1:2] == mine
            chosen = jnp.where(first | second, 1.0, 0.0)
            rank = dot(jnp.broadcast_to(chosen, (8, batch)).astype(BF16), upper)[0:1]
            onehot = jnp.where(rank == slot_of, chosen, 0.0)
            gate = jnp.sum(
                onehot * (jnp.where(first, meta[2:3], 0.0) + jnp.where(second, meta[3:4], 0.0)),
                axis=1,
                keepdims=True,
            )
            parts.append((half, rows, onehot, gate, first, second))

    def pack(pair):
        for number, (half, rows, onehot, gate, first, second) in enumerate(parts):
            places = slice(number * capacity, (number + 1) * capacity)
            pick = onehot.astype(BF16)
            xr_out[places, :] = dot(pick, pair[half][rows, :]).astype(BF16)
            cot = dot(pick, pair[half][count + META + rows.start : count + META + rows.stop, :])
            cot_buf[places, :] = cot
            q_out[places, :] = (gate * cot).astype(BF16)

    chosen_input(pack)
    xr = xr_out[...]
    pre_gate = dot(xr, weights[0, 0])
    pre_up = dot(xr, weights[0, 1])
    sig = jax.nn.sigmoid(pre_gate)
    activated = pre_gate * sig
    hidden = (activated * pre_up).astype(BF16)
    h_out[...] = hidden
    output = dot(hidden, weights[0, 2], LAST)
    gate_grad = jnp.sum(output * cot_buf[...], axis=1, keepdims=True)
    hidden_grad = dot(q_out[...], weights[0, 2])
    da = (hidden_grad * pre_up * sig * (1.0 + pre_gate * (1.0 - sig))).astype(BF16)
    db = (hidden_grad * activated).astype(BF16)
    da_out[...] = da
    db_out[...] = db
    dx = (dot(da, weights[0, 0], LAST) + dot(db, weights[0, 1], LAST)).astype(BF16)
    line = lax.broadcasted_iota(jnp.int32, (META, batch), 0)
    outs = (dxa_out, dxb_out)
    for out in outs:
        out[count : count + META, :] = jnp.zeros((META, out.shape[1]), BF16)
    for number, (half, rows, onehot, gate, first, second) in enumerate(parts):
        places = slice(number * capacity, (number + 1) * capacity)
        outs[half][rows, :] = dot(onehot.astype(BF16), dx[places], FIRST).astype(BF16)
        spread = jnp.sum(onehot * gate_grad[places], axis=0, keepdims=True)
        values = jnp.where(line == 0, jnp.where(first, spread, 0.0), 0.0) + jnp.where(
            line == 1, jnp.where(second, spread, 0.0), 0.0
        )
        outs[half][count : count + META, rows] = values.astype(BF16)


def run_slot(alternatives, weights, batch, capacity, middle):
    choices = len(alternatives)
    width = weights.shape[2]
    rows = MICRO * batch + META
    hidden_width = weights.shape[-1]
    slots = CORES * MICRO * capacity
    operands = [array for group in alternatives for array in group]
    shape = jax.ShapeDtypeStruct
    return pl.pallas_call(
        functools.partial(slot_kernel, choices, batch, capacity, middle),
        out_shape=[
            shape((slots, width), BF16),
            shape((slots, width), BF16),
            shape((slots, hidden_width), BF16),
            shape((slots, hidden_width), BF16),
            shape((slots, hidden_width), BF16),
            shape((rows, width), BF16),
            shape((rows, width), BF16),
        ],
        in_specs=[pl.BlockSpec(memory_space=pltpu.VMEM)] * (len(operands) + 1),
        out_specs=[pl.BlockSpec(memory_space=pltpu.VMEM)] * 7,
        scratch_shapes=[
            pltpu.VMEM((CORES, META, MICRO * batch), BF16),
            pltpu.VMEM((slots, width), F32),
        ],
        compiler_params=pltpu.CompilerParams(vmem_limit_bytes=24 * 1024 * 1024),
        cost_estimate=pl.CostEstimate(flops=1, bytes_accessed=1, transcendentals=0),
        name="expert_block",
    )(*operands, weights)


def partial_kernel(pieces, *refs):
    operands, out = refs[:-1], refs[-1]
    quarter = out.shape[1] // 4
    for at in range(0, out.shape[1], quarter):
        for product in range(out.shape[0]):
            group = operands[2 * pieces * product : 2 * pieces * (product + 1)]
            total = None
            for left, right in zip(group[:pieces], group[pieces:]):
                term = dot(left[:, at : at + quarter], right[...], FIRST)
                total = term if total is None else total + term
            out[product, at : at + quarter, :] = total


def run_partial(products):
    lefts, rights = products[0]
    operands = [array for pair in products for group in pair for array in group]
    whole = pl.BlockSpec(memory_space=pltpu.VMEM)
    shape = (len(products), lefts[0].shape[1], rights[0].shape[1])
    return pl.pallas_call(
        functools.partial(partial_kernel, len(lefts)),
        out_shape=jax.ShapeDtypeStruct(shape, F32),
        in_specs=[whole] * len(operands),
        out_specs=whole,
        compiler_params=pltpu.CompilerParams(vmem_limit_bytes=24 * 1024 * 1024),
        cost_estimate=pl.CostEstimate(flops=1, bytes_accessed=1, transcendentals=0),
        name="partial_weights",
    )(*operands)


def weight_kernel(*refs):
    operands = refs[:-5]
    partial, a_send, a_keep, b_send, b_keep = refs[-5:]
    here = lax.axis_index("dp")
    products, width, hidden_width = partial.shape
    quarter = width // 4
    half = hidden_width // 2
    places = (
        (3, a_send, 0, b_send, 0),
        (1, a_send, 1, b_keep, 0),
        (2, a_keep, 0, b_send, 1),
        (0, a_keep, 1, b_keep, 1),
    )
    for place, a_out, a_at, b_out, b_at in places:
        rows = pl.ds(pl.multiple_of((here ^ place) * quarter, quarter), quarter)
        for product in range(products):
            left, right = operands[2 * product : 2 * product + 2]
            value = (partial[product, rows, :] + dot(left[:, rows], right[...], FIRST)).astype(BF16)
            a_out[a_at, product] = value[:, :half]
            b_out[b_at, product] = value[:, half:]


def run_weight(products, partial):
    count, width, hidden_width = partial.shape
    piece = jax.ShapeDtypeStruct((2, count, width // 4, hidden_width // 2), BF16)
    operands = [array for pair in products for array in pair]
    whole = pl.BlockSpec(memory_space=pltpu.VMEM)
    return pl.pallas_call(
        weight_kernel,
        out_shape=[piece] * 4,
        in_specs=[whole] * (len(operands) + 1),
        out_specs=[whole] * 4,
        compiler_params=pltpu.CompilerParams(vmem_limit_bytes=24 * 1024 * 1024),
        cost_estimate=pl.CostEstimate(flops=1, bytes_accessed=1, transcendentals=0),
        name="weight_block",
    )(*operands, partial)


def add(*values):
    total = values[0].astype(F32)
    for value in values[1:]:
        total = total + value.astype(F32)
    return total.astype(BF16)


def final_kernel(a_keep, a_came, a_last, b_keep, b_came, b_last, out):
    half = out.shape[2] // 2
    out[:, :, :half] = (
        a_keep[1].astype(F32) + a_came[1].astype(F32) + a_last[...].astype(F32)
    ).astype(BF16)
    out[:, :, half:] = (
        b_keep[1].astype(F32) + b_came[1].astype(F32) + b_last[...].astype(F32)
    ).astype(BF16)


def run_final(*operands):
    products, rows, half = operands[2].shape
    whole = pl.BlockSpec(memory_space=pltpu.VMEM)
    return pl.pallas_call(
        final_kernel,
        out_shape=jax.ShapeDtypeStruct((products, rows, 2 * half), BF16),
        in_specs=[whole] * 6,
        out_specs=whole,
        compiler_params=pltpu.CompilerParams(vmem_limit_bytes=12 * 1024 * 1024),
        cost_estimate=pl.CostEstimate(flops=1, bytes_accessed=1, transcendentals=0),
        name="final_step",
    )(*operands)


def payload_kernel(tokens, cotangent, ids_hbm, gates_hbm, out, ids, gates, sems):
    count = tokens.shape[0]
    copies = [
        pltpu.make_async_copy(ids_hbm, ids, sems.at[2]),
        pltpu.make_async_copy(gates_hbm, gates, sems.at[3]),
        pltpu.make_async_copy(tokens, out.at[:count], sems.at[0]),
        pltpu.make_async_copy(cotangent, out.at[count + META :], sems.at[1]),
    ]
    for copy in copies:
        copy.start()
    copies[0].wait()
    copies[1].wait()
    line = lax.broadcasted_iota(jnp.int32, (META, count), 0)
    routing = jnp.zeros((META, count), F32)
    rows = (
        ids[0:1, :].astype(F32) + 1.0,
        ids[1:2, :].astype(F32) + 1.0,
        gates[0:1, :].astype(F32),
        gates[1:2, :].astype(F32),
    )
    for number, row in enumerate(rows):
        routing = jnp.where(line == number, row, routing)
    out[count : count + META, :] = jnp.zeros((META, out.shape[1]), BF16)
    out[count : count + META, :count] = routing.astype(BF16)
    copies[2].wait()
    copies[3].wait()


def make_payload(tokens, cotangent, gates, expert_ids):
    count, width = tokens.shape
    whole = pl.BlockSpec(memory_space=pltpu.VMEM)
    return pl.pallas_call(
        payload_kernel,
        out_shape=jax.ShapeDtypeStruct((2 * count + META, width), BF16),
        in_specs=[pl.BlockSpec(memory_space=pltpu.HBM)] * 4,
        out_specs=whole,
        scratch_shapes=[
            pltpu.VMEM((2, count), jnp.int32),
            pltpu.VMEM((2, count), BF16),
            pltpu.SemaphoreType.DMA((4,)),
        ],
        compiler_params=pltpu.CompilerParams(vmem_limit_bytes=4 * 1024 * 1024),
        cost_estimate=pl.CostEstimate(flops=1, bytes_accessed=1, transcendentals=0),
        name="payload",
    )(tokens, cotangent, expert_ids.T, gates.T)


def total_kernel(parts, *refs):
    values, (tokens_out, gates_out) = refs[:parts], refs[parts:]
    count = tokens_out.shape[0]
    total = values[0][...].astype(F32)
    for value in values[1:]:
        total = total + value[...].astype(F32)
    tokens_out[...] = total[:count].astype(BF16)
    gates_out[...] = total[count : count + META, :count].astype(BF16)[:2]


def split_total(values, count):
    width = values[0].shape[1]
    whole = pl.BlockSpec(memory_space=pltpu.VMEM)
    tokens_grad, gates_grad = pl.pallas_call(
        functools.partial(total_kernel, len(values)),
        out_shape=[
            jax.ShapeDtypeStruct((count, width), BF16),
            jax.ShapeDtypeStruct((2, count), BF16),
        ],
        in_specs=[whole] * len(values),
        out_specs=[whole] * 2,
        compiler_params=pltpu.CompilerParams(vmem_limit_bytes=8 * 1024 * 1024),
        cost_estimate=pl.CostEstimate(flops=1, bytes_accessed=1, transcendentals=0),
        name="total",
    )(*values)
    return tokens_grad, gates_grad.T


def after(value, *earlier):
    return lax.optimization_barrier((value, earlier))[0]


def products_of(rows):
    xr, q, h, da, db = rows
    return (xr, da), (xr, db), (q, h)


def sum_early(kept):
    return run_partial(
        [
            (tuple(pair[0] for pair in pairs), tuple(pair[1] for pair in pairs))
            for pairs in zip(*[products_of(rows) for rows in kept])
        ]
    )


def on_device(tokens, cotangent, gates, expert_ids, expert_weights):
    devices = lax.axis_size("expert")
    chips = devices // CORES
    count, width = tokens.shape
    batch = count // MICRO
    capacity = 4 * batch // devices
    own = make_payload(tokens, cotangent, gates, expert_ids)

    def move(value, pairs):
        full = [(a * CORES + k, b * CORES + k) for a, b in pairs for k in range(CORES)]
        return lax.ppermute(value, "expert", full)

    def swap(value):
        return lax.ppermute(value, "expert", [(i, i ^ 1) for i in range(devices)])

    def compute(*alternatives):
        result = run_slot(alternatives, expert_weights, batch, capacity, (1, chips - 2))
        return result[:5], (result[5], result[6])

    def joined(grads):
        return (grads[0], swap(grads[1]))

    ahead = [(z, (z + 1) % chips) for z in range(chips)]
    behind = [(b, a) for a, b in ahead]
    if chips == 4:
        outer = [(0, 1), (1, 0), (2, 3), (3, 2)]
        inner = [(1, 2), (2, 1)]
        to_ends = [(1, 0), (2, 3)]
        from_ends = [(0, 1), (3, 2)]
        second = move(own, inner)
        first = move(own, outer)
        rows, grads = compute((own, swap(own)))
        kept = [rows]
        own_sum = joined(grads)
        second, first = after((second, first), own_sum[1])
        third = move(second, to_ends)
        fourth = move(first, inner)
        rows, grads = compute((first, swap(first)))
        kept.append(rows)
        first_sum = joined(grads)
        fourth, third = after((fourth, third), first_sum[1])
        fifth = move(fourth, to_ends)
        rows, grads = compute((second, swap(second)), (third, swap(third)))
        kept.append(rows)
        third_sum = joined(grads)
        partial = sum_early(kept)
        fifth = after(fifth, third_sum[1], partial)
        rows, grads = compute((fourth, swap(fourth)), (fifth, swap(fifth)))
        kept.append(rows)
        fourth_sum = joined(grads)
        sent = add(*fourth_sum)
        landed = move(sent, from_ends)
        came = move(after(add(*third_sum), landed), from_ends)
        landed = move(add(*fourth_sum, landed), inner)
        third_back = move(after(add(*third_sum, came), landed), inner)
        back = move(add(*first_sum, landed), outer)
        total = [*own_sum, third_back, back]
    else:
        rows, grads = compute((own, swap(own)))
        kept = [rows]
        sent = grads[0]
        total = [*joined(grads)]
        reach = chips // 2
        for forth, back, steps in ((ahead, behind, reach), (behind, ahead, chips - 1 - reach)):
            current, sums = own, []
            for _ in range(steps):
                current = move(current, forth)
                rows, grads = compute((current, swap(current)))
                kept.append(rows)
                sums.append(joined(grads))
            value = None
            for pair in reversed(sums):
                value = move(add(*pair) if value is None else add(*pair, value), back)
            if value is not None:
                total.append(value)
        partial = sum_early(kept[:-1])
    tokens_grad, gates_grad = split_total(total, count)

    if lax.axis_size("dp") == 4:

        def across(value, bit):
            return lax.ppermute(value, "dp", [(i, i ^ bit) for i in range(4)])

        a_send, a_keep, b_send, b_keep = run_weight(products_of(kept[-1]), partial)
        a_came = across(a_send, 1)
        b_came = across(b_send, 2)
        a_last = across(add(a_keep[0], a_came[0]), 2)
        b_last = across(add(b_keep[0], b_came[0]), 1)
        weights_grad = run_final(a_keep, a_came, a_last, b_keep, b_came, b_last)[None]
    else:
        whole = [jnp.concatenate(value, axis=0) for value in zip(*kept)]
        partial = jnp.stack(
            [
                dot(whole[0], whole[3], FIRST),
                dot(whole[0], whole[4], FIRST),
                dot(whole[1], whole[2], FIRST),
            ]
        ).astype(BF16)
        weights_grad = lax.psum_scatter(
            partial[None], "dp", scatter_dimension=2, tiled=True
        )
    return tokens_grad, gates_grad, weights_grad


def solution(mesh):
    placed = (
        P(("dp", "expert"), None),
        P(("dp", "expert"), None),
        P(("dp", "expert"), None),
        P(("dp", "expert"), None),
        P("expert", None, None, None),
    )
    return jax.shard_map(
        on_device,
        mesh=mesh,
        in_specs=placed,
        out_specs=(
            P(("dp", "expert"), None),
            P(("dp", "expert"), None),
            P("expert", None, "dp", None),
        ),
        check_vma=False,
    )
```

```python
import functools

import jax
import jax.numpy as jnp
from jax import lax
from jax.experimental import pallas as pl
from jax.experimental.pallas import tpu as pltpu
from jax.sharding import PartitionSpec as P

MICRO = 2
CORES = 2
META = 16
LAST = (((1,), (1,)), ((), ()))
FIRST = (((0,), (0,)), ((), ()))
F32 = jnp.float32
BF16 = jnp.bfloat16


def dot(lhs, rhs, dims=(((1,), (0,)), ((), ()))):
    return lax.dot_general(lhs, rhs, dims, preferred_element_type=F32)


def slot_kernel(choices, batch, capacity, middle, *refs):
    inputs = refs[: 2 * choices]
    weights = refs[2 * choices]
    xr_out, q_out, h_out, da_out, db_out, dxa_out, dxb_out = refs[2 * choices + 1 : 2 * choices + 8]
    meta_buf, cot_buf = refs[2 * choices + 8 :]
    count = MICRO * batch
    me = lax.axis_index("expert")
    inner = (me // CORES >= middle[0]) & (me // CORES <= middle[1])

    def chosen_input(task):
        if choices == 1:
            task(inputs[:2])
        else:
            pl.when(inner)(lambda: task(inputs[:2]))
            pl.when(jnp.logical_not(inner))(lambda: task(inputs[2:]))

    def take_meta(pair):
        for half in range(CORES):
            meta_buf[half] = pair[half][count : count + META, :count]

    chosen_input(take_meta)
    mine = (me + 1).astype(F32)
    upper = (
        lax.broadcasted_iota(jnp.int32, (batch, batch), 0)
        < lax.broadcasted_iota(jnp.int32, (batch, batch), 1)
    ).astype(BF16)
    slot_of = lax.broadcasted_iota(jnp.int32, (capacity, batch), 0).astype(F32)
    parts = []
    for half in range(CORES):
        for micro in range(MICRO):
            rows = slice(micro * batch, (micro + 1) * batch)
            meta = meta_buf[half, :, rows].astype(F32)
            first = meta[0:1] == mine
            second = meta[1:2] == mine
            chosen = jnp.where(first | second, 1.0, 0.0)
            rank = dot(jnp.broadcast_to(chosen, (8, batch)).astype(BF16), upper)[0:1]
            onehot = jnp.where(rank == slot_of, chosen, 0.0)
            gate = jnp.sum(
                onehot * (jnp.where(first, meta[2:3], 0.0) + jnp.where(second, meta[3:4], 0.0)),
                axis=1,
                keepdims=True,
            )
            parts.append((half, rows, onehot, gate, first, second))

    def pack(pair):
        for number, (half, rows, onehot, gate, first, second) in enumerate(parts):
            places = slice(number * capacity, (number + 1) * capacity)
            pick = onehot.astype(BF16)
            xr_out[places, :] = dot(pick, pair[half][rows, :]).astype(BF16)
            cot = dot(pick, pair[half][count + META + rows.start : count + META + rows.stop, :])
            cot_buf[places, :] = cot
            q_out[places, :] = (gate * cot).astype(BF16)

    chosen_input(pack)
    xr = xr_out[...]
    pre_gate = dot(xr, weights[0, 0])
    pre_up = dot(xr, weights[0, 1])
    sig = jax.nn.sigmoid(pre_gate)
    activated = pre_gate * sig
    hidden = (activated * pre_up).astype(BF16)
    h_out[...] = hidden
    output = dot(hidden, weights[0, 2], LAST)
    gate_grad = jnp.sum(output * cot_buf[...], axis=1, keepdims=True)
    hidden_grad = dot(q_out[...], weights[0, 2])
    da = (hidden_grad * pre_up * sig * (1.0 + pre_gate * (1.0 - sig))).astype(BF16)
    db = (hidden_grad * activated).astype(BF16)
    da_out[...] = da
    db_out[...] = db
    dx = (dot(da, weights[0, 0], LAST) + dot(db, weights[0, 1], LAST)).astype(BF16)
    line = lax.broadcasted_iota(jnp.int32, (META, batch), 0)
    outs = (dxa_out, dxb_out)
    for out in outs:
        out[count : count + META, :] = jnp.zeros((META, out.shape[1]), BF16)
    for number, (half, rows, onehot, gate, first, second) in enumerate(parts):
        places = slice(number * capacity, (number + 1) * capacity)
        outs[half][rows, :] = dot(onehot.astype(BF16), dx[places], FIRST).astype(BF16)
        spread = jnp.sum(onehot * gate_grad[places], axis=0, keepdims=True)
        values = jnp.where(line == 0, jnp.where(first, spread, 0.0), 0.0) + jnp.where(
            line == 1, jnp.where(second, spread, 0.0), 0.0
        )
        outs[half][count : count + META, rows] = values.astype(BF16)


def run_slot(alternatives, weights, batch, capacity, middle):
    choices = len(alternatives)
    width = weights.shape[2]
    rows = MICRO * batch + META
    hidden_width = weights.shape[-1]
    slots = CORES * MICRO * capacity
    operands = [array for group in alternatives for array in group]
    shape = jax.ShapeDtypeStruct
    return pl.pallas_call(
        functools.partial(slot_kernel, choices, batch, capacity, middle),
        out_shape=[
            shape((slots, width), BF16),
            shape((slots, width), BF16),
            shape((slots, hidden_width), BF16),
            shape((slots, hidden_width), BF16),
            shape((slots, hidden_width), BF16),
            shape((rows, width), BF16),
            shape((rows, width), BF16),
        ],
        in_specs=[pl.BlockSpec(memory_space=pltpu.VMEM)] * (len(operands) + 1),
        out_specs=[pl.BlockSpec(memory_space=pltpu.VMEM)] * 7,
        scratch_shapes=[
            pltpu.VMEM((CORES, META, MICRO * batch), BF16),
            pltpu.VMEM((slots, width), F32),
        ],
        compiler_params=pltpu.CompilerParams(vmem_limit_bytes=24 * 1024 * 1024),
        cost_estimate=pl.CostEstimate(flops=1, bytes_accessed=1, transcendentals=0),
        name="expert_block",
    )(*operands, weights)


def partial_kernel(pieces, *refs):
    operands, out = refs[:-1], refs[-1]
    quarter = out.shape[1] // 4
    for at in range(0, out.shape[1], quarter):
        for product in range(out.shape[0]):
            group = operands[2 * pieces * product : 2 * pieces * (product + 1)]
            total = None
            for left, right in zip(group[:pieces], group[pieces:]):
                term = dot(left[:, at : at + quarter], right[...], FIRST)
                total = term if total is None else total + term
            out[product, at : at + quarter, :] = total


def run_partial(products):
    lefts, rights = products[0]
    operands = [array for pair in products for group in pair for array in group]
    whole = pl.BlockSpec(memory_space=pltpu.VMEM)
    shape = (len(products), lefts[0].shape[1], rights[0].shape[1])
    return pl.pallas_call(
        functools.partial(partial_kernel, len(lefts)),
        out_shape=jax.ShapeDtypeStruct(shape, F32),
        in_specs=[whole] * len(operands),
        out_specs=whole,
        compiler_params=pltpu.CompilerParams(vmem_limit_bytes=24 * 1024 * 1024),
        cost_estimate=pl.CostEstimate(flops=1, bytes_accessed=1, transcendentals=0),
        name="partial_weights",
    )(*operands)


def weight_kernel(*refs):
    operands = refs[:-5]
    partial, a_send, a_keep, b_send, b_keep = refs[-5:]
    here = lax.axis_index("dp")
    products, width, hidden_width = partial.shape
    quarter = width // 4
    half = hidden_width // 2
    places = (
        (3, a_send, 0, b_send, 0),
        (1, a_send, 1, b_keep, 0),
        (2, a_keep, 0, b_send, 1),
        (0, a_keep, 1, b_keep, 1),
    )
    for place, a_out, a_at, b_out, b_at in places:
        rows = pl.ds(pl.multiple_of((here ^ place) * quarter, quarter), quarter)
        for product in range(products):
            left, right = operands[2 * product : 2 * product + 2]
            value = (partial[product, rows, :] + dot(left[:, rows], right[...], FIRST)).astype(BF16)
            a_out[a_at, product] = value[:, :half]
            b_out[b_at, product] = value[:, half:]


def run_weight(products, partial):
    count, width, hidden_width = partial.shape
    piece = jax.ShapeDtypeStruct((2, count, width // 4, hidden_width // 2), BF16)
    operands = [array for pair in products for array in pair]
    whole = pl.BlockSpec(memory_space=pltpu.VMEM)
    return pl.pallas_call(
        weight_kernel,
        out_shape=[piece] * 4,
        in_specs=[whole] * (len(operands) + 1),
        out_specs=[whole] * 4,
        compiler_params=pltpu.CompilerParams(vmem_limit_bytes=24 * 1024 * 1024),
        cost_estimate=pl.CostEstimate(flops=1, bytes_accessed=1, transcendentals=0),
        name="weight_block",
    )(*operands, partial)


def add(*values):
    total = values[0].astype(F32)
    for value in values[1:]:
        total = total + value.astype(F32)
    return total.astype(BF16)


def final_kernel(a_keep, a_came, a_last, b_keep, b_came, b_last, out):
    half = out.shape[2] // 2
    out[:, :, :half] = (
        a_keep[1].astype(F32) + a_came[1].astype(F32) + a_last[...].astype(F32)
    ).astype(BF16)
    out[:, :, half:] = (
        b_keep[1].astype(F32) + b_came[1].astype(F32) + b_last[...].astype(F32)
    ).astype(BF16)


def run_final(*operands):
    products, rows, half = operands[2].shape
    whole = pl.BlockSpec(memory_space=pltpu.VMEM)
    return pl.pallas_call(
        final_kernel,
        out_shape=jax.ShapeDtypeStruct((products, rows, 2 * half), BF16),
        in_specs=[whole] * 6,
        out_specs=whole,
        compiler_params=pltpu.CompilerParams(vmem_limit_bytes=12 * 1024 * 1024),
        cost_estimate=pl.CostEstimate(flops=1, bytes_accessed=1, transcendentals=0),
        name="final_step",
    )(*operands)


def payload_kernel(tokens, cotangent, ids_hbm, gates_hbm, out, ids, gates, sems):
    count = tokens.shape[0]
    copies = [
        pltpu.make_async_copy(ids_hbm, ids, sems.at[2]),
        pltpu.make_async_copy(gates_hbm, gates, sems.at[3]),
        pltpu.make_async_copy(tokens, out.at[:count], sems.at[0]),
        pltpu.make_async_copy(cotangent, out.at[count + META :], sems.at[1]),
    ]
    for copy in copies:
        copy.start()
    copies[0].wait()
    copies[1].wait()
    line = lax.broadcasted_iota(jnp.int32, (META, count), 0)
    routing = jnp.zeros((META, count), F32)
    rows = (
        ids[0:1, :].astype(F32) + 1.0,
        ids[1:2, :].astype(F32) + 1.0,
        gates[0:1, :].astype(F32),
        gates[1:2, :].astype(F32),
    )
    for number, row in enumerate(rows):
        routing = jnp.where(line == number, row, routing)
    out[count : count + META, :] = jnp.zeros((META, out.shape[1]), BF16)
    out[count : count + META, :count] = routing.astype(BF16)
    copies[2].wait()
    copies[3].wait()


def make_payload(tokens, cotangent, gates, expert_ids):
    count, width = tokens.shape
    whole = pl.BlockSpec(memory_space=pltpu.VMEM)
    return pl.pallas_call(
        payload_kernel,
        out_shape=jax.ShapeDtypeStruct((2 * count + META, width), BF16),
        in_specs=[pl.BlockSpec(memory_space=pltpu.HBM)] * 4,
        out_specs=whole,
        scratch_shapes=[
            pltpu.VMEM((2, count), jnp.int32),
            pltpu.VMEM((2, count), BF16),
            pltpu.SemaphoreType.DMA((4,)),
        ],
        compiler_params=pltpu.CompilerParams(vmem_limit_bytes=60 * 1024 * 1024),
        cost_estimate=pl.CostEstimate(flops=1, bytes_accessed=1, transcendentals=0),
        name="payload",
    )(tokens, cotangent, expert_ids.T, gates.T)


def total_kernel(parts, *refs):
    values, (tokens_out, gates_out) = refs[:parts], refs[parts:]
    count = tokens_out.shape[0]
    total = values[0][...].astype(F32)
    for value in values[1:]:
        total = total + value[...].astype(F32)
    tokens_out[...] = total[:count].astype(BF16)
    gates_out[...] = total[count : count + META, :count].astype(BF16)[:2]


def split_total(values, count):
    width = values[0].shape[1]
    whole = pl.BlockSpec(memory_space=pltpu.VMEM)
    tokens_grad, gates_grad = pl.pallas_call(
        functools.partial(total_kernel, len(values)),
        out_shape=[
            jax.ShapeDtypeStruct((count, width), BF16),
            jax.ShapeDtypeStruct((2, count), BF16),
        ],
        in_specs=[whole] * len(values),
        out_specs=[whole] * 2,
        compiler_params=pltpu.CompilerParams(vmem_limit_bytes=8 * 1024 * 1024),
        cost_estimate=pl.CostEstimate(flops=1, bytes_accessed=1, transcendentals=0),
        name="total",
    )(*values)
    return tokens_grad, gates_grad.T


def after(value, *earlier):
    return lax.optimization_barrier((value, earlier))[0]


def products_of(rows):
    xr, q, h, da, db = rows
    return (xr, da), (xr, db), (q, h)


def sum_early(kept):
    return run_partial(
        [
            (tuple(pair[0] for pair in pairs), tuple(pair[1] for pair in pairs))
            for pairs in zip(*[products_of(rows) for rows in kept])
        ]
    )


def on_device(tokens, cotangent, gates, expert_ids, expert_weights):
    devices = lax.axis_size("expert")
    chips = devices // CORES
    count, width = tokens.shape
    batch = count // MICRO
    capacity = 4 * batch // devices
    own = make_payload(tokens, cotangent, gates, expert_ids)

    def move(value, pairs):
        full = [(a * CORES + k, b * CORES + k) for a, b in pairs for k in range(CORES)]
        return lax.ppermute(value, "expert", full)

    def swap(value):
        return lax.ppermute(value, "expert", [(i, i ^ 1) for i in range(devices)])

    def compute(*alternatives):
        result = run_slot(alternatives, expert_weights, batch, capacity, (1, chips - 2))
        return result[:5], (result[5], result[6])

    def joined(grads):
        return (grads[0], swap(grads[1]))

    ahead = [(z, (z + 1) % chips) for z in range(chips)]
    behind = [(b, a) for a, b in ahead]
    if chips == 4:
        outer = [(0, 1), (1, 0), (2, 3), (3, 2)]
        inner = [(1, 2), (2, 1)]
        to_ends = [(1, 0), (2, 3)]
        from_ends = [(0, 1), (3, 2)]
        across_all = [(0, 3), (3, 0)]
        first = move(own, outer)
        second = move(own, inner)
        far = move(own, across_all)
        rows, grads = compute((own, swap(own)))
        kept = [rows]
        own_sum = joined(grads)
        first, second, far = after((first, second, far), own_sum[1])
        third = move(second, to_ends)
        fourth = move(first, inner)
        rows, grads = compute((first, swap(first)))
        kept.append(rows)
        first_sum = joined(grads)
        rows, grads = compute((second, swap(second)), (far, swap(far)))
        kept.append(rows)
        far_sum = joined(grads)
        partial = sum_early(kept)
        third, fourth = after((third, fourth), first_sum[1], far_sum[1], partial)
        last = add(fourth, third)
        rows, grads = compute((last, swap(last)))
        kept.append(rows)
        last_sum = joined(grads)
        sent = add(*last_sum)
        if lax.axis_size("dp") == 4:
            pieces = run_weight(products_of(rows), partial)
            far_sum = after(far_sum, pieces[1])
        landed = move(sent, inner)
        came = move(sent, from_ends)
        far_back = move(add(*far_sum), across_all)
        second_back = move(after(add(*far_sum, came), far_back), inner)
        back = move(add(*first_sum, landed), outer)
        total = [*own_sum, second_back, back, far_back]
    else:
        rows, grads = compute((own, swap(own)))
        kept = [rows]
        sent = grads[0]
        total = [*joined(grads)]
        reach = chips // 2
        for forth, back, steps in ((ahead, behind, reach), (behind, ahead, chips - 1 - reach)):
            current, sums = own, []
            for _ in range(steps):
                current = move(current, forth)
                rows, grads = compute((current, swap(current)))
                kept.append(rows)
                sums.append(joined(grads))
            value = None
            for pair in reversed(sums):
                value = move(add(*pair) if value is None else add(*pair, value), back)
            if value is not None:
                total.append(value)
        if lax.axis_size("dp") == 4:
            pieces = run_weight(products_of(rows), sum_early(kept[:-1]))
    tokens_grad, gates_grad = split_total(total, count)

    if lax.axis_size("dp") == 4:

        def across(value, bit):
            return lax.ppermute(value, "dp", [(i, i ^ bit) for i in range(4)])

        a_send, a_keep, b_send, b_keep = pieces
        a_came = across(a_send, 1)
        b_came = across(b_send, 2)
        a_last = across(add(a_keep[0], a_came[0]), 2)
        b_last = across(add(b_keep[0], b_came[0]), 1)
        weights_grad = run_final(a_keep, a_came, a_last, b_keep, b_came, b_last)[None]
    else:
        whole = [jnp.concatenate(value, axis=0) for value in zip(*kept)]
        partial = jnp.stack(
            [
                dot(whole[0], whole[3], FIRST),
                dot(whole[0], whole[4], FIRST),
                dot(whole[1], whole[2], FIRST),
            ]
        ).astype(BF16)
        weights_grad = lax.psum_scatter(
            partial[None], "dp", scatter_dimension=2, tiled=True
        )
    return tokens_grad, gates_grad, weights_grad


def solution(mesh):
    placed = (
        P(("dp", "expert"), None),
        P(("dp", "expert"), None),
        P(("dp", "expert"), None),
        P(("dp", "expert"), None),
        P("expert", None, None, None),
    )
    return jax.shard_map(
        on_device,
        mesh=mesh,
        in_specs=placed,
        out_specs=(
            P(("dp", "expert"), None),
            P(("dp", "expert"), None),
            P("expert", None, "dp", None),
        ),
        check_vma=False,
    )
```

```python
import functools

import jax
import jax.numpy as jnp
from jax import lax
from jax.experimental import pallas as pl
from jax.experimental.pallas import tpu as pltpu
from jax.sharding import PartitionSpec as P

MICRO = 2
CORES = 2
META = 16
LAST = (((1,), (1,)), ((), ()))
FIRST = (((0,), (0,)), ((), ()))
F32 = jnp.float32
BF16 = jnp.bfloat16


def dot(lhs, rhs, dims=(((1,), (0,)), ((), ()))):
    return lax.dot_general(lhs, rhs, dims, preferred_element_type=F32)


def slot_kernel(choices, batch, capacity, middle, *refs):
    inputs = refs[: 2 * choices]
    weights = refs[2 * choices]
    xr_out, q_out, h_out, da_out, db_out, dxa_out, dxb_out = refs[2 * choices + 1 : 2 * choices + 8]
    meta_buf, cot_buf = refs[2 * choices + 8 :]
    count = MICRO * batch
    me = lax.axis_index("expert")
    inner = (me // CORES >= middle[0]) & (me // CORES <= middle[1])

    def chosen_input(task):
        if choices == 1:
            task(inputs[:2])
        else:
            pl.when(inner)(lambda: task(inputs[:2]))
            pl.when(jnp.logical_not(inner))(lambda: task(inputs[2:]))

    def take_meta(pair):
        for half in range(CORES):
            meta_buf[half] = pair[half][count : count + META, :count]

    chosen_input(take_meta)
    mine = (me + 1).astype(F32)
    upper = (
        lax.broadcasted_iota(jnp.int32, (batch, batch), 0)
        < lax.broadcasted_iota(jnp.int32, (batch, batch), 1)
    ).astype(BF16)
    slot_of = lax.broadcasted_iota(jnp.int32, (capacity, batch), 0).astype(F32)
    parts = []
    for half in range(CORES):
        for micro in range(MICRO):
            rows = slice(micro * batch, (micro + 1) * batch)
            meta = meta_buf[half, :, rows].astype(F32)
            first = meta[0:1] == mine
            second = meta[1:2] == mine
            chosen = jnp.where(first | second, 1.0, 0.0)
            rank = dot(jnp.broadcast_to(chosen, (8, batch)).astype(BF16), upper)[0:1]
            onehot = jnp.where(rank == slot_of, chosen, 0.0)
            gate = jnp.sum(
                onehot * (jnp.where(first, meta[2:3], 0.0) + jnp.where(second, meta[3:4], 0.0)),
                axis=1,
                keepdims=True,
            )
            parts.append((half, rows, onehot, gate, first, second))

    def pack(pair):
        for number, (half, rows, onehot, gate, first, second) in enumerate(parts):
            places = slice(number * capacity, (number + 1) * capacity)
            pick = onehot.astype(BF16)
            xr_out[places, :] = dot(pick, pair[half][rows, :]).astype(BF16)
            cot = dot(pick, pair[half][count + META + rows.start : count + META + rows.stop, :])
            cot_buf[places, :] = cot
            q_out[places, :] = (gate * cot).astype(BF16)

    chosen_input(pack)
    xr = xr_out[...]
    pre_gate = dot(xr, weights[0, 0])
    pre_up = dot(xr, weights[0, 1])
    sig = jax.nn.sigmoid(pre_gate)
    activated = pre_gate * sig
    hidden = (activated * pre_up).astype(BF16)
    h_out[...] = hidden
    output = dot(hidden, weights[0, 2], LAST)
    gate_grad = jnp.sum(output * cot_buf[...], axis=1, keepdims=True)
    hidden_grad = dot(q_out[...], weights[0, 2])
    da = (hidden_grad * pre_up * sig * (1.0 + pre_gate * (1.0 - sig))).astype(BF16)
    db = (hidden_grad * activated).astype(BF16)
    da_out[...] = da
    db_out[...] = db
    dx = (dot(da, weights[0, 0], LAST) + dot(db, weights[0, 1], LAST)).astype(BF16)
    line = lax.broadcasted_iota(jnp.int32, (META, batch), 0)
    outs = (dxa_out, dxb_out)
    for out in outs:
        out[count : count + META, :] = jnp.zeros((META, out.shape[1]), BF16)
    for number, (half, rows, onehot, gate, first, second) in enumerate(parts):
        places = slice(number * capacity, (number + 1) * capacity)
        outs[half][rows, :] = dot(onehot.astype(BF16), dx[places], FIRST).astype(BF16)
        spread = jnp.sum(onehot * gate_grad[places], axis=0, keepdims=True)
        values = jnp.where(line == 0, jnp.where(first, spread, 0.0), 0.0) + jnp.where(
            line == 1, jnp.where(second, spread, 0.0), 0.0
        )
        outs[half][count : count + META, rows] = values.astype(BF16)


def run_slot(alternatives, weights, batch, capacity, middle):
    choices = len(alternatives)
    width = weights.shape[2]
    rows = MICRO * batch + META
    hidden_width = weights.shape[-1]
    slots = CORES * MICRO * capacity
    operands = [array for group in alternatives for array in group]
    shape = jax.ShapeDtypeStruct
    return pl.pallas_call(
        functools.partial(slot_kernel, choices, batch, capacity, middle),
        out_shape=[
            shape((slots, width), BF16),
            shape((slots, width), BF16),
            shape((slots, hidden_width), BF16),
            shape((slots, hidden_width), BF16),
            shape((slots, hidden_width), BF16),
            shape((rows, width), BF16),
            shape((rows, width), BF16),
        ],
        in_specs=[pl.BlockSpec(memory_space=pltpu.VMEM)] * (len(operands) + 1),
        out_specs=[pl.BlockSpec(memory_space=pltpu.VMEM)] * 7,
        scratch_shapes=[
            pltpu.VMEM((CORES, META, MICRO * batch), BF16),
            pltpu.VMEM((slots, width), F32),
        ],
        compiler_params=pltpu.CompilerParams(vmem_limit_bytes=24 * 1024 * 1024),
        cost_estimate=pl.CostEstimate(flops=1, bytes_accessed=1, transcendentals=0),
        name="expert_block",
    )(*operands, weights)


def partial_kernel(pieces, *refs):
    operands, out = refs[:-1], refs[-1]
    quarter = out.shape[1] // 4
    for at in range(0, out.shape[1], quarter):
        for product in range(out.shape[0]):
            group = operands[2 * pieces * product : 2 * pieces * (product + 1)]
            total = None
            for left, right in zip(group[:pieces], group[pieces:]):
                term = dot(left[:, at : at + quarter], right[...], FIRST)
                total = term if total is None else total + term
            out[product, at : at + quarter, :] = total


def run_partial(products):
    lefts, rights = products[0]
    operands = [array for pair in products for group in pair for array in group]
    whole = pl.BlockSpec(memory_space=pltpu.VMEM)
    shape = (len(products), lefts[0].shape[1], rights[0].shape[1])
    return pl.pallas_call(
        functools.partial(partial_kernel, len(lefts)),
        out_shape=jax.ShapeDtypeStruct(shape, F32),
        in_specs=[whole] * len(operands),
        out_specs=whole,
        compiler_params=pltpu.CompilerParams(vmem_limit_bytes=24 * 1024 * 1024),
        cost_estimate=pl.CostEstimate(flops=1, bytes_accessed=1, transcendentals=0),
        name="partial_weights",
    )(*operands)


def weight_kernel(*refs):
    operands = refs[:-5]
    partial, a_send, a_keep, b_send, b_keep = refs[-5:]
    here = lax.axis_index("dp")
    products, width, hidden_width = partial.shape
    quarter = width // 4
    half = hidden_width // 2
    places = (
        (3, a_send, 0, b_send, 0),
        (1, a_send, 1, b_keep, 0),
        (2, a_keep, 0, b_send, 1),
        (0, a_keep, 1, b_keep, 1),
    )
    for place, a_out, a_at, b_out, b_at in places:
        rows = pl.ds(pl.multiple_of((here ^ place) * quarter, quarter), quarter)
        for product in range(products):
            left, right = operands[2 * product : 2 * product + 2]
            value = (partial[product, rows, :] + dot(left[:, rows], right[...], FIRST)).astype(BF16)
            a_out[a_at, product] = value[:, :half]
            b_out[b_at, product] = value[:, half:]


def run_weight(products, partial):
    count, width, hidden_width = partial.shape
    piece = jax.ShapeDtypeStruct((2, count, width // 4, hidden_width // 2), BF16)
    operands = [array for pair in products for array in pair]
    whole = pl.BlockSpec(memory_space=pltpu.VMEM)
    return pl.pallas_call(
        weight_kernel,
        out_shape=[piece] * 4,
        in_specs=[whole] * (len(operands) + 1),
        out_specs=[whole] * 4,
        compiler_params=pltpu.CompilerParams(vmem_limit_bytes=24 * 1024 * 1024),
        cost_estimate=pl.CostEstimate(flops=1, bytes_accessed=1, transcendentals=0),
        name="weight_block",
    )(*operands, partial)


def add(*values):
    total = values[0].astype(F32)
    for value in values[1:]:
        total = total + value.astype(F32)
    return total.astype(BF16)


def final_kernel(a_keep, a_came, a_last, b_keep, b_came, b_last, out):
    half = out.shape[2] // 2
    out[:, :, :half] = (
        a_keep[1].astype(F32) + a_came[1].astype(F32) + a_last[...].astype(F32)
    ).astype(BF16)
    out[:, :, half:] = (
        b_keep[1].astype(F32) + b_came[1].astype(F32) + b_last[...].astype(F32)
    ).astype(BF16)


def run_final(*operands):
    products, rows, half = operands[2].shape
    whole = pl.BlockSpec(memory_space=pltpu.VMEM)
    return pl.pallas_call(
        final_kernel,
        out_shape=jax.ShapeDtypeStruct((products, rows, 2 * half), BF16),
        in_specs=[whole] * 6,
        out_specs=whole,
        compiler_params=pltpu.CompilerParams(vmem_limit_bytes=12 * 1024 * 1024),
        cost_estimate=pl.CostEstimate(flops=1, bytes_accessed=1, transcendentals=0),
        name="final_step",
    )(*operands)


def payload_kernel(tokens, cotangent, ids_hbm, gates_hbm, out, ids, gates, held, sems):
    count = tokens.shape[0]
    small = [
        pltpu.make_async_copy(ids_hbm, ids, sems.at[0]),
        pltpu.make_async_copy(gates_hbm, gates, sems.at[1]),
    ]
    large = [
        pltpu.make_async_copy(tokens, held.at[:count], sems.at[2]),
        pltpu.make_async_copy(cotangent, held.at[count + META :], sems.at[3]),
    ]
    outward = [
        pltpu.make_async_copy(held.at[part], out.at[part], sems.at[4 + number])
        for number, part in enumerate(
            (pl.ds(0, count), pl.ds(count + META, count), pl.ds(count, META))
        )
    ]
    for copy in small + large:
        copy.start()
    for copy in small:
        copy.wait()
    line = lax.broadcasted_iota(jnp.int32, (META, count), 0)
    values = jnp.zeros((META, count), F32)
    rows = (
        ids[0:1, :].astype(F32) + 1.0,
        ids[1:2, :].astype(F32) + 1.0,
        gates[0:1, :].astype(F32),
        gates[1:2, :].astype(F32),
    )
    for number, row in enumerate(rows):
        values = jnp.where(line == number, row, values)
    held[count : count + META, :] = jnp.zeros((META, held.shape[1]), BF16)
    held[count : count + META, :count] = values.astype(BF16)
    outward[2].start()
    for came, sent in zip(large, outward):
        came.wait()
        sent.start()
    for copy in outward:
        copy.wait()


def make_payload(tokens, cotangent, gates, expert_ids):
    count, width = tokens.shape
    return pl.pallas_call(
        payload_kernel,
        out_shape=jax.ShapeDtypeStruct((2 * count + META, width), BF16),
        in_specs=[pl.BlockSpec(memory_space=pltpu.HBM)] * 4,
        out_specs=pl.BlockSpec(memory_space=pltpu.HBM),
        scratch_shapes=[
            pltpu.VMEM((2, count), jnp.int32),
            pltpu.VMEM((2, count), BF16),
            pltpu.VMEM((2 * count + META, width), BF16),
            pltpu.SemaphoreType.DMA((7,)),
        ],
        compiler_params=pltpu.CompilerParams(vmem_limit_bytes=60 * 1024 * 1024),
        cost_estimate=pl.CostEstimate(flops=1, bytes_accessed=1, transcendentals=0),
        name="payload",
    )(tokens, cotangent, expert_ids.T, gates.T)


def total_kernel(parts, *refs):
    values, (tokens_out, gates_out) = refs[:parts], refs[parts:]
    count = tokens_out.shape[0]
    total = values[0][...].astype(F32)
    for value in values[1:]:
        total = total + value[...].astype(F32)
    tokens_out[...] = total[:count].astype(BF16)
    gates_out[...] = total[count : count + META, :count].astype(BF16)[:2]


def split_total(values, count):
    width = values[0].shape[1]
    whole = pl.BlockSpec(memory_space=pltpu.VMEM)
    tokens_grad, gates_grad = pl.pallas_call(
        functools.partial(total_kernel, len(values)),
        out_shape=[
            jax.ShapeDtypeStruct((count, width), BF16),
            jax.ShapeDtypeStruct((2, count), BF16),
        ],
        in_specs=[whole] * len(values),
        out_specs=[whole] * 2,
        compiler_params=pltpu.CompilerParams(vmem_limit_bytes=8 * 1024 * 1024),
        cost_estimate=pl.CostEstimate(flops=1, bytes_accessed=1, transcendentals=0),
        name="total",
    )(*values)
    return tokens_grad, gates_grad.T


def after(value, *earlier):
    return lax.optimization_barrier((value, earlier))[0]


def products_of(rows):
    xr, q, h, da, db = rows
    return (xr, da), (xr, db), (q, h)


def sum_early(kept):
    return run_partial(
        [
            (tuple(pair[0] for pair in pairs), tuple(pair[1] for pair in pairs))
            for pairs in zip(*[products_of(rows) for rows in kept])
        ]
    )


def on_device(tokens, cotangent, gates, expert_ids, expert_weights):
    devices = lax.axis_size("expert")
    chips = devices // CORES
    count, width = tokens.shape
    batch = count // MICRO
    capacity = 4 * batch // devices
    own = make_payload(tokens, cotangent, gates, expert_ids)

    def across(value, bit):
        return lax.ppermute(value, "dp", [(i, i ^ bit) for i in range(4)])

    def first_step(rows, partial):
        a_send, a_keep, b_send, b_keep = run_weight(products_of(rows), partial)
        a_came = across(a_send, 1)
        b_came = across(b_send, 2)
        next_pair = (add(a_keep[0], a_came[0]), add(b_keep[0], b_came[0]))
        return (a_keep, a_came, b_keep, b_came), next_pair, a_keep

    def move(value, pairs):
        full = [(a * CORES + k, b * CORES + k) for a, b in pairs for k in range(CORES)]
        return lax.ppermute(value, "expert", full)

    def swap(value):
        return lax.ppermute(value, "expert", [(i, i ^ 1) for i in range(devices)])

    def compute(*alternatives):
        result = run_slot(alternatives, expert_weights, batch, capacity, (1, chips - 2))
        return result[:5], (result[5], result[6])

    def joined(grads):
        return (grads[0], swap(grads[1]))

    ahead = [(z, (z + 1) % chips) for z in range(chips)]
    behind = [(b, a) for a, b in ahead]
    if chips == 4:
        outer = [(0, 1), (1, 0), (2, 3), (3, 2)]
        inner = [(1, 2), (2, 1)]
        to_ends = [(1, 0), (2, 3)]
        from_ends = [(0, 1), (3, 2)]
        across_all = [(0, 3), (3, 0)]
        first = move(own, outer)
        second = move(own, inner)
        far = move(own, across_all)
        rows, grads = compute((own, swap(own)))
        kept = [rows]
        own_sum = joined(grads)
        first, second, far = after((first, second, far), own_sum[1])
        third = move(second, to_ends)
        fourth = move(first, inner)
        rows, grads = compute((first, swap(first)))
        kept.append(rows)
        first_sum = joined(grads)
        rows, grads = compute((second, swap(second)), (far, swap(far)))
        kept.append(rows)
        far_sum = joined(grads)
        partial = sum_early(kept)
        third, fourth = after((third, fourth), first_sum[1], far_sum[1], partial)
        last = add(fourth, third)
        rows, grads = compute((last, swap(last)))
        kept.append(rows)
        last_sum = joined(grads)
        sent = add(*last_sum)
        if lax.axis_size("dp") == 4:
            halves, next_pair, ready = first_step(rows, partial)
            far_sum = after(far_sum, ready)
        else:
            next_pair = ()
        landed = move(sent, inner)
        came = move(sent, from_ends)
        far_back = move(add(*far_sum), across_all)
        landed, came, far_back = after((landed, came, far_back), next_pair)
        back = move(add(*first_sum, landed), outer)
        second_back = move(add(*far_sum, came), inner)
        total = [*own_sum, second_back, back, far_back]
    else:
        rows, grads = compute((own, swap(own)))
        kept = [rows]
        sent = grads[0]
        total = [*joined(grads)]
        reach = chips // 2
        for forth, back, steps in ((ahead, behind, reach), (behind, ahead, chips - 1 - reach)):
            current, sums = own, []
            for _ in range(steps):
                current = move(current, forth)
                rows, grads = compute((current, swap(current)))
                kept.append(rows)
                sums.append(joined(grads))
            value = None
            for pair in reversed(sums):
                value = move(add(*pair) if value is None else add(*pair, value), back)
            if value is not None:
                total.append(value)
        if lax.axis_size("dp") == 4:
            halves, next_pair, _ = first_step(rows, sum_early(kept[:-1]))

    if lax.axis_size("dp") == 4:
        a_keep, a_came, b_keep, b_came = halves
        a_last = across(next_pair[0], 2)
        b_last = across(next_pair[1], 1)
        weights_grad = run_final(a_keep, a_came, a_last, b_keep, b_came, b_last)[None]
    else:
        whole = [jnp.concatenate(value, axis=0) for value in zip(*kept)]
        partial = jnp.stack(
            [
                dot(whole[0], whole[3], FIRST),
                dot(whole[0], whole[4], FIRST),
                dot(whole[1], whole[2], FIRST),
            ]
        ).astype(BF16)
        weights_grad = lax.psum_scatter(
            partial[None], "dp", scatter_dimension=2, tiled=True
        )
    total = after(total, weights_grad)
    tokens_grad, gates_grad = split_total(total, count)
    return tokens_grad, gates_grad, weights_grad


def solution(mesh):
    placed = (
        P(("dp", "expert"), None),
        P(("dp", "expert"), None),
        P(("dp", "expert"), None),
        P(("dp", "expert"), None),
        P("expert", None, None, None),
    )
    return jax.shard_map(
        on_device,
        mesh=mesh,
        in_specs=placed,
        out_specs=(
            P(("dp", "expert"), None),
            P(("dp", "expert"), None),
            P("expert", None, "dp", None),
        ),
        check_vma=False,
    )
```

```python
import functools

import jax
import jax.numpy as jnp
from jax import lax
from jax.experimental import pallas as pl
from jax.experimental.pallas import tpu as pltpu
from jax.sharding import PartitionSpec as P

MICRO = 2
CORES = 2
META = 8
LAST = (((1,), (1,)), ((), ()))
FIRST = (((0,), (0,)), ((), ()))
F32 = jnp.float32
BF16 = jnp.bfloat16


def dot(lhs, rhs, dims=(((1,), (0,)), ((), ()))):
    return lax.dot_general(lhs, rhs, dims, preferred_element_type=F32)


def slot_kernel(choices, batch, capacity, middle, *refs):
    inputs = refs[: 2 * choices]
    weights = refs[2 * choices]
    xr_out, q_out, h_out, da_out, db_out, dxa_out, dxb_out = refs[2 * choices + 1 : 2 * choices + 8]
    meta_buf, cot_buf = refs[2 * choices + 8 :]
    count = MICRO * batch
    me = lax.axis_index("expert")
    inner = (me // CORES >= middle[0]) & (me // CORES <= middle[1])

    def chosen_input(task):
        if choices == 1:
            task(inputs[:2])
        else:
            pl.when(inner)(lambda: task(inputs[:2]))
            pl.when(jnp.logical_not(inner))(lambda: task(inputs[2:]))

    def take_meta(pair):
        for half in range(CORES):
            meta_buf[half] = pair[half][2 * count : 2 * count + META, :count]

    chosen_input(take_meta)
    mine = (me + 1).astype(F32)
    upper = (
        lax.broadcasted_iota(jnp.int32, (batch, batch), 0)
        < lax.broadcasted_iota(jnp.int32, (batch, batch), 1)
    ).astype(BF16)
    slot_of = lax.broadcasted_iota(jnp.int32, (capacity, batch), 0).astype(F32)
    parts = []
    for half in range(CORES):
        for micro in range(MICRO):
            rows = slice(micro * batch, (micro + 1) * batch)
            meta = meta_buf[half, :, rows].astype(F32)
            first = meta[0:1] == mine
            second = meta[1:2] == mine
            chosen = jnp.where(first | second, 1.0, 0.0)
            rank = dot(jnp.broadcast_to(chosen, (8, batch)).astype(BF16), upper)[0:1]
            onehot = jnp.where(rank == slot_of, chosen, 0.0)
            gate = jnp.sum(
                onehot * (jnp.where(first, meta[2:3], 0.0) + jnp.where(second, meta[3:4], 0.0)),
                axis=1,
                keepdims=True,
            )
            parts.append((half, rows, onehot, gate, first, second))

    def pack(pair):
        for number, (half, rows, onehot, gate, first, second) in enumerate(parts):
            places = slice(number * capacity, (number + 1) * capacity)
            pick = onehot.astype(BF16)
            xr_out[places, :] = dot(pick, pair[half][rows, :]).astype(BF16)
            cot = dot(pick, pair[half][count + rows.start : count + rows.stop, :])
            cot_buf[places, :] = cot
            q_out[places, :] = (gate * cot).astype(BF16)

    chosen_input(pack)
    xr = xr_out[...]
    pre_gate = dot(xr, weights[0, 0])
    pre_up = dot(xr, weights[0, 1])
    sig = jax.nn.sigmoid(pre_gate)
    activated = pre_gate * sig
    hidden = (activated * pre_up).astype(BF16)
    h_out[...] = hidden
    output = dot(hidden, weights[0, 2], LAST)
    gate_grad = jnp.sum(output * cot_buf[...], axis=1, keepdims=True)
    hidden_grad = dot(q_out[...], weights[0, 2])
    da = (hidden_grad * pre_up * sig * (1.0 + pre_gate * (1.0 - sig))).astype(BF16)
    db = (hidden_grad * activated).astype(BF16)
    da_out[...] = da
    db_out[...] = db
    dx = (dot(da, weights[0, 0], LAST) + dot(db, weights[0, 1], LAST)).astype(BF16)
    line = lax.broadcasted_iota(jnp.int32, (META, batch), 0)
    outs = (dxa_out, dxb_out)
    for out in outs:
        out[count : count + META, :] = jnp.zeros((META, out.shape[1]), BF16)
    for number, (half, rows, onehot, gate, first, second) in enumerate(parts):
        places = slice(number * capacity, (number + 1) * capacity)
        outs[half][rows, :] = dot(onehot.astype(BF16), dx[places], FIRST).astype(BF16)
        spread = jnp.sum(onehot * gate_grad[places], axis=0, keepdims=True)
        values = jnp.where(line == 0, jnp.where(first, spread, 0.0), 0.0) + jnp.where(
            line == 1, jnp.where(second, spread, 0.0), 0.0
        )
        outs[half][count : count + META, rows] = values.astype(BF16)


def run_slot(alternatives, weights, batch, capacity, middle):
    choices = len(alternatives)
    width = weights.shape[2]
    rows = MICRO * batch + META
    hidden_width = weights.shape[-1]
    slots = CORES * MICRO * capacity
    operands = [array for group in alternatives for array in group]
    shape = jax.ShapeDtypeStruct
    return pl.pallas_call(
        functools.partial(slot_kernel, choices, batch, capacity, middle),
        out_shape=[
            shape((slots, width), BF16),
            shape((slots, width), BF16),
            shape((slots, hidden_width), BF16),
            shape((slots, hidden_width), BF16),
            shape((slots, hidden_width), BF16),
            shape((rows, width), BF16),
            shape((rows, width), BF16),
        ],
        in_specs=[pl.BlockSpec(memory_space=pltpu.VMEM)] * (len(operands) + 1),
        out_specs=[pl.BlockSpec(memory_space=pltpu.VMEM)] * 7,
        scratch_shapes=[
            pltpu.VMEM((CORES, META, MICRO * batch), BF16),
            pltpu.VMEM((slots, width), F32),
        ],
        compiler_params=pltpu.CompilerParams(vmem_limit_bytes=24 * 1024 * 1024),
        cost_estimate=pl.CostEstimate(flops=1, bytes_accessed=1, transcendentals=0),
        name="expert_block",
    )(*operands, weights)


def partial_kernel(pieces, *refs):
    operands, out = refs[:-1], refs[-1]
    quarter = out.shape[1] // 4
    for at in range(0, out.shape[1], quarter):
        for product in range(out.shape[0]):
            group = operands[2 * pieces * product : 2 * pieces * (product + 1)]
            total = None
            for left, right in zip(group[:pieces], group[pieces:]):
                term = dot(left[:, at : at + quarter], right[...], FIRST)
                total = term if total is None else total + term
            out[product, at : at + quarter, :] = total


def run_partial(products):
    lefts, rights = products[0]
    operands = [array for pair in products for group in pair for array in group]
    whole = pl.BlockSpec(memory_space=pltpu.VMEM)
    shape = (len(products), lefts[0].shape[1], rights[0].shape[1])
    return pl.pallas_call(
        functools.partial(partial_kernel, len(lefts)),
        out_shape=jax.ShapeDtypeStruct(shape, F32),
        in_specs=[whole] * len(operands),
        out_specs=whole,
        compiler_params=pltpu.CompilerParams(vmem_limit_bytes=24 * 1024 * 1024),
        cost_estimate=pl.CostEstimate(flops=1, bytes_accessed=1, transcendentals=0),
        name="partial_weights",
    )(*operands)


def weight_kernel(*refs):
    operands = refs[:-5]
    partial, a_send, a_keep, b_send, b_keep = refs[-5:]
    here = lax.axis_index("dp")
    products, width, hidden_width = partial.shape
    quarter = width // 4
    half = hidden_width // 2
    places = (
        (3, a_send, 0, b_send, 0),
        (1, a_send, 1, b_keep, 0),
        (2, a_keep, 0, b_send, 1),
        (0, a_keep, 1, b_keep, 1),
    )
    for place, a_out, a_at, b_out, b_at in places:
        rows = pl.ds(pl.multiple_of((here ^ place) * quarter, quarter), quarter)
        for product in range(products):
            left, right = operands[2 * product : 2 * product + 2]
            value = (partial[product, rows, :] + dot(left[:, rows], right[...], FIRST)).astype(BF16)
            a_out[a_at, product] = value[:, :half]
            b_out[b_at, product] = value[:, half:]


def run_weight(products, partial):
    count, width, hidden_width = partial.shape
    piece = jax.ShapeDtypeStruct((2, count, width // 4, hidden_width // 2), BF16)
    operands = [array for pair in products for array in pair]
    whole = pl.BlockSpec(memory_space=pltpu.VMEM)
    return pl.pallas_call(
        weight_kernel,
        out_shape=[piece] * 4,
        in_specs=[whole] * (len(operands) + 1),
        out_specs=[whole] * 4,
        compiler_params=pltpu.CompilerParams(vmem_limit_bytes=24 * 1024 * 1024),
        cost_estimate=pl.CostEstimate(flops=1, bytes_accessed=1, transcendentals=0),
        name="weight_block",
    )(*operands, partial)


def add(*values):
    total = values[0].astype(F32)
    for value in values[1:]:
        total = total + value.astype(F32)
    return total.astype(BF16)


def final_kernel(a_base, a_last, b_base, b_last, out):
    half = out.shape[2] // 2
    out[:, :, :half] = (a_base[...] + a_last[...].astype(F32)).astype(BF16)
    out[:, :, half:] = (b_base[...] + b_last[...].astype(F32)).astype(BF16)


def run_final(*operands):
    products, rows, half = operands[1].shape
    whole = pl.BlockSpec(memory_space=pltpu.VMEM)
    return pl.pallas_call(
        final_kernel,
        out_shape=jax.ShapeDtypeStruct((products, rows, 2 * half), BF16),
        in_specs=[whole] * 4,
        out_specs=whole,
        compiler_params=pltpu.CompilerParams(vmem_limit_bytes=12 * 1024 * 1024),
        cost_estimate=pl.CostEstimate(flops=1, bytes_accessed=1, transcendentals=0),
        name="final_step",
    )(*operands)


def payload_kernel(tokens, cotangent, ids_hbm, gates_hbm, out, ids, gates, held, sems):
    count = tokens.shape[0]
    small = [
        pltpu.make_async_copy(ids_hbm, ids, sems.at[0]),
        pltpu.make_async_copy(gates_hbm, gates, sems.at[1]),
    ]
    large = [
        pltpu.make_async_copy(tokens, held.at[:count], sems.at[2]),
        pltpu.make_async_copy(cotangent, held.at[count : 2 * count], sems.at[3]),
    ]
    outward = pltpu.make_async_copy(held, out, sems.at[4])
    for copy in small + large:
        copy.start()
    for copy in small:
        copy.wait()
    line = lax.broadcasted_iota(jnp.int32, (META, count), 0)
    values = jnp.zeros((META, count), F32)
    rows = (
        ids[0:1, :].astype(F32) + 1.0,
        ids[1:2, :].astype(F32) + 1.0,
        gates[0:1, :].astype(F32),
        gates[1:2, :].astype(F32),
    )
    for number, row in enumerate(rows):
        values = jnp.where(line == number, row, values)
    held[2 * count :, :] = jnp.zeros((META, held.shape[1]), BF16)
    held[2 * count :, :count] = values.astype(BF16)
    for copy in large:
        copy.wait()
    outward.start()
    outward.wait()


def make_payload(tokens, cotangent, gates, expert_ids):
    count, width = tokens.shape
    return pl.pallas_call(
        payload_kernel,
        out_shape=jax.ShapeDtypeStruct((2 * count + META, width), BF16),
        in_specs=[pl.BlockSpec(memory_space=pltpu.HBM)] * 4,
        out_specs=pl.BlockSpec(memory_space=pltpu.HBM),
        scratch_shapes=[
            pltpu.VMEM((2, count), jnp.int32),
            pltpu.VMEM((2, count), BF16),
            pltpu.VMEM((2 * count + META, width), BF16),
            pltpu.SemaphoreType.DMA((5,)),
        ],
        compiler_params=pltpu.CompilerParams(vmem_limit_bytes=60 * 1024 * 1024),
        cost_estimate=pl.CostEstimate(flops=1, bytes_accessed=1, transcendentals=0),
        name="payload",
    )(tokens, cotangent, expert_ids.T, gates.T)


def total_kernel(parts, *refs):
    values, (tokens_out, gates_out) = refs[:parts], refs[parts:]
    count = tokens_out.shape[0]
    total = values[0][...].astype(F32)
    for value in values[1:]:
        total = total + value[...].astype(F32)
    tokens_out[...] = total[:count].astype(BF16)
    gates_out[...] = total[count : count + META, :count].astype(BF16)[:2]


def split_total(values, count):
    width = values[0].shape[1]
    whole = pl.BlockSpec(memory_space=pltpu.VMEM)
    tokens_grad, gates_grad = pl.pallas_call(
        functools.partial(total_kernel, len(values)),
        out_shape=[
            jax.ShapeDtypeStruct((count, width), BF16),
            jax.ShapeDtypeStruct((2, count), BF16),
        ],
        in_specs=[whole] * len(values),
        out_specs=[whole] * 2,
        compiler_params=pltpu.CompilerParams(vmem_limit_bytes=8 * 1024 * 1024),
        cost_estimate=pl.CostEstimate(flops=1, bytes_accessed=1, transcendentals=0),
        name="total",
    )(*values)
    return tokens_grad, gates_grad.T


def after(value, *earlier):
    return lax.optimization_barrier((value, earlier))[0]


def products_of(rows):
    xr, q, h, da, db = rows
    return (xr, da), (xr, db), (q, h)


def sum_early(kept):
    return run_partial(
        [
            (tuple(pair[0] for pair in pairs), tuple(pair[1] for pair in pairs))
            for pairs in zip(*[products_of(rows) for rows in kept])
        ]
    )


def on_device(tokens, cotangent, gates, expert_ids, expert_weights):
    devices = lax.axis_size("expert")
    chips = devices // CORES
    count, width = tokens.shape
    batch = count // MICRO
    capacity = 4 * batch // devices
    own = make_payload(tokens, cotangent, gates, expert_ids)

    def across(value, bit):
        return lax.ppermute(value, "dp", [(i, i ^ bit) for i in range(4)])

    def first_step(rows, partial):
        a_send, a_keep, b_send, b_keep = run_weight(products_of(rows), partial)
        a_came = across(a_send, 1)
        b_came = across(b_send, 2)
        next_pair = (add(a_keep[0], a_came[0]), add(b_keep[0], b_came[0]))
        a_base = a_keep[1].astype(F32) + a_came[1].astype(F32)
        b_base = b_keep[1].astype(F32) + b_came[1].astype(F32)
        return (a_base, b_base), next_pair, a_keep

    def move(value, pairs):
        full = [(a * CORES + k, b * CORES + k) for a, b in pairs for k in range(CORES)]
        return lax.ppermute(value, "expert", full)

    def swap(value):
        return lax.ppermute(value, "expert", [(i, i ^ 1) for i in range(devices)])

    def compute(*alternatives):
        result = run_slot(alternatives, expert_weights, batch, capacity, (1, chips - 2))
        return result[:5], (result[5], result[6])

    def joined(grads):
        return (grads[0], swap(grads[1]))

    ahead = [(z, (z + 1) % chips) for z in range(chips)]
    behind = [(b, a) for a, b in ahead]
    if chips == 4:
        outer = [(0, 1), (1, 0), (2, 3), (3, 2)]
        inner = [(1, 2), (2, 1)]
        to_ends = [(1, 0), (2, 3)]
        from_ends = [(0, 1), (3, 2)]
        across_all = [(0, 3), (3, 0)]
        first = move(own, outer)
        second = move(own, inner)
        far = move(own, across_all)
        rows, grads = compute((own, swap(own)))
        kept = [rows]
        own_sum = joined(grads)
        first, second, far = after((first, second, far), own_sum[1])
        third = move(second, to_ends)
        fourth = move(first, inner)
        rows, grads = compute((first, swap(first)))
        kept.append(rows)
        first_sum = joined(grads)
        rows, grads = compute((second, swap(second)), (far, swap(far)))
        kept.append(rows)
        far_sum = joined(grads)
        partial = sum_early(kept)
        third, fourth = after((third, fourth), first_sum[1], far_sum[1], partial)
        last = add(fourth, third)
        rows, grads = compute((last, swap(last)))
        kept.append(rows)
        last_sum = joined(grads)
        sent = add(*last_sum)
        if lax.axis_size("dp") == 4:
            bases, next_pair, ready = first_step(rows, partial)
            far_sum = after(far_sum, ready)
        else:
            next_pair = ()
        landed = move(sent, inner)
        came = move(sent, from_ends)
        far_back = move(add(*far_sum), across_all)
        landed, came, far_back = after((landed, came, far_back), next_pair)
        back = move(add(*first_sum, landed), outer)
        second_back = move(add(*far_sum, came), inner)
        total = [add(*own_sum, far_back), back, second_back]
    else:
        rows, grads = compute((own, swap(own)))
        kept = [rows]
        sent = grads[0]
        total = [*joined(grads)]
        reach = chips // 2
        for forth, back, steps in ((ahead, behind, reach), (behind, ahead, chips - 1 - reach)):
            current, sums = own, []
            for _ in range(steps):
                current = move(current, forth)
                rows, grads = compute((current, swap(current)))
                kept.append(rows)
                sums.append(joined(grads))
            value = None
            for pair in reversed(sums):
                value = move(add(*pair) if value is None else add(*pair, value), back)
            if value is not None:
                total.append(value)
        if lax.axis_size("dp") == 4:
            bases, next_pair, _ = first_step(rows, sum_early(kept[:-1]))

    if lax.axis_size("dp") == 4:
        a_base, b_base = bases
        a_last = across(next_pair[0], 2)
        b_last = across(next_pair[1], 1)
        weights_grad = run_final(a_base, a_last, b_base, b_last)[None]
    else:
        whole = [jnp.concatenate(value, axis=0) for value in zip(*kept)]
        partial = jnp.stack(
            [
                dot(whole[0], whole[3], FIRST),
                dot(whole[0], whole[4], FIRST),
                dot(whole[1], whole[2], FIRST),
            ]
        ).astype(BF16)
        weights_grad = lax.psum_scatter(
            partial[None], "dp", scatter_dimension=2, tiled=True
        )
    total = after(total, weights_grad)
    tokens_grad, gates_grad = split_total(total, count)
    return tokens_grad, gates_grad, weights_grad


def solution(mesh):
    placed = (
        P(("dp", "expert"), None),
        P(("dp", "expert"), None),
        P(("dp", "expert"), None),
        P(("dp", "expert"), None),
        P("expert", None, None, None),
    )
    return jax.shard_map(
        on_device,
        mesh=mesh,
        in_specs=placed,
        out_specs=(
            P(("dp", "expert"), None),
            P(("dp", "expert"), None),
            P("expert", None, "dp", None),
        ),
        check_vma=False,
    )
```

```python
import functools

import jax
import jax.numpy as jnp
from jax import lax
from jax.experimental import pallas as pl
from jax.experimental.pallas import tpu as pltpu
from jax.sharding import PartitionSpec as P

MICRO = 2
CORES = 2
META = 8
LAST = (((1,), (1,)), ((), ()))
FIRST = (((0,), (0,)), ((), ()))
F32 = jnp.float32
BF16 = jnp.bfloat16


def dot(lhs, rhs, dims=(((1,), (0,)), ((), ()))):
    return lax.dot_general(lhs, rhs, dims, preferred_element_type=F32)


def slot_kernel(choices, fused, batch, capacity, middle, *refs):
    inputs, rest = refs[: 2 * choices], refs[2 * choices :]
    weights, rest = rest[0], rest[1:]
    if fused:
        partial, pieces, rest = rest[0], rest[1:5], rest[5:]
        dxa_out, dxb_out, xr_out, q_out, h_out, da_out, db_out = rest[:7]
    else:
        xr_out, q_out, h_out, da_out, db_out, dxa_out, dxb_out = rest[:7]
    meta_buf, cot_buf = rest[7:]
    count = MICRO * batch
    me = lax.axis_index("expert")
    inner = (me // CORES >= middle[0]) & (me // CORES <= middle[1])

    def chosen_input(task):
        if choices == 1:
            task(inputs[:2])
        else:
            pl.when(inner)(lambda: task(inputs[:2]))
            pl.when(jnp.logical_not(inner))(lambda: task(inputs[2:]))

    def take_meta(pair):
        for half in range(CORES):
            meta_buf[half] = pair[half][2 * count : 2 * count + META, :count]

    chosen_input(take_meta)
    mine = (me + 1).astype(F32)
    upper = (
        lax.broadcasted_iota(jnp.int32, (batch, batch), 0)
        < lax.broadcasted_iota(jnp.int32, (batch, batch), 1)
    ).astype(BF16)
    slot_of = lax.broadcasted_iota(jnp.int32, (capacity, batch), 0).astype(F32)
    parts = []
    for half in range(CORES):
        for micro in range(MICRO):
            rows = slice(micro * batch, (micro + 1) * batch)
            meta = meta_buf[half, :, rows].astype(F32)
            first = meta[0:1] == mine
            second = meta[1:2] == mine
            chosen = jnp.where(first | second, 1.0, 0.0)
            rank = dot(jnp.broadcast_to(chosen, (8, batch)).astype(BF16), upper)[0:1]
            onehot = jnp.where(rank == slot_of, chosen, 0.0)
            gate = jnp.sum(
                onehot * (jnp.where(first, meta[2:3], 0.0) + jnp.where(second, meta[3:4], 0.0)),
                axis=1,
                keepdims=True,
            )
            parts.append((half, rows, onehot, gate, first, second))

    def pack(pair):
        for number, (half, rows, onehot, gate, first, second) in enumerate(parts):
            places = slice(number * capacity, (number + 1) * capacity)
            pick = onehot.astype(BF16)
            xr_out[places, :] = dot(pick, pair[half][rows, :]).astype(BF16)
            cot = dot(pick, pair[half][count + rows.start : count + rows.stop, :])
            cot_buf[places, :] = cot
            q_out[places, :] = (gate * cot).astype(BF16)

    chosen_input(pack)
    xr = xr_out[...]
    pre_gate = dot(xr, weights[0, 0])
    pre_up = dot(xr, weights[0, 1])
    sig = jax.nn.sigmoid(pre_gate)
    activated = pre_gate * sig
    hidden = (activated * pre_up).astype(BF16)
    h_out[...] = hidden
    output = dot(hidden, weights[0, 2], LAST)
    gate_grad = jnp.sum(output * cot_buf[...], axis=1, keepdims=True)
    hidden_grad = dot(q_out[...], weights[0, 2])
    da = (hidden_grad * pre_up * sig * (1.0 + pre_gate * (1.0 - sig))).astype(BF16)
    db = (hidden_grad * activated).astype(BF16)
    da_out[...] = da
    db_out[...] = db
    if fused:
        weight_sums(((xr_out, da_out), (xr_out, db_out), (q_out, h_out)), partial, *pieces)
    dx = (dot(da, weights[0, 0], LAST) + dot(db, weights[0, 1], LAST)).astype(BF16)
    line = lax.broadcasted_iota(jnp.int32, (META, batch), 0)
    outs = (dxa_out, dxb_out)
    for out in outs:
        out[count : count + META, :] = jnp.zeros((META, out.shape[1]), BF16)
    for number, (half, rows, onehot, gate, first, second) in enumerate(parts):
        places = slice(number * capacity, (number + 1) * capacity)
        outs[half][rows, :] = dot(onehot.astype(BF16), dx[places], FIRST).astype(BF16)
        spread = jnp.sum(onehot * gate_grad[places], axis=0, keepdims=True)
        values = jnp.where(line == 0, jnp.where(first, spread, 0.0), 0.0) + jnp.where(
            line == 1, jnp.where(second, spread, 0.0), 0.0
        )
        outs[half][count : count + META, rows] = values.astype(BF16)


def run_slot(alternatives, weights, batch, capacity, middle, partial=None):
    choices = len(alternatives)
    width = weights.shape[2]
    rows = MICRO * batch + META
    hidden_width = weights.shape[-1]
    slots = CORES * MICRO * capacity
    operands = [array for group in alternatives for array in group] + [weights]
    wide, narrow = (slots, width), (slots, hidden_width)
    packed = [wide, wide, narrow, narrow, narrow]
    returned = [(rows, width)] * 2
    scratch = [
        pltpu.VMEM((CORES, META, MICRO * batch), BF16),
        pltpu.VMEM(wide, F32),
    ]
    if partial is None:
        shapes = packed + returned
    else:
        operands.append(partial)
        shapes = [(2, partial.shape[0], width // 4, hidden_width // 2)] * 4 + returned
        scratch = [pltpu.VMEM(shape, BF16) for shape in packed] + scratch
    return pl.pallas_call(
        functools.partial(slot_kernel, choices, partial is not None, batch, capacity, middle),
        out_shape=[jax.ShapeDtypeStruct(shape, BF16) for shape in shapes],
        in_specs=[pl.BlockSpec(memory_space=pltpu.VMEM)] * len(operands),
        out_specs=[pl.BlockSpec(memory_space=pltpu.VMEM)] * len(shapes),
        scratch_shapes=scratch,
        compiler_params=pltpu.CompilerParams(
            vmem_limit_bytes=(24 if partial is None else 32) * 1024 * 1024
        ),
        cost_estimate=pl.CostEstimate(flops=1, bytes_accessed=1, transcendentals=0),
        name="expert_block",
    )(*operands)


def partial_kernel(pieces, *refs):
    operands, out = refs[:-1], refs[-1]
    quarter = out.shape[1] // 4
    for at in range(0, out.shape[1], quarter):
        for product in range(out.shape[0]):
            group = operands[2 * pieces * product : 2 * pieces * (product + 1)]
            total = None
            for left, right in zip(group[:pieces], group[pieces:]):
                term = dot(left[:, at : at + quarter], right[...], FIRST)
                total = term if total is None else total + term
            out[product, at : at + quarter, :] = total


def run_partial(products):
    lefts, rights = products[0]
    operands = [array for pair in products for group in pair for array in group]
    whole = pl.BlockSpec(memory_space=pltpu.VMEM)
    shape = (len(products), lefts[0].shape[1], rights[0].shape[1])
    return pl.pallas_call(
        functools.partial(partial_kernel, len(lefts)),
        out_shape=jax.ShapeDtypeStruct(shape, F32),
        in_specs=[whole] * len(operands),
        out_specs=whole,
        compiler_params=pltpu.CompilerParams(vmem_limit_bytes=24 * 1024 * 1024),
        cost_estimate=pl.CostEstimate(flops=1, bytes_accessed=1, transcendentals=0),
        name="partial_weights",
    )(*operands)


def weight_sums(products, partial, a_send, a_keep, b_send, b_keep):
    here = lax.axis_index("dp")
    width, hidden_width = partial.shape[1:]
    quarter = width // 4
    half = hidden_width // 2
    places = (
        (3, a_send, 0, b_send, 0),
        (1, a_send, 1, b_keep, 0),
        (2, a_keep, 0, b_send, 1),
        (0, a_keep, 1, b_keep, 1),
    )
    for place, a_out, a_at, b_out, b_at in places:
        rows = pl.ds(pl.multiple_of((here ^ place) * quarter, quarter), quarter)
        for product, (left, right) in enumerate(products):
            value = (partial[product, rows, :] + dot(left[:, rows], right[...], FIRST)).astype(BF16)
            a_out[a_at, product] = value[:, :half]
            b_out[b_at, product] = value[:, half:]


def add(*values):
    total = values[0].astype(F32)
    for value in values[1:]:
        total = total + value.astype(F32)
    return total.astype(BF16)


def final_kernel(a_base, a_last, b_base, b_last, out):
    half = out.shape[2] // 2
    out[:, :, :half] = (a_base[...] + a_last[...].astype(F32)).astype(BF16)
    out[:, :, half:] = (b_base[...] + b_last[...].astype(F32)).astype(BF16)


def run_final(*operands):
    products, rows, half = operands[1].shape
    whole = pl.BlockSpec(memory_space=pltpu.VMEM)
    return pl.pallas_call(
        final_kernel,
        out_shape=jax.ShapeDtypeStruct((products, rows, 2 * half), BF16),
        in_specs=[whole] * 4,
        out_specs=whole,
        compiler_params=pltpu.CompilerParams(vmem_limit_bytes=12 * 1024 * 1024),
        cost_estimate=pl.CostEstimate(flops=1, bytes_accessed=1, transcendentals=0),
        name="final_step",
    )(*operands)


def payload_kernel(tokens, cotangent, ids_hbm, gates_hbm, out, ids, gates, held, sems):
    count = tokens.shape[0]
    small = [
        pltpu.make_async_copy(ids_hbm, ids, sems.at[0]),
        pltpu.make_async_copy(gates_hbm, gates, sems.at[1]),
    ]
    large = [
        pltpu.make_async_copy(tokens, held.at[:count], sems.at[2]),
        pltpu.make_async_copy(cotangent, held.at[count : 2 * count], sems.at[3]),
    ]
    outward = pltpu.make_async_copy(held, out, sems.at[4])
    for copy in small + large:
        copy.start()
    for copy in small:
        copy.wait()
    line = lax.broadcasted_iota(jnp.int32, (META, count), 0)
    values = jnp.zeros((META, count), F32)
    rows = (
        ids[0:1, :].astype(F32) + 1.0,
        ids[1:2, :].astype(F32) + 1.0,
        gates[0:1, :].astype(F32),
        gates[1:2, :].astype(F32),
    )
    for number, row in enumerate(rows):
        values = jnp.where(line == number, row, values)
    held[2 * count :, :] = jnp.zeros((META, held.shape[1]), BF16)
    held[2 * count :, :count] = values.astype(BF16)
    for copy in large:
        copy.wait()
    outward.start()
    outward.wait()


def make_payload(tokens, cotangent, gates, expert_ids):
    count, width = tokens.shape
    return pl.pallas_call(
        payload_kernel,
        out_shape=jax.ShapeDtypeStruct((2 * count + META, width), BF16),
        in_specs=[pl.BlockSpec(memory_space=pltpu.HBM)] * 4,
        out_specs=pl.BlockSpec(memory_space=pltpu.HBM),
        scratch_shapes=[
            pltpu.VMEM((2, count), jnp.int32),
            pltpu.VMEM((2, count), BF16),
            pltpu.VMEM((2 * count + META, width), BF16),
            pltpu.SemaphoreType.DMA((5,)),
        ],
        compiler_params=pltpu.CompilerParams(vmem_limit_bytes=60 * 1024 * 1024),
        cost_estimate=pl.CostEstimate(flops=1, bytes_accessed=1, transcendentals=0),
        name="payload",
    )(tokens, cotangent, expert_ids.T, gates.T)


def total_kernel(parts, *refs):
    values, (tokens_out, gates_out) = refs[:parts], refs[parts:]
    count = tokens_out.shape[0]
    total = values[0][...].astype(F32)
    for value in values[1:]:
        total = total + value[...].astype(F32)
    tokens_out[...] = total[:count].astype(BF16)
    gates_out[...] = total[count : count + META, :count].astype(BF16)[:2]


def split_total(values, count):
    width = values[0].shape[1]
    whole = pl.BlockSpec(memory_space=pltpu.VMEM)
    tokens_grad, gates_grad = pl.pallas_call(
        functools.partial(total_kernel, len(values)),
        out_shape=[
            jax.ShapeDtypeStruct((count, width), BF16),
            jax.ShapeDtypeStruct((2, count), BF16),
        ],
        in_specs=[whole] * len(values),
        out_specs=[whole] * 2,
        compiler_params=pltpu.CompilerParams(vmem_limit_bytes=8 * 1024 * 1024),
        cost_estimate=pl.CostEstimate(flops=1, bytes_accessed=1, transcendentals=0),
        name="total",
    )(*values)
    return tokens_grad, gates_grad.T


def after(value, *earlier):
    return lax.optimization_barrier((value, earlier))[0]


def products_of(rows):
    xr, q, h, da, db = rows
    return (xr, da), (xr, db), (q, h)


def sum_early(kept):
    return run_partial(
        [
            (tuple(pair[0] for pair in pairs), tuple(pair[1] for pair in pairs))
            for pairs in zip(*[products_of(rows) for rows in kept])
        ]
    )


def on_device(tokens, cotangent, gates, expert_ids, expert_weights):
    devices = lax.axis_size("expert")
    chips = devices // CORES
    count, width = tokens.shape
    batch = count // MICRO
    capacity = 4 * batch // devices
    own = make_payload(tokens, cotangent, gates, expert_ids)

    def across(value, bit):
        return lax.ppermute(value, "dp", [(i, i ^ bit) for i in range(4)])

    def first_step(sums):
        a_send, a_keep, b_send, b_keep = sums
        a_came = across(a_send, 1)
        b_came = across(b_send, 2)
        next_pair = (add(a_keep[0], a_came[0]), add(b_keep[0], b_came[0]))
        a_base = a_keep[1].astype(F32) + a_came[1].astype(F32)
        b_base = b_keep[1].astype(F32) + b_came[1].astype(F32)
        return (a_base, b_base), next_pair, a_keep

    def move(value, pairs):
        full = [(a * CORES + k, b * CORES + k) for a, b in pairs for k in range(CORES)]
        return lax.ppermute(value, "expert", full)

    def swap(value):
        return lax.ppermute(value, "expert", [(i, i ^ 1) for i in range(devices)])

    def compute(*alternatives, partial=None):
        result = run_slot(alternatives, expert_weights, batch, capacity, (1, chips - 2), partial)
        return result[:-2], (result[-2], result[-1])

    def joined(grads):
        return (grads[0], swap(grads[1]))

    ahead = [(z, (z + 1) % chips) for z in range(chips)]
    behind = [(b, a) for a, b in ahead]
    tuned = chips == 4 and lax.axis_size("dp") == 4
    if tuned:
        outer = [(0, 1), (1, 0), (2, 3), (3, 2)]
        inner = [(1, 2), (2, 1)]
        to_ends = [(1, 0), (2, 3)]
        from_ends = [(0, 1), (3, 2)]
        across_all = [(0, 3), (3, 0)]
        first = move(own, outer)
        second = move(own, inner)
        far = move(own, across_all)
        rows, grads = compute((own, swap(own)))
        kept = [rows]
        own_sum = joined(grads)
        first, second, far = after((first, second, far), own_sum[1])
        third = move(second, to_ends)
        fourth = move(first, inner)
        rows, grads = compute((first, swap(first)))
        kept.append(rows)
        first_sum = joined(grads)
        rows, grads = compute((second, swap(second)), (far, swap(far)))
        kept.append(rows)
        far_sum = joined(grads)
        partial = sum_early(kept)
        third, fourth = after((third, fourth), first_sum[1], far_sum[1], partial)
        last = add(fourth, third)
        sums, grads = compute((last, swap(last)), partial=partial)
        last_sum = joined(grads)
        sent = add(*last_sum)
        bases, next_pair, ready = first_step(sums)
        far_sum = after(far_sum, ready)
        landed = move(sent, inner)
        came = move(sent, from_ends)
        far_back = move(add(*far_sum), across_all)
        landed, came, far_back = after((landed, came, far_back), next_pair)
        back = move(add(*first_sum, landed), outer)
        second_back = move(add(*far_sum, came), inner)
        total = [add(*own_sum, far_back), back, second_back]
    else:
        rows, grads = compute((own, swap(own)))
        kept = [rows]
        total = [*joined(grads)]
        reach = chips // 2
        for forth, back, steps in ((ahead, behind, reach), (behind, ahead, chips - 1 - reach)):
            current, sums = own, []
            for _ in range(steps):
                current = move(current, forth)
                rows, grads = compute((current, swap(current)))
                kept.append(rows)
                sums.append(joined(grads))
            value = None
            for pair in reversed(sums):
                value = move(add(*pair) if value is None else add(*pair, value), back)
            if value is not None:
                total.append(value)

    if tuned:
        a_base, b_base = bases
        a_last = across(next_pair[0], 2)
        b_last = across(next_pair[1], 1)
        weights_grad = run_final(a_base, a_last, b_base, b_last)[None]
    else:
        whole = [jnp.concatenate(value, axis=0) for value in zip(*kept)]
        partial = jnp.stack(
            [
                dot(whole[0], whole[3], FIRST),
                dot(whole[0], whole[4], FIRST),
                dot(whole[1], whole[2], FIRST),
            ]
        ).astype(BF16)
        weights_grad = lax.psum_scatter(
            partial[None], "dp", scatter_dimension=2, tiled=True
        )
    total = after(total, weights_grad)
    tokens_grad, gates_grad = split_total(total, count)
    return tokens_grad, gates_grad, weights_grad


def solution(mesh):
    placed = (
        P(("dp", "expert"), None),
        P(("dp", "expert"), None),
        P(("dp", "expert"), None),
        P(("dp", "expert"), None),
        P("expert", None, None, None),
    )
    return jax.shard_map(
        on_device,
        mesh=mesh,
        in_specs=placed,
        out_specs=(
            P(("dp", "expert"), None),
            P(("dp", "expert"), None),
            P("expert", None, "dp", None),
        ),
        check_vma=False,
    )
```

```python
import functools

import jax
import jax.numpy as jnp
from jax import lax
from jax.experimental import pallas as pl
from jax.experimental.pallas import tpu as pltpu
from jax.sharding import PartitionSpec as P

MICRO = 2
CORES = 2
META = 8
LAST = (((1,), (1,)), ((), ()))
FIRST = (((0,), (0,)), ((), ()))
F32 = jnp.float32
BF16 = jnp.bfloat16


def dot(lhs, rhs, dims=(((1,), (0,)), ((), ()))):
    return lax.dot_general(lhs, rhs, dims, preferred_element_type=F32)


def slot_kernel(choices, fused, batch, capacity, middle, *refs):
    inputs, rest = refs[: 2 * choices], refs[2 * choices :]
    weights, rest = rest[0], rest[1:]
    if fused:
        partial, pieces, rest = rest[0], rest[1:5], rest[5:]
        dxa_out, dxb_out, xr_out, q_out, h_out, da_out, db_out = rest[:7]
    else:
        xr_out, q_out, h_out, da_out, db_out, dxa_out, dxb_out = rest[:7]
    meta_buf, cot_buf = rest[7:]
    count = MICRO * batch
    me = lax.axis_index("expert")
    inner = (me // CORES >= middle[0]) & (me // CORES <= middle[1])

    def chosen_input(task):
        if choices == 1:
            task(inputs[:2])
        else:
            pl.when(inner)(lambda: task(inputs[:2]))
            pl.when(jnp.logical_not(inner))(lambda: task(inputs[2:]))

    def take_meta(pair):
        for half in range(CORES):
            meta_buf[half] = pair[half][2 * count : 2 * count + META, :count]

    chosen_input(take_meta)
    mine = (me + 1).astype(F32)
    upper = (
        lax.broadcasted_iota(jnp.int32, (batch, batch), 0)
        < lax.broadcasted_iota(jnp.int32, (batch, batch), 1)
    ).astype(BF16)
    slot_of = lax.broadcasted_iota(jnp.int32, (capacity, batch), 0).astype(F32)
    parts = []
    for half in range(CORES):
        for micro in range(MICRO):
            rows = slice(micro * batch, (micro + 1) * batch)
            meta = meta_buf[half, :, rows].astype(F32)
            first = meta[0:1] == mine
            second = meta[1:2] == mine
            chosen = jnp.where(first | second, 1.0, 0.0)
            rank = dot(jnp.broadcast_to(chosen, (8, batch)).astype(BF16), upper)[0:1]
            onehot = jnp.where(rank == slot_of, chosen, 0.0)
            gate = jnp.sum(
                onehot * (jnp.where(first, meta[2:3], 0.0) + jnp.where(second, meta[3:4], 0.0)),
                axis=1,
                keepdims=True,
            )
            parts.append((half, rows, onehot, gate, first, second))

    def pack(pair):
        for number, (half, rows, onehot, gate, first, second) in enumerate(parts):
            places = slice(number * capacity, (number + 1) * capacity)
            pick = onehot.astype(BF16)
            xr_out[places, :] = dot(pick, pair[half][rows, :]).astype(BF16)
            cot = dot(pick, pair[half][count + rows.start : count + rows.stop, :])
            cot_buf[places, :] = cot
            q_out[places, :] = (gate * cot).astype(BF16)

    chosen_input(pack)
    xr = xr_out[...]
    pre_gate = dot(xr, weights[0, 0])
    pre_up = dot(xr, weights[0, 1])
    sig = jax.nn.sigmoid(pre_gate)
    activated = pre_gate * sig
    hidden = (activated * pre_up).astype(BF16)
    h_out[...] = hidden
    output = dot(hidden, weights[0, 2], LAST)
    gate_grad = jnp.sum(output * cot_buf[...], axis=1, keepdims=True)
    hidden_grad = dot(q_out[...], weights[0, 2])
    da = (hidden_grad * pre_up * sig * (1.0 + pre_gate * (1.0 - sig))).astype(BF16)
    db = (hidden_grad * activated).astype(BF16)
    da_out[...] = da
    db_out[...] = db
    if fused:
        weight_sums(((xr_out, da_out), (xr_out, db_out), (q_out, h_out)), partial, *pieces)
    dx = (dot(da, weights[0, 0], LAST) + dot(db, weights[0, 1], LAST)).astype(BF16)
    line = lax.broadcasted_iota(jnp.int32, (META, batch), 0)
    outs = (dxa_out, dxb_out)
    for out in outs:
        out[count : count + META, :] = jnp.zeros((META, out.shape[1]), BF16)
    for number, (half, rows, onehot, gate, first, second) in enumerate(parts):
        places = slice(number * capacity, (number + 1) * capacity)
        outs[half][rows, :] = dot(onehot.astype(BF16), dx[places], FIRST).astype(BF16)
        spread = jnp.sum(onehot * gate_grad[places], axis=0, keepdims=True)
        values = jnp.where(line == 0, jnp.where(first, spread, 0.0), 0.0) + jnp.where(
            line == 1, jnp.where(second, spread, 0.0), 0.0
        )
        outs[half][count : count + META, rows] = values.astype(BF16)


def run_slot(alternatives, weights, batch, capacity, middle, partial=None):
    choices = len(alternatives)
    width = weights.shape[2]
    rows = MICRO * batch + META
    hidden_width = weights.shape[-1]
    slots = CORES * MICRO * capacity
    operands = [array for group in alternatives for array in group] + [weights]
    wide, narrow = (slots, width), (slots, hidden_width)
    packed = [wide, wide, narrow, narrow, narrow]
    returned = [(rows, width)] * 2
    scratch = [
        pltpu.VMEM((CORES, META, MICRO * batch), BF16),
        pltpu.VMEM(wide, F32),
    ]
    if partial is None:
        shapes = packed + returned
    else:
        operands.append(partial)
        shapes = [(2, partial.shape[0], width // 4, hidden_width // 2)] * 4 + returned
        scratch = [pltpu.VMEM(shape, BF16) for shape in packed] + scratch
    return pl.pallas_call(
        functools.partial(slot_kernel, choices, partial is not None, batch, capacity, middle),
        out_shape=[jax.ShapeDtypeStruct(shape, BF16) for shape in shapes],
        in_specs=[pl.BlockSpec(memory_space=pltpu.VMEM)] * len(operands),
        out_specs=[pl.BlockSpec(memory_space=pltpu.VMEM)] * len(shapes),
        scratch_shapes=scratch,
        compiler_params=pltpu.CompilerParams(
            vmem_limit_bytes=(24 if partial is None else 32) * 1024 * 1024
        ),
        cost_estimate=pl.CostEstimate(flops=1, bytes_accessed=1, transcendentals=0),
        name="expert_block",
    )(*operands)


def partial_kernel(pieces, *refs):
    operands, out = refs[:-1], refs[-1]
    quarter = out.shape[1] // 4
    for at in range(0, out.shape[1], quarter):
        for product in range(out.shape[0]):
            group = operands[2 * pieces * product : 2 * pieces * (product + 1)]
            total = None
            for left, right in zip(group[:pieces], group[pieces:]):
                term = dot(left[:, at : at + quarter], right[...], FIRST)
                total = term if total is None else total + term
            out[product, at : at + quarter, :] = total


def run_partial(products):
    lefts, rights = products[0]
    operands = [array for pair in products for group in pair for array in group]
    whole = pl.BlockSpec(memory_space=pltpu.VMEM)
    shape = (len(products), lefts[0].shape[1], rights[0].shape[1])
    return pl.pallas_call(
        functools.partial(partial_kernel, len(lefts)),
        out_shape=jax.ShapeDtypeStruct(shape, F32),
        in_specs=[whole] * len(operands),
        out_specs=whole,
        compiler_params=pltpu.CompilerParams(vmem_limit_bytes=24 * 1024 * 1024),
        cost_estimate=pl.CostEstimate(flops=1, bytes_accessed=1, transcendentals=0),
        name="partial_weights",
    )(*operands)


def weight_sums(products, partial, a_send, a_keep, b_send, b_keep):
    here = lax.axis_index("dp")
    width, hidden_width = partial.shape[1:]
    quarter = width // 4
    half = hidden_width // 2
    places = (
        (3, a_send, 0, b_send, 0),
        (1, a_send, 1, b_keep, 0),
        (2, a_keep, 0, b_send, 1),
        (0, a_keep, 1, b_keep, 1),
    )
    for place, a_out, a_at, b_out, b_at in places:
        rows = pl.ds(pl.multiple_of((here ^ place) * quarter, quarter), quarter)
        for product, (left, right) in enumerate(products):
            value = (partial[product, rows, :] + dot(left[:, rows], right[...], FIRST)).astype(BF16)
            a_out[a_at, product] = value[:, :half]
            b_out[b_at, product] = value[:, half:]


def add(*values):
    total = values[0].astype(F32)
    for value in values[1:]:
        total = total + value.astype(F32)
    return total.astype(BF16)


def final_kernel(a_base, a_last, b_base, b_last, out):
    half = out.shape[2] // 2
    out[:, :, :half] = (a_base[...] + a_last[...].astype(F32)).astype(BF16)
    out[:, :, half:] = (b_base[...] + b_last[...].astype(F32)).astype(BF16)


def run_final(*operands):
    products, rows, half = operands[1].shape
    whole = pl.BlockSpec(memory_space=pltpu.VMEM)
    return pl.pallas_call(
        final_kernel,
        out_shape=jax.ShapeDtypeStruct((products, rows, 2 * half), BF16),
        in_specs=[whole] * 4,
        out_specs=whole,
        compiler_params=pltpu.CompilerParams(vmem_limit_bytes=12 * 1024 * 1024),
        cost_estimate=pl.CostEstimate(flops=1, bytes_accessed=1, transcendentals=0),
        name="final_step",
    )(*operands)


def payload_kernel(tokens, cotangent, ids_hbm, gates_hbm, out, ids, gates, held, sems):
    count = tokens.shape[0]
    small = [
        pltpu.make_async_copy(ids_hbm, ids, sems.at[0]),
        pltpu.make_async_copy(gates_hbm, gates, sems.at[1]),
    ]
    large = [
        pltpu.make_async_copy(tokens, held.at[:count], sems.at[2]),
        pltpu.make_async_copy(cotangent, held.at[count : 2 * count], sems.at[3]),
    ]
    outward = pltpu.make_async_copy(held, out, sems.at[4])
    for copy in small + large:
        copy.start()
    for copy in small:
        copy.wait()
    line = lax.broadcasted_iota(jnp.int32, (META, count), 0)
    values = jnp.zeros((META, count), F32)
    rows = (
        ids[0:1, :].astype(F32) + 1.0,
        ids[1:2, :].astype(F32) + 1.0,
        gates[0:1, :].astype(F32),
        gates[1:2, :].astype(F32),
    )
    for number, row in enumerate(rows):
        values = jnp.where(line == number, row, values)
    held[2 * count :, :] = jnp.zeros((META, held.shape[1]), BF16)
    held[2 * count :, :count] = values.astype(BF16)
    for copy in large:
        copy.wait()
    outward.start()
    outward.wait()


def make_payload(tokens, cotangent, gates, expert_ids):
    count, width = tokens.shape
    return pl.pallas_call(
        payload_kernel,
        out_shape=jax.ShapeDtypeStruct((2 * count + META, width), BF16),
        in_specs=[pl.BlockSpec(memory_space=pltpu.HBM)] * 4,
        out_specs=pl.BlockSpec(memory_space=pltpu.HBM),
        scratch_shapes=[
            pltpu.VMEM((2, count), jnp.int32),
            pltpu.VMEM((2, count), BF16),
            pltpu.VMEM((2 * count + META, width), BF16),
            pltpu.SemaphoreType.DMA((5,)),
        ],
        compiler_params=pltpu.CompilerParams(vmem_limit_bytes=60 * 1024 * 1024),
        cost_estimate=pl.CostEstimate(flops=1, bytes_accessed=1, transcendentals=0),
        name="payload",
    )(tokens, cotangent, expert_ids.T, gates.T)


def total_kernel(parts, *refs):
    values, (tokens_out, gates_out) = refs[:parts], refs[parts:]
    count = tokens_out.shape[0]
    total = values[0][...].astype(F32)
    for value in values[1:]:
        total = total + value[...].astype(F32)
    tokens_out[...] = total[:count].astype(BF16)
    gates_out[...] = total[count : count + META, :count].astype(BF16)[:2]


def split_total(values, count):
    width = values[0].shape[1]
    whole = pl.BlockSpec(memory_space=pltpu.VMEM)
    tokens_grad, gates_grad = pl.pallas_call(
        functools.partial(total_kernel, len(values)),
        out_shape=[
            jax.ShapeDtypeStruct((count, width), BF16),
            jax.ShapeDtypeStruct((2, count), BF16),
        ],
        in_specs=[whole] * len(values),
        out_specs=[whole] * 2,
        compiler_params=pltpu.CompilerParams(vmem_limit_bytes=8 * 1024 * 1024),
        cost_estimate=pl.CostEstimate(flops=1, bytes_accessed=1, transcendentals=0),
        name="total",
    )(*values)
    return tokens_grad, gates_grad.T


def after(value, *earlier):
    return lax.optimization_barrier((value, earlier))[0]


def products_of(rows):
    xr, q, h, da, db = rows
    return (xr, da), (xr, db), (q, h)


def sum_early(kept):
    return run_partial(
        [
            (tuple(pair[0] for pair in pairs), tuple(pair[1] for pair in pairs))
            for pairs in zip(*[products_of(rows) for rows in kept])
        ]
    )


def on_device(tokens, cotangent, gates, expert_ids, expert_weights):
    devices = lax.axis_size("expert")
    chips = devices // CORES
    count, width = tokens.shape
    batch = count // MICRO
    capacity = 4 * batch // devices
    own = make_payload(tokens, cotangent, gates, expert_ids)

    def across(value, bit):
        return lax.ppermute(value, "dp", [(i, i ^ bit) for i in range(4)])

    def first_step(sums):
        a_send, a_keep, b_send, b_keep = sums
        a_came = across(a_send, 1)
        b_came = across(b_send, 2)
        next_pair = (add(a_keep[0], a_came[0]), add(b_keep[0], b_came[0]))
        a_base = a_keep[1].astype(F32) + a_came[1].astype(F32)
        b_base = b_keep[1].astype(F32) + b_came[1].astype(F32)
        return (a_base, b_base), next_pair, a_keep

    def move(value, pairs):
        full = [(a * CORES + k, b * CORES + k) for a, b in pairs for k in range(CORES)]
        return lax.ppermute(value, "expert", full)

    def swap(value):
        return lax.ppermute(value, "expert", [(i, i ^ 1) for i in range(devices)])

    def compute(*alternatives, partial=None):
        result = run_slot(alternatives, expert_weights, batch, capacity, (1, chips - 2), partial)
        return result[:-2], (result[-2], result[-1])

    def joined(grads):
        return (grads[0], swap(grads[1]))

    ahead = [(z, (z + 1) % chips) for z in range(chips)]
    behind = [(b, a) for a, b in ahead]
    tuned = chips == 4 and lax.axis_size("dp") == 4
    if tuned:
        outer = [(0, 1), (1, 0), (2, 3), (3, 2)]
        inner = [(1, 2), (2, 1)]
        to_ends = [(1, 0), (2, 3)]
        from_ends = [(0, 1), (3, 2)]
        across_all = [(0, 3), (3, 0)]
        first = move(own, outer)
        second = move(own, inner)
        far = move(own, across_all)
        rows, grads = compute((own, swap(own)))
        kept = [rows]
        own_sum = joined(grads)
        far, second, first = after((far, second, first), own_sum[1])
        third = move(second, to_ends)
        fourth = move(first, inner)
        rows, grads = compute((first, swap(first)))
        kept.append(rows)
        first_sum = joined(grads)
        rows, grads = compute((second, swap(second)), (far, swap(far)))
        kept.append(rows)
        far_sum = joined(grads)
        partial = sum_early(kept)
        third, fourth = after((third, fourth), first_sum[1], far_sum[1], partial)
        last = add(fourth, third)
        sums, grads = compute((last, swap(last)), partial=partial)
        last_sum = joined(grads)
        sent = add(*last_sum)
        bases, next_pair, ready = first_step(sums)
        far_sum = after(far_sum, ready)
        landed = move(sent, inner)
        came = move(sent, from_ends)
        far_back = move(add(*far_sum), across_all)
        landed, came, far_back = after((landed, came, far_back), next_pair)
        back = move(add(*first_sum, landed), outer)
        second_back = move(add(*far_sum, came), inner)
        total = [add(*own_sum, far_back), back, second_back]
    else:
        rows, grads = compute((own, swap(own)))
        kept = [rows]
        total = [*joined(grads)]
        reach = chips // 2
        for forth, back, steps in ((ahead, behind, reach), (behind, ahead, chips - 1 - reach)):
            current, sums = own, []
            for _ in range(steps):
                current = move(current, forth)
                rows, grads = compute((current, swap(current)))
                kept.append(rows)
                sums.append(joined(grads))
            value = None
            for pair in reversed(sums):
                value = move(add(*pair) if value is None else add(*pair, value), back)
            if value is not None:
                total.append(value)

    if tuned:
        a_base, b_base = bases
        a_last = across(next_pair[0], 2)
        b_last = across(next_pair[1], 1)
        weights_grad = run_final(a_base, a_last, b_base, b_last)[None]
    else:
        whole = [jnp.concatenate(value, axis=0) for value in zip(*kept)]
        partial = jnp.stack(
            [
                dot(whole[0], whole[3], FIRST),
                dot(whole[0], whole[4], FIRST),
                dot(whole[1], whole[2], FIRST),
            ]
        ).astype(BF16)
        weights_grad = lax.psum_scatter(
            partial[None], "dp", scatter_dimension=2, tiled=True
        )
    total = after(total, weights_grad)
    tokens_grad, gates_grad = split_total(total, count)
    return tokens_grad, gates_grad, weights_grad


def solution(mesh):
    placed = (
        P(("dp", "expert"), None),
        P(("dp", "expert"), None),
        P(("dp", "expert"), None),
        P(("dp", "expert"), None),
        P("expert", None, None, None),
    )
    return jax.shard_map(
        on_device,
        mesh=mesh,
        in_specs=placed,
        out_specs=(
            P(("dp", "expert"), None),
            P(("dp", "expert"), None),
            P("expert", None, "dp", None),
        ),
        check_vma=False,
    )
```

```python
import functools

import jax
import jax.numpy as jnp
from jax import lax
from jax.experimental import pallas as pl
from jax.experimental.pallas import tpu as pltpu
from jax.sharding import PartitionSpec as P

MICRO = 2
CORES = 2
META = 8
LAST = (((1,), (1,)), ((), ()))
FIRST = (((0,), (0,)), ((), ()))
F32 = jnp.float32
BF16 = jnp.bfloat16


def dot(lhs, rhs, dims=(((1,), (0,)), ((), ()))):
    return lax.dot_general(lhs, rhs, dims, preferred_element_type=F32)


def slot_kernel(choices, fused, batch, capacity, middle, *refs):
    inputs, rest = refs[: 2 * choices], refs[2 * choices :]
    weights, rest = rest[0], rest[1:]
    if fused:
        partial, pieces, rest = rest[0], rest[1:5], rest[5:]
        dxa_out, dxb_out, xr_out, q_out, h_out, da_out, db_out = rest[:7]
    else:
        xr_out, q_out, h_out, da_out, db_out, dxa_out, dxb_out = rest[:7]
    meta_buf, cot_buf = rest[7:]
    count = MICRO * batch
    me = lax.axis_index("expert")
    inner = (me // CORES >= middle[0]) & (me // CORES <= middle[1])

    def chosen_input(task):
        if choices == 1:
            task(inputs[:2])
        else:
            pl.when(inner)(lambda: task(inputs[:2]))
            pl.when(jnp.logical_not(inner))(lambda: task(inputs[2:]))

    def take_meta(pair):
        for half in range(CORES):
            meta_buf[half] = pair[half][2 * count : 2 * count + META, :count]

    chosen_input(take_meta)
    mine = (me + 1).astype(F32)
    upper = (
        lax.broadcasted_iota(jnp.int32, (batch, batch), 0)
        < lax.broadcasted_iota(jnp.int32, (batch, batch), 1)
    ).astype(BF16)
    slot_of = lax.broadcasted_iota(jnp.int32, (capacity, batch), 0).astype(F32)
    parts = []
    for half in range(CORES):
        for micro in range(MICRO):
            rows = slice(micro * batch, (micro + 1) * batch)
            meta = meta_buf[half, :, rows].astype(F32)
            first = meta[0:1] == mine
            second = meta[1:2] == mine
            chosen = jnp.where(first | second, 1.0, 0.0)
            rank = dot(jnp.broadcast_to(chosen, (8, batch)).astype(BF16), upper)[0:1]
            onehot = jnp.where(rank == slot_of, chosen, 0.0)
            gate = jnp.sum(
                onehot * (jnp.where(first, meta[2:3], 0.0) + jnp.where(second, meta[3:4], 0.0)),
                axis=1,
                keepdims=True,
            )
            parts.append((half, rows, onehot, gate, first, second))

    def pack(pair):
        for number, (half, rows, onehot, gate, first, second) in enumerate(parts):
            places = slice(number * capacity, (number + 1) * capacity)
            pick = onehot.astype(BF16)
            xr_out[places, :] = dot(pick, pair[half][rows, :]).astype(BF16)
            cot = dot(pick, pair[half][count + rows.start : count + rows.stop, :])
            cot_buf[places, :] = cot
            q_out[places, :] = (gate * cot).astype(BF16)

    chosen_input(pack)
    xr = xr_out[...]
    pre_gate = dot(xr, weights[0, 0])
    pre_up = dot(xr, weights[0, 1])
    sig = jax.nn.sigmoid(pre_gate)
    activated = pre_gate * sig
    hidden = (activated * pre_up).astype(BF16)
    h_out[...] = hidden
    output = dot(hidden, weights[0, 2], LAST)
    gate_grad = jnp.sum(output * cot_buf[...], axis=1, keepdims=True)
    hidden_grad = dot(q_out[...], weights[0, 2])
    da = (hidden_grad * pre_up * sig * (1.0 + pre_gate * (1.0 - sig))).astype(BF16)
    db = (hidden_grad * activated).astype(BF16)
    da_out[...] = da
    db_out[...] = db
    if fused:
        weight_sums(((xr_out, da_out), (xr_out, db_out), (q_out, h_out)), partial, *pieces)
    dx = (dot(da, weights[0, 0], LAST) + dot(db, weights[0, 1], LAST)).astype(BF16)
    line = lax.broadcasted_iota(jnp.int32, (META, batch), 0)
    outs = (dxa_out, dxb_out)
    for out in outs:
        out[count : count + META, :] = jnp.zeros((META, out.shape[1]), BF16)
    for number, (half, rows, onehot, gate, first, second) in enumerate(parts):
        places = slice(number * capacity, (number + 1) * capacity)
        outs[half][rows, :] = dot(onehot.astype(BF16), dx[places], FIRST).astype(BF16)
        spread = jnp.sum(onehot * gate_grad[places], axis=0, keepdims=True)
        values = jnp.where(line == 0, jnp.where(first, spread, 0.0), 0.0) + jnp.where(
            line == 1, jnp.where(second, spread, 0.0), 0.0
        )
        outs[half][count : count + META, rows] = values.astype(BF16)


def run_slot(alternatives, weights, batch, capacity, middle, partial=None):
    choices = len(alternatives)
    width = weights.shape[2]
    rows = MICRO * batch + META
    hidden_width = weights.shape[-1]
    slots = CORES * MICRO * capacity
    operands = [array for group in alternatives for array in group] + [weights]
    wide, narrow = (slots, width), (slots, hidden_width)
    packed = [wide, wide, narrow, narrow, narrow]
    returned = [(rows, width)] * 2
    scratch = [
        pltpu.VMEM((CORES, META, MICRO * batch), BF16),
        pltpu.VMEM(wide, F32),
    ]
    if partial is None:
        shapes = packed + returned
    else:
        operands.append(partial)
        shapes = [(2, partial.shape[0], width // 4, hidden_width // 2)] * 4 + returned
        scratch = [pltpu.VMEM(shape, BF16) for shape in packed] + scratch
    return pl.pallas_call(
        functools.partial(slot_kernel, choices, partial is not None, batch, capacity, middle),
        out_shape=[jax.ShapeDtypeStruct(shape, BF16) for shape in shapes],
        in_specs=[pl.BlockSpec(memory_space=pltpu.VMEM)] * len(operands),
        out_specs=[pl.BlockSpec(memory_space=pltpu.VMEM)] * len(shapes),
        scratch_shapes=scratch,
        compiler_params=pltpu.CompilerParams(
            vmem_limit_bytes=(24 if partial is None else 32) * 1024 * 1024
        ),
        cost_estimate=pl.CostEstimate(flops=1, bytes_accessed=1, transcendentals=0),
        name="expert_block",
    )(*operands)


def partial_kernel(pieces, *refs):
    operands, out = refs[:-1], refs[-1]
    quarter = out.shape[1] // 4
    for at in range(0, out.shape[1], quarter):
        for product in range(out.shape[0]):
            group = operands[2 * pieces * product : 2 * pieces * (product + 1)]
            total = None
            for left, right in zip(group[:pieces], group[pieces:]):
                term = dot(left[:, at : at + quarter], right[...], FIRST)
                total = term if total is None else total + term
            out[product, at : at + quarter, :] = total


def run_partial(products):
    lefts, rights = products[0]
    operands = [array for pair in products for group in pair for array in group]
    whole = pl.BlockSpec(memory_space=pltpu.VMEM)
    shape = (len(products), lefts[0].shape[1], rights[0].shape[1])
    return pl.pallas_call(
        functools.partial(partial_kernel, len(lefts)),
        out_shape=jax.ShapeDtypeStruct(shape, F32),
        in_specs=[whole] * len(operands),
        out_specs=whole,
        compiler_params=pltpu.CompilerParams(vmem_limit_bytes=24 * 1024 * 1024),
        cost_estimate=pl.CostEstimate(flops=1, bytes_accessed=1, transcendentals=0),
        name="partial_weights",
    )(*operands)


def weight_sums(products, partial, a_send, a_keep, b_send, b_keep):
    here = lax.axis_index("dp")
    width, hidden_width = partial.shape[1:]
    quarter = width // 4
    half = hidden_width // 2
    places = (
        (3, a_send, 0, b_send, 0),
        (1, a_send, 1, b_keep, 0),
        (2, a_keep, 0, b_send, 1),
        (0, a_keep, 1, b_keep, 1),
    )
    for place, a_out, a_at, b_out, b_at in places:
        rows = pl.ds(pl.multiple_of((here ^ place) * quarter, quarter), quarter)
        for product, (left, right) in enumerate(products):
            value = (partial[product, rows, :] + dot(left[:, rows], right[...], FIRST)).astype(BF16)
            a_out[a_at, product] = value[:, :half]
            b_out[b_at, product] = value[:, half:]


def add(*values):
    total = values[0].astype(F32)
    for value in values[1:]:
        total = total + value.astype(F32)
    return total.astype(BF16)


def final_kernel(a_base, a_last, b_base, b_last, out):
    half = out.shape[2] // 2
    out[:, :, :half] = (a_base[...] + a_last[...].astype(F32)).astype(BF16)
    out[:, :, half:] = (b_base[...] + b_last[...].astype(F32)).astype(BF16)


def run_final(*operands):
    products, rows, half = operands[1].shape
    whole = pl.BlockSpec(memory_space=pltpu.VMEM)
    return pl.pallas_call(
        final_kernel,
        out_shape=jax.ShapeDtypeStruct((products, rows, 2 * half), BF16),
        in_specs=[whole] * 4,
        out_specs=whole,
        compiler_params=pltpu.CompilerParams(vmem_limit_bytes=12 * 1024 * 1024),
        cost_estimate=pl.CostEstimate(flops=1, bytes_accessed=1, transcendentals=0),
        name="final_step",
    )(*operands)


def payload_kernel(tokens, cotangent, ids_hbm, gates_hbm, out, ids, gates, held, sems):
    count = tokens.shape[0]
    small = [
        pltpu.make_async_copy(ids_hbm, ids, sems.at[0]),
        pltpu.make_async_copy(gates_hbm, gates, sems.at[1]),
    ]
    large = [
        pltpu.make_async_copy(tokens, held.at[:count], sems.at[2]),
        pltpu.make_async_copy(cotangent, held.at[count : 2 * count], sems.at[3]),
    ]
    outward = pltpu.make_async_copy(held, out, sems.at[4])
    for copy in small + large:
        copy.start()
    for copy in small:
        copy.wait()
    line = lax.broadcasted_iota(jnp.int32, (META, count), 0)
    values = jnp.zeros((META, count), F32)
    rows = (
        ids[0:1, :].astype(F32) + 1.0,
        ids[1:2, :].astype(F32) + 1.0,
        gates[0:1, :].astype(F32),
        gates[1:2, :].astype(F32),
    )
    for number, row in enumerate(rows):
        values = jnp.where(line == number, row, values)
    held[2 * count :, :] = jnp.zeros((META, held.shape[1]), BF16)
    held[2 * count :, :count] = values.astype(BF16)
    for copy in large:
        copy.wait()
    outward.start()
    outward.wait()


def make_payload(tokens, cotangent, gates, expert_ids):
    count, width = tokens.shape
    return pl.pallas_call(
        payload_kernel,
        out_shape=jax.ShapeDtypeStruct((2 * count + META, width), BF16),
        in_specs=[pl.BlockSpec(memory_space=pltpu.HBM)] * 4,
        out_specs=pl.BlockSpec(memory_space=pltpu.HBM),
        scratch_shapes=[
            pltpu.VMEM((2, count), jnp.int32),
            pltpu.VMEM((2, count), BF16),
            pltpu.VMEM((2 * count + META, width), BF16),
            pltpu.SemaphoreType.DMA((5,)),
        ],
        compiler_params=pltpu.CompilerParams(vmem_limit_bytes=60 * 1024 * 1024),
        cost_estimate=pl.CostEstimate(flops=1, bytes_accessed=1, transcendentals=0),
        name="payload",
    )(tokens, cotangent, expert_ids.T, gates.T)


def total_kernel(parts, *refs):
    values, (tokens_out, gates_out) = refs[:parts], refs[parts:]
    count = tokens_out.shape[0]
    total = values[0][...].astype(F32)
    for value in values[1:]:
        total = total + value[...].astype(F32)
    tokens_out[...] = total[:count].astype(BF16)
    gates_out[...] = total[count : count + META, :count].astype(BF16)[:2]


def split_total(values, count):
    width = values[0].shape[1]
    whole = pl.BlockSpec(memory_space=pltpu.VMEM)
    tokens_grad, gates_grad = pl.pallas_call(
        functools.partial(total_kernel, len(values)),
        out_shape=[
            jax.ShapeDtypeStruct((count, width), BF16),
            jax.ShapeDtypeStruct((2, count), BF16),
        ],
        in_specs=[whole] * len(values),
        out_specs=[whole] * 2,
        compiler_params=pltpu.CompilerParams(vmem_limit_bytes=8 * 1024 * 1024),
        cost_estimate=pl.CostEstimate(flops=1, bytes_accessed=1, transcendentals=0),
        name="total",
    )(*values)
    return tokens_grad, gates_grad.T


def after(value, *earlier):
    return lax.optimization_barrier((value, earlier))[0]


def products_of(rows):
    xr, q, h, da, db = rows
    return (xr, da), (xr, db), (q, h)


def sum_early(kept):
    return run_partial(
        [
            (tuple(pair[0] for pair in pairs), tuple(pair[1] for pair in pairs))
            for pairs in zip(*[products_of(rows) for rows in kept])
        ]
    )


def on_device(tokens, cotangent, gates, expert_ids, expert_weights):
    devices = lax.axis_size("expert")
    chips = devices // CORES
    count, width = tokens.shape
    batch = count // MICRO
    capacity = 4 * batch // devices
    own = make_payload(tokens, cotangent, gates, expert_ids)

    def across(value, bit):
        return lax.ppermute(value, "dp", [(i, i ^ bit) for i in range(4)])

    def first_step(sums):
        a_send, a_keep, b_send, b_keep = sums
        a_came = across(a_send, 1)
        b_came = across(b_send, 2)
        next_pair = (add(a_keep[0], a_came[0]), add(b_keep[0], b_came[0]))
        a_base = a_keep[1].astype(F32) + a_came[1].astype(F32)
        b_base = b_keep[1].astype(F32) + b_came[1].astype(F32)
        return (a_base, b_base), next_pair, a_keep

    def move(value, pairs):
        full = [(a * CORES + k, b * CORES + k) for a, b in pairs for k in range(CORES)]
        return lax.ppermute(value, "expert", full)

    def swap(value):
        return lax.ppermute(value, "expert", [(i, i ^ 1) for i in range(devices)])

    def compute(*alternatives, partial=None):
        result = run_slot(alternatives, expert_weights, batch, capacity, (1, chips - 2), partial)
        return result[:-2], (result[-2], result[-1])

    def joined(grads):
        return (grads[0], swap(grads[1]))

    ahead = [(z, (z + 1) % chips) for z in range(chips)]
    behind = [(b, a) for a, b in ahead]
    tuned = chips == 4 and lax.axis_size("dp") == 4
    if tuned:
        outer = [(0, 1), (1, 0), (2, 3), (3, 2)]
        inner = [(1, 2), (2, 1)]
        to_ends = [(1, 0), (2, 3)]
        from_ends = [(0, 1), (3, 2)]
        across_all = [(0, 3), (3, 0)]
        first = move(own, outer)
        second = move(own, inner)
        far = move(own, across_all)
        rows, grads = compute((own, swap(own)))
        kept = [rows]
        own_sum = joined(grads)
        far, second, first = after((far, second, first), own_sum[1])
        third = move(second, to_ends)
        fourth = move(first, inner)
        rows, grads = compute((first, swap(first)))
        kept.append(rows)
        first_sum = joined(grads)
        rows, grads = compute((second, swap(second)), (far, swap(far)))
        kept.append(rows)
        far_sum = joined(grads)
        partial = sum_early(kept)
        third, fourth = after((third, fourth), first_sum[1], far_sum[1], partial)
        last = add(fourth, third)
        sums, grads = compute((last, swap(last)), partial=partial)
        last_sum = joined(grads)
        sent = add(*last_sum)
        bases, next_pair, ready = first_step(sums)
        far_sum = after(far_sum, ready)
        landed = move(sent, inner)
        came = move(sent, from_ends)
        far_back = move(add(*far_sum), across_all)
        came, landed, far_back = after((came, landed, far_back), next_pair)
        back = move(add(*first_sum, landed), outer)
        second_back = move(add(*far_sum, came), inner)
        total = [add(*own_sum, far_back), back, second_back]
    else:
        rows, grads = compute((own, swap(own)))
        kept = [rows]
        total = [*joined(grads)]
        reach = chips // 2
        for forth, back, steps in ((ahead, behind, reach), (behind, ahead, chips - 1 - reach)):
            current, sums = own, []
            for _ in range(steps):
                current = move(current, forth)
                rows, grads = compute((current, swap(current)))
                kept.append(rows)
                sums.append(joined(grads))
            value = None
            for pair in reversed(sums):
                value = move(add(*pair) if value is None else add(*pair, value), back)
            if value is not None:
                total.append(value)

    if tuned:
        a_base, b_base = bases
        a_last = across(next_pair[0], 2)
        b_last = across(next_pair[1], 1)
        weights_grad = run_final(a_base, a_last, b_base, b_last)[None]
    else:
        whole = [jnp.concatenate(value, axis=0) for value in zip(*kept)]
        partial = jnp.stack(
            [
                dot(whole[0], whole[3], FIRST),
                dot(whole[0], whole[4], FIRST),
                dot(whole[1], whole[2], FIRST),
            ]
        ).astype(BF16)
        weights_grad = lax.psum_scatter(
            partial[None], "dp", scatter_dimension=2, tiled=True
        )
    total = after(total, weights_grad)
    tokens_grad, gates_grad = split_total(total, count)
    return tokens_grad, gates_grad, weights_grad


def solution(mesh):
    placed = (
        P(("dp", "expert"), None),
        P(("dp", "expert"), None),
        P(("dp", "expert"), None),
        P(("dp", "expert"), None),
        P("expert", None, None, None),
    )
    return jax.shard_map(
        on_device,
        mesh=mesh,
        in_specs=placed,
        out_specs=(
            P(("dp", "expert"), None),
            P(("dp", "expert"), None),
            P("expert", None, "dp", None),
        ),
        check_vma=False,
    )
```

```python
import functools

import jax
import jax.numpy as jnp
from jax import lax
from jax.experimental import pallas as pl
from jax.experimental.pallas import tpu as pltpu
from jax.sharding import PartitionSpec as P

MICRO = 2
CORES = 2
META = 8
LAST = (((1,), (1,)), ((), ()))
FIRST = (((0,), (0,)), ((), ()))
F32 = jnp.float32
BF16 = jnp.bfloat16


def dot(lhs, rhs, dims=(((1,), (0,)), ((), ()))):
    return lax.dot_general(lhs, rhs, dims, preferred_element_type=F32)


def slot_kernel(choices, fused, batch, capacity, middle, *refs):
    inputs, rest = refs[: 2 * choices], refs[2 * choices :]
    weights, rest = rest[0], rest[1:]
    if fused:
        partial, pieces, rest = rest[0], rest[1:5], rest[5:]
        dxa_out, dxb_out, xr_out, q_out, h_out, da_out, db_out = rest[:7]
    else:
        xr_out, q_out, h_out, da_out, db_out, dxa_out, dxb_out = rest[:7]
    meta_buf, cot_buf = rest[7:]
    count = MICRO * batch
    me = lax.axis_index("expert")
    inner = (me // CORES >= middle[0]) & (me // CORES <= middle[1])

    def chosen_input(task):
        if choices == 1:
            task(inputs[:2])
        else:
            pl.when(inner)(lambda: task(inputs[:2]))
            pl.when(jnp.logical_not(inner))(lambda: task(inputs[2:]))

    def take_meta(pair):
        for half in range(CORES):
            meta_buf[half] = pair[half][2 * count : 2 * count + META, :count]

    chosen_input(take_meta)
    mine = (me + 1).astype(F32)
    upper = (
        lax.broadcasted_iota(jnp.int32, (batch, batch), 0)
        < lax.broadcasted_iota(jnp.int32, (batch, batch), 1)
    ).astype(BF16)
    slot_of = lax.broadcasted_iota(jnp.int32, (capacity, batch), 0).astype(F32)
    parts = []
    for half in range(CORES):
        for micro in range(MICRO):
            rows = slice(micro * batch, (micro + 1) * batch)
            meta = meta_buf[half, :, rows].astype(F32)
            first = meta[0:1] == mine
            second = meta[1:2] == mine
            chosen = jnp.where(first | second, 1.0, 0.0)
            rank = dot(jnp.broadcast_to(chosen, (8, batch)).astype(BF16), upper)[0:1]
            onehot = jnp.where(rank == slot_of, chosen, 0.0)
            gate = jnp.sum(
                onehot * (jnp.where(first, meta[2:3], 0.0) + jnp.where(second, meta[3:4], 0.0)),
                axis=1,
                keepdims=True,
            )
            parts.append((half, rows, onehot, gate, first, second))

    def pack(pair):
        for number, (half, rows, onehot, gate, first, second) in enumerate(parts):
            places = slice(number * capacity, (number + 1) * capacity)
            pick = onehot.astype(BF16)
            xr_out[places, :] = dot(pick, pair[half][rows, :]).astype(BF16)
            cot = dot(pick, pair[half][count + rows.start : count + rows.stop, :])
            cot_buf[places, :] = cot
            q_out[places, :] = (gate * cot).astype(BF16)

    chosen_input(pack)
    xr = xr_out[...]
    pre_gate = dot(xr, weights[0, 0])
    pre_up = dot(xr, weights[0, 1])
    sig = jax.nn.sigmoid(pre_gate)
    activated = pre_gate * sig
    hidden = (activated * pre_up).astype(BF16)
    h_out[...] = hidden
    output = dot(hidden, weights[0, 2], LAST)
    gate_grad = jnp.sum(output * cot_buf[...], axis=1, keepdims=True)
    hidden_grad = dot(q_out[...], weights[0, 2])
    da = (hidden_grad * pre_up * sig * (1.0 + pre_gate * (1.0 - sig))).astype(BF16)
    db = (hidden_grad * activated).astype(BF16)
    da_out[...] = da
    db_out[...] = db
    if fused:
        pair = jnp.concatenate([da, db], axis=1)
        weight_sums(xr_out, q_out, h_out, pair, partial, *pieces)
    dx = (dot(da, weights[0, 0], LAST) + dot(db, weights[0, 1], LAST)).astype(BF16)
    line = lax.broadcasted_iota(jnp.int32, (META, batch), 0)
    outs = (dxa_out, dxb_out)
    for out in outs:
        out[count : count + META, :] = jnp.zeros((META, out.shape[1]), BF16)
    for number, (half, rows, onehot, gate, first, second) in enumerate(parts):
        places = slice(number * capacity, (number + 1) * capacity)
        outs[half][rows, :] = dot(onehot.astype(BF16), dx[places], FIRST).astype(BF16)
        spread = jnp.sum(onehot * gate_grad[places], axis=0, keepdims=True)
        values = jnp.where(line == 0, jnp.where(first, spread, 0.0), 0.0) + jnp.where(
            line == 1, jnp.where(second, spread, 0.0), 0.0
        )
        outs[half][count : count + META, rows] = values.astype(BF16)


def run_slot(alternatives, weights, batch, capacity, middle, partial=None):
    choices = len(alternatives)
    width = weights.shape[2]
    rows = MICRO * batch + META
    hidden_width = weights.shape[-1]
    slots = CORES * MICRO * capacity
    operands = [array for group in alternatives for array in group] + [weights]
    wide, narrow = (slots, width), (slots, hidden_width)
    packed = [wide, wide, narrow, narrow, narrow]
    returned = [(rows, width)] * 2
    scratch = [
        pltpu.VMEM((CORES, META, MICRO * batch), BF16),
        pltpu.VMEM(wide, F32),
    ]
    if partial is None:
        shapes = packed + returned
    else:
        operands.append(partial)
        shapes = [(2, partial.shape[0], width // 4, hidden_width // 2)] * 4 + returned
        scratch = [pltpu.VMEM(shape, BF16) for shape in packed] + scratch
    return pl.pallas_call(
        functools.partial(slot_kernel, choices, partial is not None, batch, capacity, middle),
        out_shape=[jax.ShapeDtypeStruct(shape, BF16) for shape in shapes],
        in_specs=[pl.BlockSpec(memory_space=pltpu.VMEM)] * len(operands),
        out_specs=[pl.BlockSpec(memory_space=pltpu.VMEM)] * len(shapes),
        scratch_shapes=scratch,
        compiler_params=pltpu.CompilerParams(
            vmem_limit_bytes=(24 if partial is None else 32) * 1024 * 1024
        ),
        cost_estimate=pl.CostEstimate(flops=1, bytes_accessed=1, transcendentals=0),
        name="expert_block",
    )(*operands)


def partial_kernel(pieces, *refs):
    operands, out = refs[:-1], refs[-1]
    quarter = out.shape[1] // 4
    for at in range(0, out.shape[1], quarter):
        for product in range(out.shape[0]):
            group = operands[2 * pieces * product : 2 * pieces * (product + 1)]
            total = None
            for left, right in zip(group[:pieces], group[pieces:]):
                term = dot(left[:, at : at + quarter], right[...], FIRST)
                total = term if total is None else total + term
            out[product, at : at + quarter, :] = total


def run_partial(products):
    lefts, rights = products[0]
    operands = [array for pair in products for group in pair for array in group]
    whole = pl.BlockSpec(memory_space=pltpu.VMEM)
    shape = (len(products), lefts[0].shape[1], rights[0].shape[1])
    return pl.pallas_call(
        functools.partial(partial_kernel, len(lefts)),
        out_shape=jax.ShapeDtypeStruct(shape, F32),
        in_specs=[whole] * len(operands),
        out_specs=whole,
        compiler_params=pltpu.CompilerParams(vmem_limit_bytes=24 * 1024 * 1024),
        cost_estimate=pl.CostEstimate(flops=1, bytes_accessed=1, transcendentals=0),
        name="partial_weights",
    )(*operands)


def weight_sums(xr, q, h, pair, partial, a_send, a_keep, b_send, b_keep):
    here = lax.axis_index("dp")
    width, hidden_width = partial.shape[1:]
    quarter = width // 4
    half = hidden_width // 2
    places = (
        (3, a_send, 0, b_send, 0),
        (1, a_send, 1, b_keep, 0),
        (2, a_keep, 0, b_send, 1),
        (0, a_keep, 1, b_keep, 1),
    )
    for place, a_out, a_at, b_out, b_at in places:
        rows = pl.ds(pl.multiple_of((here ^ place) * quarter, quarter), quarter)
        joint = dot(xr[:, rows], pair, FIRST)
        sums = (joint[:, :hidden_width], joint[:, hidden_width:], dot(q[:, rows], h[...], FIRST))
        for product, term in enumerate(sums):
            value = (partial[product, rows, :] + term).astype(BF16)
            a_out[a_at, product] = value[:, :half]
            b_out[b_at, product] = value[:, half:]


def add(*values):
    total = values[0].astype(F32)
    for value in values[1:]:
        total = total + value.astype(F32)
    return total.astype(BF16)


def final_kernel(a_base, a_last, b_base, b_last, out):
    half = out.shape[2] // 2
    out[:, :, :half] = (a_base[...] + a_last[...].astype(F32)).astype(BF16)
    out[:, :, half:] = (b_base[...] + b_last[...].astype(F32)).astype(BF16)


def run_final(*operands):
    products, rows, half = operands[1].shape
    whole = pl.BlockSpec(memory_space=pltpu.VMEM)
    return pl.pallas_call(
        final_kernel,
        out_shape=jax.ShapeDtypeStruct((products, rows, 2 * half), BF16),
        in_specs=[whole] * 4,
        out_specs=whole,
        compiler_params=pltpu.CompilerParams(vmem_limit_bytes=12 * 1024 * 1024),
        cost_estimate=pl.CostEstimate(flops=1, bytes_accessed=1, transcendentals=0),
        name="final_step",
    )(*operands)


def payload_kernel(tokens, cotangent, ids_hbm, gates_hbm, out, ids, gates, held, sems):
    count = tokens.shape[0]
    small = [
        pltpu.make_async_copy(ids_hbm, ids, sems.at[0]),
        pltpu.make_async_copy(gates_hbm, gates, sems.at[1]),
    ]
    large = [
        pltpu.make_async_copy(tokens, held.at[:count], sems.at[2]),
        pltpu.make_async_copy(cotangent, held.at[count : 2 * count], sems.at[3]),
    ]
    outward = pltpu.make_async_copy(held, out, sems.at[4])
    for copy in small + large:
        copy.start()
    for copy in small:
        copy.wait()
    line = lax.broadcasted_iota(jnp.int32, (META, count), 0)
    values = jnp.zeros((META, count), F32)
    rows = (
        ids[0:1, :].astype(F32) + 1.0,
        ids[1:2, :].astype(F32) + 1.0,
        gates[0:1, :].astype(F32),
        gates[1:2, :].astype(F32),
    )
    for number, row in enumerate(rows):
        values = jnp.where(line == number, row, values)
    held[2 * count :, :] = jnp.zeros((META, held.shape[1]), BF16)
    held[2 * count :, :count] = values.astype(BF16)
    for copy in large:
        copy.wait()
    outward.start()
    outward.wait()


def make_payload(tokens, cotangent, gates, expert_ids):
    count, width = tokens.shape
    return pl.pallas_call(
        payload_kernel,
        out_shape=jax.ShapeDtypeStruct((2 * count + META, width), BF16),
        in_specs=[pl.BlockSpec(memory_space=pltpu.HBM)] * 4,
        out_specs=pl.BlockSpec(memory_space=pltpu.HBM),
        scratch_shapes=[
            pltpu.VMEM((2, count), jnp.int32),
            pltpu.VMEM((2, count), BF16),
            pltpu.VMEM((2 * count + META, width), BF16),
            pltpu.SemaphoreType.DMA((5,)),
        ],
        compiler_params=pltpu.CompilerParams(vmem_limit_bytes=60 * 1024 * 1024),
        cost_estimate=pl.CostEstimate(flops=1, bytes_accessed=1, transcendentals=0),
        name="payload",
    )(tokens, cotangent, expert_ids.T, gates.T)


def total_kernel(parts, *refs):
    values, (tokens_out, gates_out) = refs[:parts], refs[parts:]
    count = tokens_out.shape[0]
    total = values[0][...].astype(F32)
    for value in values[1:]:
        total = total + value[...].astype(F32)
    tokens_out[...] = total[:count].astype(BF16)
    gates_out[...] = total[count : count + META, :count].astype(BF16)[:2]


def split_total(values, count):
    width = values[0].shape[1]
    whole = pl.BlockSpec(memory_space=pltpu.VMEM)
    tokens_grad, gates_grad = pl.pallas_call(
        functools.partial(total_kernel, len(values)),
        out_shape=[
            jax.ShapeDtypeStruct((count, width), BF16),
            jax.ShapeDtypeStruct((2, count), BF16),
        ],
        in_specs=[whole] * len(values),
        out_specs=[whole] * 2,
        compiler_params=pltpu.CompilerParams(vmem_limit_bytes=8 * 1024 * 1024),
        cost_estimate=pl.CostEstimate(flops=1, bytes_accessed=1, transcendentals=0),
        name="total",
    )(*values)
    return tokens_grad, gates_grad.T


def after(value, *earlier):
    return lax.optimization_barrier((value, earlier))[0]


def products_of(rows):
    xr, q, h, da, db = rows
    return (xr, da), (xr, db), (q, h)


def sum_early(kept):
    return run_partial(
        [
            (tuple(pair[0] for pair in pairs), tuple(pair[1] for pair in pairs))
            for pairs in zip(*[products_of(rows) for rows in kept])
        ]
    )


def on_device(tokens, cotangent, gates, expert_ids, expert_weights):
    devices = lax.axis_size("expert")
    chips = devices // CORES
    count, width = tokens.shape
    batch = count // MICRO
    capacity = 4 * batch // devices
    own = make_payload(tokens, cotangent, gates, expert_ids)

    def across(value, bit):
        return lax.ppermute(value, "dp", [(i, i ^ bit) for i in range(4)])

    def first_step(sums):
        a_send, a_keep, b_send, b_keep = sums
        a_came = across(a_send, 1)
        b_came = across(b_send, 2)
        next_pair = (add(a_keep[0], a_came[0]), add(b_keep[0], b_came[0]))
        a_base = a_keep[1].astype(F32) + a_came[1].astype(F32)
        b_base = b_keep[1].astype(F32) + b_came[1].astype(F32)
        return (a_base, b_base), next_pair, a_keep

    def move(value, pairs):
        full = [(a * CORES + k, b * CORES + k) for a, b in pairs for k in range(CORES)]
        return lax.ppermute(value, "expert", full)

    def swap(value):
        return lax.ppermute(value, "expert", [(i, i ^ 1) for i in range(devices)])

    def compute(*alternatives, partial=None):
        result = run_slot(alternatives, expert_weights, batch, capacity, (1, chips - 2), partial)
        return result[:-2], (result[-2], result[-1])

    def joined(grads):
        return (grads[0], swap(grads[1]))

    ahead = [(z, (z + 1) % chips) for z in range(chips)]
    behind = [(b, a) for a, b in ahead]
    tuned = chips == 4 and lax.axis_size("dp") == 4
    if tuned:
        outer = [(0, 1), (1, 0), (2, 3), (3, 2)]
        inner = [(1, 2), (2, 1)]
        to_ends = [(1, 0), (2, 3)]
        from_ends = [(0, 1), (3, 2)]
        across_all = [(0, 3), (3, 0)]
        first = move(own, outer)
        second = move(own, inner)
        far = move(own, across_all)
        rows, grads = compute((own, swap(own)))
        kept = [rows]
        own_sum = joined(grads)
        far, second, first = after((far, second, first), own_sum[1])
        third = move(second, to_ends)
        fourth = move(first, inner)
        rows, grads = compute((first, swap(first)))
        kept.append(rows)
        first_sum = joined(grads)
        rows, grads = compute((second, swap(second)), (far, swap(far)))
        kept.append(rows)
        far_sum = joined(grads)
        partial = sum_early(kept)
        third, fourth = after((third, fourth), first_sum[1], far_sum[1], partial)
        last = fourth + third
        sums, grads = compute((last, swap(last)), partial=partial)
        last_sum = joined(grads)
        sent = add(*last_sum)
        bases, next_pair, ready = first_step(sums)
        far_sum = after(far_sum, ready)
        landed = move(sent, inner)
        came = move(sent, from_ends)
        far_back = move(add(*far_sum), across_all)
        came, landed, far_back = after((came, landed, far_back), next_pair)
        back = move(add(*first_sum, landed), outer)
        second_back = move(add(*far_sum, came), inner)
        total = [add(*own_sum, far_back), back, second_back]
    else:
        rows, grads = compute((own, swap(own)))
        kept = [rows]
        total = [*joined(grads)]
        reach = chips // 2
        for forth, back, steps in ((ahead, behind, reach), (behind, ahead, chips - 1 - reach)):
            current, sums = own, []
            for _ in range(steps):
                current = move(current, forth)
                rows, grads = compute((current, swap(current)))
                kept.append(rows)
                sums.append(joined(grads))
            value = None
            for pair in reversed(sums):
                value = move(add(*pair) if value is None else add(*pair, value), back)
            if value is not None:
                total.append(value)

    if tuned:
        a_base, b_base = bases
        a_last = across(next_pair[0], 2)
        b_last = across(next_pair[1], 1)
        weights_grad = run_final(a_base, a_last, b_base, b_last)[None]
    else:
        whole = [jnp.concatenate(value, axis=0) for value in zip(*kept)]
        partial = jnp.stack(
            [
                dot(whole[0], whole[3], FIRST),
                dot(whole[0], whole[4], FIRST),
                dot(whole[1], whole[2], FIRST),
            ]
        ).astype(BF16)
        weights_grad = lax.psum_scatter(
            partial[None], "dp", scatter_dimension=2, tiled=True
        )
    total = after(total, weights_grad)
    tokens_grad, gates_grad = split_total(total, count)
    return tokens_grad, gates_grad, weights_grad


def solution(mesh):
    placed = (
        P(("dp", "expert"), None),
        P(("dp", "expert"), None),
        P(("dp", "expert"), None),
        P(("dp", "expert"), None),
        P("expert", None, None, None),
    )
    return jax.shard_map(
        on_device,
        mesh=mesh,
        in_specs=placed,
        out_specs=(
            P(("dp", "expert"), None),
            P(("dp", "expert"), None),
            P("expert", None, "dp", None),
        ),
        check_vma=False,
    )
```

```python
import functools

import jax
import jax.numpy as jnp
from jax import lax
from jax.experimental import pallas as pl
from jax.experimental.pallas import tpu as pltpu
from jax.sharding import PartitionSpec as P

MICRO = 2
CORES = 2
META = 8
LAST = (((1,), (1,)), ((), ()))
FIRST = (((0,), (0,)), ((), ()))
F32 = jnp.float32
BF16 = jnp.bfloat16


def dot(lhs, rhs, dims=(((1,), (0,)), ((), ()))):
    return lax.dot_general(lhs, rhs, dims, preferred_element_type=F32)


def slot_kernel(choices, fused, batch, capacity, middle, *refs):
    inputs, rest = refs[: 2 * choices], refs[2 * choices :]
    weights, rest = rest[0], rest[1:]
    if fused:
        partial, pieces, rest = rest[0], rest[1:5], rest[5:]
        dxa_out, dxb_out, xr_out, q_out, h_out, da_out, db_out = rest[:7]
    else:
        xr_out, q_out, h_out, da_out, db_out, dxa_out, dxb_out = rest[:7]
    meta_buf, cot_buf = rest[7:]
    count = MICRO * batch
    me = lax.axis_index("expert")
    inner = (me // CORES >= middle[0]) & (me // CORES <= middle[1])

    def chosen_input(task):
        if choices == 1:
            task(inputs[:2])
        else:
            pl.when(inner)(lambda: task(inputs[:2]))
            pl.when(jnp.logical_not(inner))(lambda: task(inputs[2:]))

    def take_meta(pair):
        for half in range(CORES):
            meta_buf[half] = pair[half][2 * count : 2 * count + META, :count]

    chosen_input(take_meta)
    mine = (me + 1).astype(F32)
    upper = (
        lax.broadcasted_iota(jnp.int32, (batch, batch), 0)
        < lax.broadcasted_iota(jnp.int32, (batch, batch), 1)
    ).astype(BF16)
    slot_of = lax.broadcasted_iota(jnp.int32, (capacity, batch), 0).astype(F32)
    parts = []
    for half in range(CORES):
        for micro in range(MICRO):
            rows = slice(micro * batch, (micro + 1) * batch)
            meta = meta_buf[half, :, rows].astype(F32)
            first = meta[0:1] == mine
            second = meta[1:2] == mine
            chosen = jnp.where(first | second, 1.0, 0.0)
            rank = dot(jnp.broadcast_to(chosen, (8, batch)).astype(BF16), upper)[0:1]
            onehot = jnp.where(rank == slot_of, chosen, 0.0)
            gate = jnp.sum(
                onehot * (jnp.where(first, meta[2:3], 0.0) + jnp.where(second, meta[3:4], 0.0)),
                axis=1,
                keepdims=True,
            )
            parts.append((half, rows, onehot, gate, first, second))

    def pack(pair):
        for number, (half, rows, onehot, gate, first, second) in enumerate(parts):
            places = slice(number * capacity, (number + 1) * capacity)
            pick = onehot.astype(BF16)
            xr_out[places, :] = dot(pick, pair[half][rows, :]).astype(BF16)
            cot = dot(pick, pair[half][count + rows.start : count + rows.stop, :])
            cot_buf[places, :] = cot
            q_out[places, :] = (gate * cot).astype(BF16)

    chosen_input(pack)
    xr = xr_out[...]
    pre_gate = dot(xr, weights[0, 0])
    pre_up = dot(xr, weights[0, 1])
    sig = jax.nn.sigmoid(pre_gate)
    activated = pre_gate * sig
    hidden = (activated * pre_up).astype(BF16)
    h_out[...] = hidden
    output = dot(hidden, weights[0, 2], LAST)
    gate_grad = jnp.sum(output * cot_buf[...], axis=1, keepdims=True)
    hidden_grad = dot(q_out[...], weights[0, 2])
    da = (hidden_grad * pre_up * sig * (1.0 + pre_gate * (1.0 - sig))).astype(BF16)
    db = (hidden_grad * activated).astype(BF16)
    da_out[...] = da
    db_out[...] = db
    if fused:
        weight_sums(((xr_out, da_out), (xr_out, db_out), (q_out, h_out)), partial, *pieces)
    dx = (dot(da, weights[0, 0], LAST) + dot(db, weights[0, 1], LAST)).astype(BF16)
    line = lax.broadcasted_iota(jnp.int32, (META, batch), 0)
    outs = (dxa_out, dxb_out)
    for out in outs:
        out[count : count + META, :] = jnp.zeros((META, out.shape[1]), BF16)
    for number, (half, rows, onehot, gate, first, second) in enumerate(parts):
        places = slice(number * capacity, (number + 1) * capacity)
        outs[half][rows, :] = dot(onehot.astype(BF16), dx[places], FIRST).astype(BF16)
        spread = jnp.sum(onehot * gate_grad[places], axis=0, keepdims=True)
        values = jnp.where(line == 0, jnp.where(first, spread, 0.0), 0.0) + jnp.where(
            line == 1, jnp.where(second, spread, 0.0), 0.0
        )
        outs[half][count : count + META, rows] = values.astype(BF16)


def run_slot(alternatives, weights, batch, capacity, middle, partial=None):
    choices = len(alternatives)
    width = weights.shape[2]
    rows = MICRO * batch + META
    hidden_width = weights.shape[-1]
    slots = CORES * MICRO * capacity
    operands = [array for group in alternatives for array in group] + [weights]
    wide, narrow = (slots, width), (slots, hidden_width)
    packed = [wide, wide, narrow, narrow, narrow]
    returned = [(rows, width)] * 2
    scratch = [
        pltpu.VMEM((CORES, META, MICRO * batch), BF16),
        pltpu.VMEM(wide, F32),
    ]
    if partial is None:
        shapes = packed + returned
    else:
        operands.append(partial)
        shapes = [(2, partial.shape[0], width // 4, hidden_width // 2)] * 4 + returned
        scratch = [pltpu.VMEM(shape, BF16) for shape in packed] + scratch
    return pl.pallas_call(
        functools.partial(slot_kernel, choices, partial is not None, batch, capacity, middle),
        out_shape=[jax.ShapeDtypeStruct(shape, BF16) for shape in shapes],
        in_specs=[pl.BlockSpec(memory_space=pltpu.VMEM)] * len(operands),
        out_specs=[pl.BlockSpec(memory_space=pltpu.VMEM)] * len(shapes),
        scratch_shapes=scratch,
        compiler_params=pltpu.CompilerParams(
            vmem_limit_bytes=(24 if partial is None else 32) * 1024 * 1024
        ),
        cost_estimate=pl.CostEstimate(flops=1, bytes_accessed=1, transcendentals=0),
        name="expert_block",
    )(*operands)


def partial_kernel(pieces, *refs):
    operands, out = refs[:-1], refs[-1]
    quarter = out.shape[1] // 4
    for at in range(0, out.shape[1], quarter):
        for product in range(out.shape[0]):
            group = operands[2 * pieces * product : 2 * pieces * (product + 1)]
            total = None
            for left, right in zip(group[:pieces], group[pieces:]):
                term = dot(left[:, at : at + quarter], right[...], FIRST)
                total = term if total is None else total + term
            out[product, at : at + quarter, :] = total


def run_partial(products):
    lefts, rights = products[0]
    operands = [array for pair in products for group in pair for array in group]
    whole = pl.BlockSpec(memory_space=pltpu.VMEM)
    shape = (len(products), lefts[0].shape[1], rights[0].shape[1])
    return pl.pallas_call(
        functools.partial(partial_kernel, len(lefts)),
        out_shape=jax.ShapeDtypeStruct(shape, F32),
        in_specs=[whole] * len(operands),
        out_specs=whole,
        compiler_params=pltpu.CompilerParams(vmem_limit_bytes=24 * 1024 * 1024),
        cost_estimate=pl.CostEstimate(flops=1, bytes_accessed=1, transcendentals=0),
        name="partial_weights",
    )(*operands)


def weight_sums(products, partial, a_send, a_keep, b_send, b_keep):
    here = lax.axis_index("dp")
    width, hidden_width = partial.shape[1:]
    quarter = width // 4
    half = hidden_width // 2
    places = (
        (3, a_send, 0, b_send, 0),
        (1, a_send, 1, b_keep, 0),
        (2, a_keep, 0, b_send, 1),
        (0, a_keep, 1, b_keep, 1),
    )
    for place, a_out, a_at, b_out, b_at in places:
        rows = pl.ds(pl.multiple_of((here ^ place) * quarter, quarter), quarter)
        for product, (left, right) in enumerate(products):
            value = (partial[product, rows, :] + dot(left[:, rows], right[...], FIRST)).astype(BF16)
            a_out[a_at, product] = value[:, :half]
            b_out[b_at, product] = value[:, half:]


def add(*values):
    total = values[0].astype(F32)
    for value in values[1:]:
        total = total + value.astype(F32)
    return total.astype(BF16)


def final_kernel(a_base, a_last, b_base, b_last, out):
    half = out.shape[2] // 2
    out[:, :, :half] = (a_base[...] + a_last[...].astype(F32)).astype(BF16)
    out[:, :, half:] = (b_base[...] + b_last[...].astype(F32)).astype(BF16)


def run_final(*operands):
    products, rows, half = operands[1].shape
    whole = pl.BlockSpec(memory_space=pltpu.VMEM)
    return pl.pallas_call(
        final_kernel,
        out_shape=jax.ShapeDtypeStruct((products, rows, 2 * half), BF16),
        in_specs=[whole] * 4,
        out_specs=whole,
        compiler_params=pltpu.CompilerParams(vmem_limit_bytes=12 * 1024 * 1024),
        cost_estimate=pl.CostEstimate(flops=1, bytes_accessed=1, transcendentals=0),
        name="final_step",
    )(*operands)


def payload_kernel(tokens, cotangent, ids_hbm, gates_hbm, out, ids, gates, held, sems):
    count = tokens.shape[0]
    small = [
        pltpu.make_async_copy(ids_hbm, ids, sems.at[0]),
        pltpu.make_async_copy(gates_hbm, gates, sems.at[1]),
    ]
    large = [
        pltpu.make_async_copy(tokens, held.at[:count], sems.at[2]),
        pltpu.make_async_copy(cotangent, held.at[count : 2 * count], sems.at[3]),
    ]
    outward = pltpu.make_async_copy(held, out, sems.at[4])
    for copy in large + small:
        copy.start()
    for copy in small:
        copy.wait()
    line = lax.broadcasted_iota(jnp.int32, (META, count), 0)
    values = jnp.zeros((META, count), F32)
    rows = (
        ids[0:1, :].astype(F32) + 1.0,
        ids[1:2, :].astype(F32) + 1.0,
        gates[0:1, :].astype(F32),
        gates[1:2, :].astype(F32),
    )
    for number, row in enumerate(rows):
        values = jnp.where(line == number, row, values)
    held[2 * count :, :] = jnp.zeros((META, held.shape[1]), BF16)
    held[2 * count :, :count] = values.astype(BF16)
    for copy in large:
        copy.wait()
    outward.start()
    outward.wait()


def make_payload(tokens, cotangent, gates, expert_ids):
    count, width = tokens.shape
    return pl.pallas_call(
        payload_kernel,
        out_shape=jax.ShapeDtypeStruct((2 * count + META, width), BF16),
        in_specs=[pl.BlockSpec(memory_space=pltpu.HBM)] * 4,
        out_specs=pl.BlockSpec(memory_space=pltpu.HBM),
        scratch_shapes=[
            pltpu.VMEM((2, count), jnp.int32),
            pltpu.VMEM((2, count), BF16),
            pltpu.VMEM((2 * count + META, width), BF16),
            pltpu.SemaphoreType.DMA((5,)),
        ],
        compiler_params=pltpu.CompilerParams(vmem_limit_bytes=60 * 1024 * 1024),
        cost_estimate=pl.CostEstimate(flops=1, bytes_accessed=1, transcendentals=0),
        name="payload",
    )(tokens, cotangent, expert_ids.T, gates.T)


def total_kernel(parts, *refs):
    values, (tokens_out, gates_out) = refs[:parts], refs[parts:]
    count = tokens_out.shape[0]
    total = values[0][...].astype(F32)
    for value in values[1:]:
        total = total + value[...].astype(F32)
    tokens_out[...] = total[:count].astype(BF16)
    gates_out[...] = total[count : count + META, :count].astype(BF16)[:2]


def split_total(values, count):
    width = values[0].shape[1]
    whole = pl.BlockSpec(memory_space=pltpu.VMEM)
    tokens_grad, gates_grad = pl.pallas_call(
        functools.partial(total_kernel, len(values)),
        out_shape=[
            jax.ShapeDtypeStruct((count, width), BF16),
            jax.ShapeDtypeStruct((2, count), BF16),
        ],
        in_specs=[whole] * len(values),
        out_specs=[whole] * 2,
        compiler_params=pltpu.CompilerParams(vmem_limit_bytes=8 * 1024 * 1024),
        cost_estimate=pl.CostEstimate(flops=1, bytes_accessed=1, transcendentals=0),
        name="total",
    )(*values)
    return tokens_grad, gates_grad.T


def after(value, *earlier):
    return lax.optimization_barrier((value, earlier))[0]


def products_of(rows):
    xr, q, h, da, db = rows
    return (xr, da), (xr, db), (q, h)


def sum_early(kept):
    return run_partial(
        [
            (tuple(pair[0] for pair in pairs), tuple(pair[1] for pair in pairs))
            for pairs in zip(*[products_of(rows) for rows in kept])
        ]
    )


def on_device(tokens, cotangent, gates, expert_ids, expert_weights):
    devices = lax.axis_size("expert")
    chips = devices // CORES
    count, width = tokens.shape
    batch = count // MICRO
    capacity = 4 * batch // devices
    own = make_payload(tokens, cotangent, gates, expert_ids)

    def across(value, bit):
        return lax.ppermute(value, "dp", [(i, i ^ bit) for i in range(4)])

    def first_step(sums):
        a_send, a_keep, b_send, b_keep = sums
        a_came = across(a_send, 1)
        b_came = across(b_send, 2)
        next_pair = (add(a_keep[0], a_came[0]), add(b_keep[0], b_came[0]))
        a_base = a_keep[1].astype(F32) + a_came[1].astype(F32)
        b_base = b_keep[1].astype(F32) + b_came[1].astype(F32)
        return (a_base, b_base), next_pair, a_keep

    def move(value, pairs):
        full = [(a * CORES + k, b * CORES + k) for a, b in pairs for k in range(CORES)]
        return lax.ppermute(value, "expert", full)

    def swap(value):
        return lax.ppermute(value, "expert", [(i, i ^ 1) for i in range(devices)])

    def compute(*alternatives, partial=None):
        result = run_slot(alternatives, expert_weights, batch, capacity, (1, chips - 2), partial)
        return result[:-2], (result[-2], result[-1])

    def joined(grads):
        return (grads[0], swap(grads[1]))

    ahead = [(z, (z + 1) % chips) for z in range(chips)]
    behind = [(b, a) for a, b in ahead]
    tuned = chips == 4 and lax.axis_size("dp") == 4
    if tuned:
        outer = [(0, 1), (1, 0), (2, 3), (3, 2)]
        inner = [(1, 2), (2, 1)]
        to_ends = [(1, 0), (2, 3)]
        from_ends = [(0, 1), (3, 2)]
        across_all = [(0, 3), (3, 0)]
        first = move(own, outer)
        second = move(own, inner)
        far = move(own, across_all)
        rows, grads = compute((own, swap(own)))
        kept = [rows]
        own_sum = joined(grads)
        far, second, first = after((far, second, first), own_sum[1])
        third = move(second, to_ends)
        fourth = move(first, inner)
        rows, grads = compute((first, swap(first)))
        kept.append(rows)
        first_sum = joined(grads)
        rows, grads = compute((second, swap(second)), (far, swap(far)))
        kept.append(rows)
        far_sum = joined(grads)
        partial = sum_early(kept)
        third, fourth = after((third, fourth), first_sum[1], far_sum[1], partial)
        last = add(fourth, third)
        sums, grads = compute((last, swap(last)), partial=partial)
        last_sum = joined(grads)
        sent = add(*last_sum)
        bases, next_pair, ready = first_step(sums)
        far_sum = after(far_sum, ready)
        landed = move(sent, inner)
        came = move(sent, from_ends)
        far_back = move(add(*far_sum), across_all)
        came, landed, far_back = after((came, landed, far_back), next_pair)
        back = move(add(*first_sum, landed), outer)
        second_back = move(add(*far_sum, came), inner)
        total = [add(*own_sum, far_back), back, second_back]
    else:
        rows, grads = compute((own, swap(own)))
        kept = [rows]
        total = [*joined(grads)]
        reach = chips // 2
        for forth, back, steps in ((ahead, behind, reach), (behind, ahead, chips - 1 - reach)):
            current, sums = own, []
            for _ in range(steps):
                current = move(current, forth)
                rows, grads = compute((current, swap(current)))
                kept.append(rows)
                sums.append(joined(grads))
            value = None
            for pair in reversed(sums):
                value = move(add(*pair) if value is None else add(*pair, value), back)
            if value is not None:
                total.append(value)

    if tuned:
        a_base, b_base = bases
        a_last = across(next_pair[0], 2)
        b_last = across(next_pair[1], 1)
        weights_grad = run_final(a_base, a_last, b_base, b_last)[None]
    else:
        whole = [jnp.concatenate(value, axis=0) for value in zip(*kept)]
        partial = jnp.stack(
            [
                dot(whole[0], whole[3], FIRST),
                dot(whole[0], whole[4], FIRST),
                dot(whole[1], whole[2], FIRST),
            ]
        ).astype(BF16)
        weights_grad = lax.psum_scatter(
            partial[None], "dp", scatter_dimension=2, tiled=True
        )
    total = after(total, weights_grad)
    tokens_grad, gates_grad = split_total(total, count)
    return tokens_grad, gates_grad, weights_grad


def solution(mesh):
    placed = (
        P(("dp", "expert"), None),
        P(("dp", "expert"), None),
        P(("dp", "expert"), None),
        P(("dp", "expert"), None),
        P("expert", None, None, None),
    )
    return jax.shard_map(
        on_device,
        mesh=mesh,
        in_specs=placed,
        out_specs=(
            P(("dp", "expert"), None),
            P(("dp", "expert"), None),
            P("expert", None, "dp", None),
        ),
        check_vma=False,
    )
```
